32 devices in a mesh: strip: 4 (over y, x), cuts: 8 (over z, core).
Axes of the slice: x: 2, y: 2, z: 4, core: 2. Of those that a mesh axis runs over, the one named last changes fastest.
Arguments:
- start_state: float32 [8, 6, 512, 512], P('cuts', None, 'strip'), may hold values from -6 to 6
- initial_state: float32 [6, 512, 512], P(None, 'strip'), may hold values from -6 to 6
- circ_stiff: float32 [512, 512], P('strip'), may hold values from 0.5 to 2
- axial_stiff: float32 [512, 512], P('strip'), may hold values from 0.5 to 2
- lumped_mass: float32 [512, 512], P('strip'), may hold values from 1 to 2
- hoop_stiff: float32 [512, 512], P('strip'), may hold values from 0.5 to 2
Outputs:
- new_start: float32 [8, 6, 512, 512], P('cuts', None, 'strip')
- fine_end: float32 [8, 6, 512, 512], P('cuts', None, 'strip')
The draws below stay inside these ranges and needn't reach their ends.
All inputs are finite; a program needn't handle non-finite values.
Results may differ from the reference program's by a relative error of at most 0.00002.
Values sent between devices are 32-bit elements; how exact they have to be, the bound alone decides.
No kernel may reach another device: no remote copies, remote signals or barrier semaphores. Data moves between devices by JAX's collectives and lax.ppermute only.
A program may use at most 192 MiB of HBM per device.

```python
import math
import jax
import jax.numpy as jnp
from jax import lax

NA = 512
NC = 512
SLICES = 8


def levels(rng, shape, shards, low, largest):
    gain = 1.0
    for axis_at, parts in shards:
        heights = jax.random.uniform(jax.random.fold_in(jax.random.fold_in(rng, 6), axis_at), (parts,), jnp.float32, low / len(shards), largest / len(shards))
        gain = gain * jnp.repeat(jnp.exp(heights), shape[axis_at] // parts).reshape((-1,) + (1,) * (len(shape) - 1 - axis_at))
    return gain


def scatter_about(rng, extent, deviation, reach, cuts=(), kind=jnp.bfloat16):
    values = deviation * jax.random.normal(rng, extent, jnp.float32)
    if cuts:
        values = values * levels(rng, extent, cuts, -0.22, 0.18)
    return jnp.clip(values, -reach, reach).astype(kind)


def setup_inputs(seed: int = 0) -> dict:
    arg_keys = jax.random.split(jax.random.key(seed), 7)
    start_state = scatter_about(arg_keys[0], (SLICES, 6, NC, NA), 1.0, 6.0, ((0, 8), (2, 4)), jnp.float32)
    initial_state = scatter_about(arg_keys[1], (6, NC, NA), 1.0, 6.0, ((1, 4),), jnp.float32)
    circ_stiff = jnp.clip(jnp.exp(math.log(2.0) - 1.3862944 * jax.random.uniform(arg_keys[2], (NC, NA), jnp.float32) ** levels(arg_keys[2], (NC, NA), ((0, 4),), -0.2, 0.2)), 0.5, 2.0)
    axial_stiff = jnp.clip(jnp.exp(math.log(2.0) - 1.3862944 * jax.random.uniform(arg_keys[3], (NC, NA), jnp.float32) ** levels(arg_keys[3], (NC, NA), ((0, 4),), -0.2, 0.2)), 0.5, 2.0)
    lumped_mass = jnp.clip(jnp.exp(math.log(2.0) - 0.6931472 * jax.random.uniform(arg_keys[4], (NC, NA), jnp.float32) ** levels(arg_keys[4], (NC, NA), ((0, 4),), -0.2, 0.2)), 1.0, 2.0)
    hoop_stiff = jnp.clip(jnp.exp(math.log(2.0) - 1.3862944 * jax.random.uniform(arg_keys[5], (NC, NA), jnp.float32) ** levels(arg_keys[5], (NC, NA), ((0, 4),), -0.2, 0.2)), 0.5, 2.0)
    return dict(start_state=start_state, initial_state=initial_state, circ_stiff=circ_stiff, axial_stiff=axial_stiff, lumped_mass=lumped_mass, hoop_stiff=hoop_stiff)


step_length = 0.35
coupling_fine = 0.25


def combine_forces(displace, above_rows, below_rows, circ_stiff, circ_low, axial_stiff, hoop_stiff, coupling):
    zero_col = jnp.zeros_like(displace[:, :, :1])
    forward = jnp.concatenate([displace[:, :, 1:], zero_col], axis=2)
    backward = jnp.concatenate([zero_col, displace[:, :, :-1]], axis=2)
    axial_low = jnp.concatenate([jnp.zeros_like(axial_stiff[:, :1]), axial_stiff[:, :-1]], axis=1)
    summed = circ_stiff * (above_rows - displace) + circ_low * (below_rows - displace)
    summed = summed + axial_stiff * (forward - displace) + axial_low * (backward - displace)
    gradient = 0.5 * (above_rows - below_rows)
    first_comp = summed[0] - coupling * gradient[2]
    third_comp = summed[2] + coupling * gradient[0] - hoop_stiff * displace[2]
    return jnp.stack([first_comp, summed[1], third_comp])


def verlet(current, force_fn, masses, increment, repeats):
    displace = current[:3]
    velocity = current[3:]
    acceleration = force_fn(displace) / masses
    for number in range(repeats):
        half_step = velocity + (0.5 * increment) * acceleration
        displace = displace + increment * half_step
        acceleration = force_fn(displace) / masses
        velocity = half_step + (0.5 * increment) * acceleration
    return jnp.concatenate([displace, velocity], axis=0)


def restrict(field):
    leading = field.shape[:-2]
    rows = field.shape[-2]
    cols = field.shape[-1]
    return field.reshape(leading + (rows // 2, 2, cols // 2, 2)).mean(axis=(-3, -1))


def prolong(field):
    return jnp.repeat(jnp.repeat(field, 2, axis=-2), 2, axis=-1)


def reference(start_state, initial_state, circ_stiff, axial_stiff, lumped_mass, hoop_stiff):
    circ_low = jnp.roll(circ_stiff, 1, axis=0)

    def fine_force(displace):
        return combine_forces(displace, jnp.roll(displace, -1, axis=1), jnp.roll(displace, 1, axis=1),
                              circ_stiff, circ_low, axial_stiff, hoop_stiff, coupling_fine)

    fine_end = lax.map(lambda slice_state: verlet(slice_state, fine_force, lumped_mass, step_length, 2), start_state)
    first_jump = initial_state[None] - start_state[:1]
    mismatch = jnp.concatenate([first_jump, fine_end[:-1] - start_state[1:]], axis=0)
    coarse_circ = restrict(circ_stiff)
    coarse_low = jnp.roll(coarse_circ, 1, axis=0)
    coarse_axial = restrict(axial_stiff)
    coarse_mass = 4.0 * restrict(lumped_mass)
    coarse_hoop = 4.0 * restrict(hoop_stiff)

    def coarse_force(displace):
        return combine_forces(displace, jnp.roll(displace, -1, axis=1), jnp.roll(displace, 1, axis=1),
                              coarse_circ, coarse_low, coarse_axial, coarse_hoop, 2.0 * coupling_fine)

    residue = restrict(mismatch)
    carried = [residue[0]]
    for number in range(1, SLICES):
        carried.append(verlet(carried[-1], coarse_force, coarse_mass, 2.0 * step_length, 1) + residue[number])
    carried = jnp.stack(carried)
    new_start = start_state + mismatch + prolong(carried - residue)
    return new_start, fine_end
```

```python
import jax
import jax.numpy as jnp
from jax import lax
from jax.experimental import pallas as pl
from jax.experimental.pallas import tpu as pltpu
from jax.sharding import PartitionSpec as P

FINE_STEP = 0.35
COARSE_STEP = 0.7
FINE_COUPLING = 0.25
COARSE_COUPLING = 0.5
SPEED = COARSE_STEP

FINE_ROWS = (3, 3, 3, 2, 2, 2, 3, 2, 2, 2)
COARSE_ROWS = (2, 2, 2, 1, 1, 1, 3, 2, 2, 2)
FINE_TOTAL = sum(FINE_ROWS)
PACK_ROWS = -(-(FINE_TOTAL + -(-sum(COARSE_ROWS) // 2)) // 8) * 8
CHUNK = 8
EDGE = 4

VMEM = pl.BlockSpec(memory_space=pltpu.VMEM)
ANY = pl.BlockSpec(memory_space=pl.ANY)
F32 = jnp.float32


def run(body, name, outs, args, scratch=(), specs=None, out_specs=None, aliases=None):
    return pl.pallas_call(
        body,
        name=name,
        out_shape=[jax.ShapeDtypeStruct(shape, F32) for shape in outs],
        in_specs=specs or [VMEM] * len(args),
        out_specs=out_specs or [VMEM] * len(outs),
        scratch_shapes=list(scratch),
        input_output_aliases=aliases or {},
        compiler_params=pltpu.CompilerParams(vmem_limit_bytes=20 << 20),
    )(*args)


def turn(value, steps, axis):
    return pltpu.roll(value, steps % value.shape[axis], axis)


def scaled_coefficients(kc, kc_low, ka, mass, hoop, step, coupling):
    lane = lax.broadcasted_iota(jnp.int32, ka.shape, 1)
    last = ka.shape[1] - 1
    ka_next = jnp.where(lane == last, 0.0, ka)
    ka_low = jnp.where(lane == 0, 0.0, turn(ka, 1, 1))
    unit = (step * step) / mass
    return (
        kc * unit,
        kc_low * unit,
        ka_next * unit,
        ka_low * unit,
        (kc + kc_low + ka + ka_low) * unit,
        hoop * unit,
        (0.5 * coupling) * unit,
    )


def accelerate(now, above, below, cf):
    up, down, fore, aft, centre, hoop, cross = cf
    out = []
    for i in range(3):
        w = now[i]
        out.append(
            up * above[i]
            + down * below[i]
            + fore * turn(w, -1, 1)
            + aft * turn(w, 1, 1)
            - centre * w
        )
    out[0] = out[0] - cross * (above[2] - below[2])
    out[2] = out[2] + cross * (above[0] - below[0]) - hoop * now[2]
    return out


def accelerate_block(now, cf):
    above = [turn(w, -1, 0) for w in now]
    below = [turn(w, 1, 0) for w in now]
    return accelerate(now, above, below, cf)


def steps_block(w, q, cf, repeats):
    acc = accelerate_block(w, cf)
    for _ in range(repeats):
        half = [a + 0.5 * b for a, b in zip(q, acc)]
        w = [a + b for a, b in zip(w, half)]
        acc = accelerate_block(w, cf)
        q = [a + 0.5 * b for a, b in zip(half, acc)]
    return w, q


def three_parts(value):
    high = value.astype(jnp.bfloat16)
    rest = value - high.astype(F32)
    middle = rest.astype(jnp.bfloat16)
    low = (rest - middle.astype(F32)).astype(jnp.bfloat16)
    return high, middle, low


def exact_dot(value, matrix):
    return sum(
        jnp.dot(part, matrix, preferred_element_type=F32) for part in three_parts(value)[::-1]
    )


def averaging(cols):
    row = lax.broadcasted_iota(jnp.int32, (cols, cols // 2), 0)
    col = lax.broadcasted_iota(jnp.int32, (cols, cols // 2), 1)
    return jnp.where(row // 2 == col, 0.25, 0.0).astype(jnp.bfloat16)


def spreading(cols):
    row = lax.broadcasted_iota(jnp.int32, (cols // 2, cols), 0)
    col = lax.broadcasted_iota(jnp.int32, (cols // 2, cols), 1)
    return jnp.where(col // 2 == row, 1.0, 0.0).astype(jnp.bfloat16)


LANES = 128


class Halver:
    def __init__(self, ref):
        self.ref = ref
        self.used = 0

    def __call__(self, source, lead, start, count):
        pieces = []
        for at in range(0, source.shape[-1], LANES):
            slot = self.ref.at[self.used]
            self.used += 1
            slot[0 : 2 * count, :] = source[
                lead + (pl.ds(start, 2 * count), pl.ds(at, LANES))
            ]
            pieces.append(
                slot[pl.ds(0, count, stride=2), :] + slot[pl.ds(1, count, stride=2), :]
            )
        return jnp.concatenate(pieces, axis=1)


def halver_scratch(fields, rows, cols):
    return pltpu.VMEM((fields * (cols // LANES), rows, LANES), F32)


def is_first():
    return (lax.axis_index("cuts") == 0).astype(F32)


def pack_body(u, init, kc, ka, mass, hoop, to_above, to_below, slots):
    pair_sum = Halver(slots)
    rows, cols = kc.shape
    first = is_first()
    fields = [(u, (i,)) for i in range(6)] + [(kc, ()), (ka, ()), (mass, ()), (hoop, ())]
    at = 0
    for (ref, lead), count in zip(fields, FINE_ROWS):
        to_above[at : at + count, :] = ref[lead + (slice(rows - count, rows), slice(None))]
        to_below[at : at + count, :] = ref[lead + (slice(0, count), slice(None))]
        at += count
    matrix = averaging(cols)
    sums = []
    for start in (rows - 8, 0):
        for number, (ref, lead) in enumerate(fields):
            value = pair_sum(ref, lead, start, 4)
            if number < 6:
                value = value - first * pair_sum(init, lead, start, 4)
            sums.append(value)
    means = exact_dot(jnp.concatenate(sums, axis=0), matrix)
    half = cols // 2
    at = 0
    for number, count in enumerate(COARSE_ROWS):
        for k in range(count):
            place = (slice(FINE_TOTAL + at // 2, FINE_TOTAL + at // 2 + 1), pl.ds((at % 2) * half, half))
            low = 4 * number + 4 - count + k
            high = 40 + 4 * number + k
            to_above[place] = means[low : low + 1]
            to_below[place] = means[high : high + 1]
            at += 1


def interior_body(u, init, kc, ka, mass, hoop, f, b, cc, raw, cf, w1, half, slots):
    pair_sum = Halver(slots)
    rows, cols = kc.shape
    starts = range(0, rows, CHUNK)

    def around(ref, lead, start):
        now = ref[lead + (pl.ds(start, CHUNK), slice(None))]
        if start + CHUNK < rows:
            above = ref[lead + (pl.ds(start + 1, CHUNK), slice(None))]
        else:
            above = turn(now, -1, 0)
        if start > 0:
            below = ref[lead + (pl.ds(start - 1, CHUNK), slice(None))]
        else:
            below = turn(now, 1, 0)
        return now, above, below

    for start in starts:
        at = pl.ds(start, CHUNK)
        stiff, _, stiff_low = around(kc, (), start)
        found = scaled_coefficients(
            stiff, stiff_low, ka[at, :], mass[at, :], hoop[at, :], FINE_STEP, FINE_COUPLING
        )
        for number in range(7):
            cf[number, at, :] = found[number]
        now, above, below = zip(*[around(u, (i,), start) for i in range(3)])
        acc = accelerate(now, above, below, found)
        for i in range(3):
            moved = FINE_STEP * u[3 + i, at, :] + 0.5 * acc[i]
            half[i, at, :] = moved
            w1[i, at, :] = now[i] + moved
    for start in starts:
        at = pl.ds(start, CHUNK)
        now, above, below = zip(*[around(w1, (i,), start) for i in range(3)])
        acc = accelerate(now, above, below, [cf[number, at, :] for number in range(7)])
        for i in range(3):
            moved = half[i, at, :] + acc[i]
            half[i, at, :] = moved
            f[i, at, :] = now[i] + moved
    for start in starts:
        at = pl.ds(start, CHUNK)
        now, above, below = zip(*[around(f, (i,), start) for i in range(3)])
        acc = accelerate(now, above, below, [cf[number, at, :] for number in range(7)])
        for i in range(3):
            f[3 + i, at, :] = (half[i, at, :] + 0.5 * acc[i]) * (1.0 / FINE_STEP)

    first = is_first()
    matrix = averaging(cols)
    few = rows // 2
    half_cols = cols // 2
    for number, ref in enumerate((kc, ka, mass, hoop)):
        raw[number] = exact_dot(pair_sum(ref, (), 0, few), matrix)
    ckc, cka, cm, ch = raw[0], raw[1], raw[2], raw[3]
    found = scaled_coefficients(
        ckc, turn(ckc, 1, 0), cka, 4.0 * cm, 4.0 * ch, COARSE_STEP, COARSE_COUPLING
    )
    for number in range(7):
        cc[number, 8 : 8 + few, :] = found[number]
    sums = [pair_sum(u, (i,), 0, few) - first * pair_sum(init, (i,), 0, few) for i in range(6)]
    means = exact_dot(jnp.concatenate(sums, axis=0), matrix)
    start_w = [means[i * few : (i + 1) * few] for i in range(3)]
    start_q = [SPEED * means[(3 + i) * few : (4 + i) * few] for i in range(3)]
    moved_w, moved_q = steps_block(start_w, start_q, found, 1)
    means = exact_dot(
        jnp.concatenate([pair_sum(f, (i,), 0, few) for i in range(6)], axis=0), matrix
    )
    for i in range(3):
        b[i] = means[i * few : (i + 1) * few] - moved_w[i]
        b[3 + i] = SPEED * means[(3 + i) * few : (4 + i) * few] - moved_q[i]


def edges_body(
    f_in, u, init, kc, ka, mass, hoop, b_in, cc_in, raw, from_below, from_above,
    f, b, cc, b_to_above, b_to_below, fine, coarse, done, means_at, slots, sems,
):
    pair_sum = Halver(slots)
    rows, cols = kc.shape
    few, half_cols = rows // 2, cols // 2
    first = is_first()
    matrix = averaging(cols)
    fields = [(u, (i,)) for i in range(6)] + [(kc, ()), (ka, ()), (mass, ()), (hoop, ())]
    at = 0
    for number, ((ref, lead), count) in enumerate(zip(fields, FINE_ROWS)):
        fine[number, 8 - count : 8, :] = from_below[at : at + count, :]
        fine[number, 8:24, :] = ref[lead + (slice(0, 16), slice(None))]
        fine[number, 24:40, :] = ref[lead + (slice(rows - 16, rows), slice(None))]
        fine[number, 40 : 40 + count, :] = from_above[at : at + count, :]
        at += count
    found = scaled_coefficients(
        fine[6], turn(fine[6], 1, 0), fine[7], fine[8], fine[9], FINE_STEP, FINE_COUPLING
    )
    w, q = steps_block(
        [fine[i] for i in range(3)], [FINE_STEP * fine[3 + i] for i in range(3)], found, 2
    )
    for i in range(3):
        done[i, 0:8, :] = w[i][8:16]
        done[i, 8:16, :] = w[i][32:40]
        done[3 + i, 0:8, :] = q[i][8:16] * (1.0 / FINE_STEP)
        done[3 + i, 8:16, :] = q[i][32:40] * (1.0 / FINE_STEP)
    low = pltpu.make_async_copy(done.at[:, 0:8], f.at[:, 0:8], sems.at[0])
    high = pltpu.make_async_copy(done.at[:, 8:16], f.at[:, rows - 8 : rows], sems.at[1])
    low.start()
    high.start()

    sums = []
    for start in (0, rows - 16):
        for i in range(6):
            sums.append(pair_sum(u, (i,), start, 8) - first * pair_sum(init, (i,), start, 8))
    for i in range(6):
        sums.append(pair_sum(done, (i,), 0, 8))
    means_at[...] = exact_dot(jnp.concatenate(sums, axis=0), matrix)
    for i in range(6):
        coarse[i, 8:16, :] = means_at[8 * i : 8 * i + 8, :]
        coarse[i, 16:24, :] = means_at[48 + 8 * i : 56 + 8 * i, :]
    for number in range(4):
        coarse[6 + number, 8:16, :] = raw[number, 0:8, :]
        coarse[6 + number, 16:24, :] = raw[number, few - 8 : few, :]
    at = 0
    for number, count in enumerate(COARSE_ROWS):
        for k in range(count):
            place = (
                slice(FINE_TOTAL + at // 2, FINE_TOTAL + at // 2 + 1),
                pl.ds((at % 2) * half_cols, half_cols),
            )
            coarse[number, 8 - count + k : 9 - count + k, :] = from_below[place]
            coarse[number, 24 + k : 25 + k, :] = from_above[place]
            at += 1
    found = scaled_coefficients(
        coarse[6], turn(coarse[6], 1, 0), coarse[7], 4.0 * coarse[8], 4.0 * coarse[9],
        COARSE_STEP, COARSE_COUPLING,
    )
    for number in range(7):
        cc[number, 0:16, :] = found[number][0:16]
        cc[number, 16 : few + 4, :] = cc_in[number, 16 : few + 4, :]
        cc[number, few + 4 : few + 16, :] = found[number][20:32]
    w, q = steps_block(
        [coarse[i] for i in range(3)], [SPEED * coarse[3 + i] for i in range(3)], found, 1
    )
    moved = w + q
    b[...] = b_in[...]
    for i in range(6):
        scale = 1.0 if i < 3 else SPEED
        ends = scale * means_at[96 + 8 * i : 104 + 8 * i, :]
        b[i, 0:4, :] = ends[0:4] - moved[i][8:12]
        b[i, few - 4 : few, :] = ends[4:8] - moved[i][20:24]
    write_edges(b, b_to_above, b_to_below)
    low.wait()
    high.wait()


def write_edges(ref, to_above, to_below):
    few = ref.shape[1]
    for i in range(6):
        to_above[EDGE * i : EDGE * (i + 1), :] = ref[i, few - EDGE : few, :]
        to_below[EDGE * i : EDGE * (i + 1), :] = ref[i, 0:EDGE, :]


def fill_ext(ext, main, below, above):
    few = main.shape[1]
    for i in range(6):
        ext[i, 8 - EDGE : 8, :] = below[EDGE * i : EDGE * (i + 1), :]
        ext[i, 8 : 8 + few, :] = main[i]
        ext[i, 8 + few : 8 + few + EDGE, :] = above[EDGE * i : EDGE * (i + 1), :]


def advance(ext, cc, repeats):
    few = ext.shape[1] - 16
    w, q = steps_block(
        [ext[i] for i in range(3)],
        [ext[3 + i] for i in range(3)],
        [cc[number] for number in range(7)],
        repeats,
    )
    return [value[8 : 8 + few] for value in w + q]


def advance_body(repeats, main, below, above, add, cc, out, to_above, to_below, ext):
    fill_ext(ext, main, below, above)
    for i, value in enumerate(advance(ext, cc, repeats)):
        out[i] = value + add[i]
    write_edges(out, to_above, to_below)


def closing_body(rounds, *refs):
    mains, belows, aboves = refs[:rounds], refs[rounds : 2 * rounds], refs[2 * rounds : 3 * rounds]
    b_even, cc, total, even_end, ext, below, above = refs[3 * rounds :]
    total[...] = sum(ref[...] for ref in mains)
    below[...] = sum(ref[...] for ref in belows)
    above[...] = sum(ref[...] for ref in aboves)
    fill_ext(ext, total, below, above)
    for i, value in enumerate(advance(ext, cc, 1)):
        even_end[i] = value + b_even[i]


def spread_add(values, base, out, cols, slots):
    wide = exact_dot(values, spreading(cols))
    few = wide.shape[0] // 6
    for i in range(6):
        for tile in range(cols // LANES):
            part = wide[i * few : (i + 1) * few, tile * LANES : (tile + 1) * LANES]
            slot = slots.at[i * (cols // LANES) + tile]
            slot[pl.ds(0, few, stride=2), :] = part
            slot[pl.ds(1, few, stride=2), :] = part
            at = (i, slice(None), pl.ds(tile * LANES, LANES))
            out[at] = base[at] + slot[...]


def remainder_body(previous, init, out, slots):
    pair_sum = Halver(slots)
    cols = previous.shape[2]
    few = previous.shape[1] // 2
    sums = [pair_sum(previous, (i,), 0, few) for i in range(6)]
    means = exact_dot(jnp.concatenate(sums, axis=0), averaging(cols))
    spread_add(-means, previous, out, cols, slots)

    @pl.when(lax.axis_index("cuts") == 0)
    def _():
        out[...] = init[...]


def correct_body(base, own, received, out, slots):
    cols = base.shape[2]
    odd = lax.axis_index("cuts") % 2
    values = []
    for i in range(6):
        value = jnp.where(odd == 1, own[i], received[i])
        values.append(value if i < 3 else value * (1.0 / SPEED))
    spread_add(jnp.concatenate(values, axis=0), base, out, cols, slots)


def per_device(start_state, initial_state, circ_stiff, axial_stiff, lumped_mass, hoop_stiff):
    u = start_state[0]
    strips, slices = lax.axis_size("strip"), lax.axis_size("cuts")
    chips = slices // 2
    _, rows, cols = u.shape
    few, half_cols = rows // 2, cols // 2
    state, coarse_state = (6, rows, cols), (6, few, half_cols)
    ext_state = (6, few + 16, half_cols)
    edge = (6 * EDGE, half_cols)
    fields = (circ_stiff, axial_stiff, lumped_mass, hoop_stiff)

    def around_loop(value, by):
        pairs = [(s, (s + by) % strips) for s in range(strips)]
        return lax.ppermute(value, "strip", pairs)

    def send(value, by, moves):
        pairs = [
            (s * slices + source, (s + by) % strips * slices + target)
            for s in range(strips)
            for source, target in moves
        ]
        return lax.ppermute(value, ("strip", "cuts"), pairs)

    def send_with_edges(main, to_above, to_below, moves):
        return (
            send(main, 0, moves),
            send(to_above, 1, moves),
            send(to_below, -1, moves),
        )

    pack = (PACK_ROWS, cols)
    to_above, to_below = run(
        pack_body, "pack", [pack, pack], [u, initial_state, *fields], [halver_scratch(32, 8, cols)]
    )
    from_below = around_loop(to_above, 1)
    from_above = around_loop(to_below, -1)
    f, b, cc, raw = run(
        interior_body,
        "interior",
        [state, coarse_state, (7, few + 16, half_cols), (4, few, half_cols)],
        [u, initial_state, *fields],
        [
            pltpu.VMEM((7, rows, cols), F32),
            pltpu.VMEM((3, rows, cols), F32),
            pltpu.VMEM((3, rows, cols), F32),
            halver_scratch(22, rows, cols),
        ],
    )
    f, b, cc, b_to_above, b_to_below = run(
        edges_body,
        "edges",
        [state, coarse_state, (7, few + 16, half_cols), edge, edge],
        [f, u, initial_state, *fields, b, cc, raw, from_below, from_above],
        [
            pltpu.VMEM((10, 48, cols), F32),
            pltpu.VMEM((10, 32, half_cols), F32),
            pltpu.VMEM((6, 16, cols), F32),
            pltpu.VMEM((144, half_cols), F32),
            halver_scratch(30, 16, cols),
            pltpu.SemaphoreType.DMA((2,)),
        ],
        specs=[ANY] + [VMEM] * 11,
        out_specs=[ANY] + [VMEM] * 4,
        aliases={0: 0},
    )
    inside = [(2 * z, 2 * z + 1) for z in range(chips)]
    b_even, b_below, b_above = send_with_edges(b, b_to_above, b_to_below, inside)
    ext = [pltpu.VMEM(ext_state, F32)]

    def advance_call(repeats, name, main, below, above, add):
        return run(
            lambda *refs: advance_body(repeats, *refs),
            name,
            [coarse_state, edge, edge],
            [main, below, above, add, cc],
            ext,
        )

    source = advance_call(1, "pair", b_even, b_below, b_above, b)
    at_end = source
    arrived = []
    for chip in range(chips - 1):
        moves = [(2 * chip + 1, 2 * chip + 3)]
        arrived.append(send_with_edges(*at_end, moves))
        if chip < chips - 2:
            at_end = advance_call(2, "chain", *arrived[-1], source[0])
    previous = lax.ppermute(f, "cuts", [(j, j + 1) for j in range(slices - 1)])
    mains, belows, aboves = zip(*arrived)
    total, even_end = run(
        lambda *refs: closing_body(chips - 1, *refs),
        "closing",
        [coarse_state, coarse_state],
        [*mains, *belows, *aboves, b_even, cc],
        ext + [pltpu.VMEM(edge, F32)] * 2,
    )
    received = send(total, 0, [(2 * z + 1, 2 * z) for z in range(chips)])
    full = [halver_scratch(6, rows, cols)]
    (base,) = run(remainder_body, "remainder", [state], [previous, initial_state], full)
    (new_start,) = run(correct_body, "correct", [state], [base, even_end, received], full)
    return new_start[None], f[None]


def solution(mesh):
    state = P("cuts", None, "strip", None)
    field = P("strip", None)
    return jax.shard_map(
        per_device,
        mesh=mesh,
        in_specs=(state, P(None, "strip", None), field, field, field, field),
        out_specs=(state, state),
        check_vma=False,
    )
```

```python
import jax
import jax.numpy as jnp
from jax import lax
from jax.experimental import pallas as pl
from jax.experimental.pallas import tpu as pltpu
from jax.sharding import PartitionSpec as P

FINE_STEP = 0.35
COARSE_STEP = 0.7
FINE_COUPLING = 0.25
COARSE_COUPLING = 0.5
SPEED = COARSE_STEP

FINE_ROWS = (3, 3, 3, 2, 2, 2, 3, 2, 2, 2)
COARSE_ROWS = (2, 2, 2, 1, 1, 1, 3, 2, 2, 2)
FINE_TOTAL = sum(FINE_ROWS)
PACK_ROWS = -(-(FINE_TOTAL + -(-sum(COARSE_ROWS) // 2)) // 8) * 8
CHUNK = 8
EDGE = 4
FRONT = 3

VMEM = pl.BlockSpec(memory_space=pltpu.VMEM)
ANY = pl.BlockSpec(memory_space=pl.ANY)
HBM = pl.BlockSpec(memory_space=pltpu.HBM)
F32 = jnp.float32


def run(body, name, outs, args, scratch=(), specs=None, out_specs=None, aliases=None, cost=None):
    if specs:
        args = [
            pltpu.with_memory_space_constraint(arg, pltpu.HBM) if spec is HBM else arg
            for arg, spec in zip(args, specs)
        ]
    return pl.pallas_call(
        body,
        name=name,
        out_shape=[jax.ShapeDtypeStruct(shape, F32) for shape in outs],
        in_specs=specs or [VMEM] * len(args),
        out_specs=out_specs or [VMEM] * len(outs),
        scratch_shapes=list(scratch),
        input_output_aliases=aliases or {},
        compiler_params=pltpu.CompilerParams(vmem_limit_bytes=20 << 20),
        cost_estimate=cost
        and pl.CostEstimate(flops=cost[0], bytes_accessed=cost[1], transcendentals=0),
    )(*args)


def turn(value, steps, axis):
    return pltpu.roll(value, steps % value.shape[axis], axis)


def scaled_coefficients(kc, kc_low, ka, mass, hoop, step, coupling):
    lane = lax.broadcasted_iota(jnp.int32, ka.shape, 1)
    last = ka.shape[1] - 1
    ka_next = jnp.where(lane == last, 0.0, ka)
    ka_low = jnp.where(lane == 0, 0.0, turn(ka, 1, 1))
    unit = (step * step) / mass
    return (
        kc * unit,
        kc_low * unit,
        ka_next * unit,
        ka_low * unit,
        (kc + kc_low + ka + ka_low) * unit,
        hoop * unit,
        (0.5 * coupling) * unit,
    )


def accelerate(now, above, below, cf):
    up, down, fore, aft, centre, hoop, cross = cf
    out = []
    for i in range(3):
        w = now[i]
        out.append(
            up * above[i]
            + down * below[i]
            + fore * turn(w, -1, 1)
            + aft * turn(w, 1, 1)
            - centre * w
        )
    out[0] = out[0] - cross * (above[2] - below[2])
    out[2] = out[2] + cross * (above[0] - below[0]) - hoop * now[2]
    return out


def accelerate_block(now, cf):
    above = [turn(w, -1, 0) for w in now]
    below = [turn(w, 1, 0) for w in now]
    return accelerate(now, above, below, cf)


def steps_block(w, q, cf, repeats):
    acc = accelerate_block(w, cf)
    for _ in range(repeats):
        half = [a + 0.5 * b for a, b in zip(q, acc)]
        w = [a + b for a, b in zip(w, half)]
        acc = accelerate_block(w, cf)
        q = [a + 0.5 * b for a, b in zip(half, acc)]
    return w, q


def three_parts(value):
    high = value.astype(jnp.bfloat16)
    rest = value - high.astype(F32)
    middle = rest.astype(jnp.bfloat16)
    low = (rest - middle.astype(F32)).astype(jnp.bfloat16)
    return high, middle, low


def exact_dot(value, matrix):
    return sum(
        jnp.dot(part, matrix, preferred_element_type=F32) for part in three_parts(value)[::-1]
    )


def averaging(cols):
    row = lax.broadcasted_iota(jnp.int32, (cols, cols // 2), 0)
    col = lax.broadcasted_iota(jnp.int32, (cols, cols // 2), 1)
    return jnp.where(row // 2 == col, 0.25, 0.0).astype(jnp.bfloat16)


def spreading(cols):
    row = lax.broadcasted_iota(jnp.int32, (cols // 2, cols), 0)
    col = lax.broadcasted_iota(jnp.int32, (cols // 2, cols), 1)
    return jnp.where(col // 2 == row, 1.0, 0.0).astype(jnp.bfloat16)


LANES = 128


class Halver:
    def __init__(self, ref):
        self.ref = ref
        self.used = 0

    def __call__(self, source, lead, start, count):
        pieces = []
        for at in range(0, source.shape[-1], LANES):
            slot = self.ref.at[self.used]
            self.used += 1
            slot[0 : 2 * count, :] = source[
                lead + (pl.ds(start, 2 * count), pl.ds(at, LANES))
            ]
            pieces.append(
                slot[pl.ds(0, count, stride=2), :] + slot[pl.ds(1, count, stride=2), :]
            )
        return jnp.concatenate(pieces, axis=1)


def halver_scratch(fields, rows, cols):
    return pltpu.VMEM((fields * (cols // LANES), rows, LANES), F32)


def field_of(front, back, i):
    return (front, i) if i < FRONT else (back, i - FRONT)


def is_first():
    return (lax.axis_index("cuts") == 0).astype(F32)


def pack_body(
    u_far, init, kc_far, ka_far, mass_far, hoop_far,
    to_above, to_below, own, own_coarse, u, kc, ka, mass, hoop, early, slots, sems,
):
    rows, cols = kc.shape
    pair_sum = Halver(slots)
    first = is_first()
    copies = [(init.at[:, start : start + 8], early.at[:, pl.ds(8 * end, 8)])
              for end, start in enumerate((0, rows - 8))]
    copies += [(u_far, u), (kc_far, kc), (ka_far, ka), (mass_far, mass), (hoop_far, hoop)]
    copies = [
        pltpu.make_async_copy(source, target, sems.at[n])
        for n, (source, target) in enumerate(copies)
    ]
    for copy in copies:
        copy.start()
    matrix = averaging(cols)
    for copy in copies:
        copy.wait()
    for end, start in enumerate((0, rows - 8)):
        at = pl.ds(8 * end, 8)
        for i in range(6):
            own[i, at, :] = u[i, start : start + 8, :]
        for number, ref in enumerate((kc, ka, mass, hoop)):
            own[6 + number, at, :] = ref[start : start + 8, :]
    at = 0
    for number, count in enumerate(FINE_ROWS):
        to_above[at : at + count, :] = own[number, 16 - count : 16, :]
        to_below[at : at + count, :] = own[number, 0:count, :]
        at += count
    sums = []
    for number in range(10):
        value = pair_sum(own, (number,), 0, 8)
        if number < 6:
            value = value - first * pair_sum(early, (number,), 0, 8)
        sums.append(value)
    means = exact_dot(jnp.concatenate(sums, axis=0), matrix)
    for number in range(10):
        own_coarse[number] = means[8 * number : 8 * number + 8]
    half = cols // 2
    at = 0
    for number, count in enumerate(COARSE_ROWS):
        for k in range(count):
            line = FINE_TOTAL + at // 2
            place = (slice(line, line + 1), pl.ds((at % 2) * half, half))
            low = 8 * number + 8 - count + k
            high = 8 * number + k
            to_above[place] = means[low : low + 1]
            to_below[place] = means[high : high + 1]
            at += 1


def interior_body(
    u, init, kc, ka, mass, hoop, front, back, b, cc, f_ends,
    cf, w1, half, sums, late, slots, sem,
):
    pair_sum = Halver(slots)
    rows, cols = kc.shape
    starts = range(0, rows, CHUNK)
    first = lax.axis_index("cuts") == 0
    prescribed = pltpu.make_async_copy(init, late, sem)

    @pl.when(first)
    def _():
        prescribed.start()

    def around(ref, lead, start):
        now = ref[lead + (pl.ds(start, CHUNK), slice(None))]
        if start + CHUNK < rows:
            above = ref[lead + (pl.ds(start + 1, CHUNK), slice(None))]
        else:
            above = turn(now, -1, 0)
        if start > 0:
            below = ref[lead + (pl.ds(start - 1, CHUNK), slice(None))]
        else:
            below = turn(now, 1, 0)
        return now, above, below

    for start in starts:
        at = pl.ds(start, CHUNK)
        stiff, _, stiff_low = around(kc, (), start)
        found = scaled_coefficients(
            stiff, stiff_low, ka[at, :], mass[at, :], hoop[at, :], FINE_STEP, FINE_COUPLING
        )
        for number in range(7):
            cf[number, at, :] = found[number]
        now, above, below = zip(*[around(u, (i,), start) for i in range(3)])
        acc = accelerate(now, above, below, found)
        for i in range(3):
            moved = FINE_STEP * u[3 + i, at, :] + 0.5 * acc[i]
            half[i, at, :] = moved
            w1[i, at, :] = now[i] + moved
    for start in starts:
        at = pl.ds(start, CHUNK)
        now, above, below = zip(*[around(w1, (i,), start) for i in range(3)])
        acc = accelerate(now, above, below, [cf[number, at, :] for number in range(7)])
        for i in range(3):
            moved = half[i, at, :] + acc[i]
            half[i, at, :] = moved
            front[i, at, :] = now[i] + moved
    for start in starts:
        at = pl.ds(start, CHUNK)
        now, above, below = zip(*[around(front, (i,), start) for i in range(3)])
        acc = accelerate(now, above, below, [cf[number, at, :] for number in range(7)])
        for i in range(3):
            ref, lead = field_of(front, back, 3 + i)
            ref[lead, at, :] = (half[i, at, :] + 0.5 * acc[i]) * (1.0 / FINE_STEP)

    for i in range(6):
        ref, lead = field_of(front, back, i)
        for end, start in enumerate((0, rows - 8)):
            f_ends[i, 8 * end : 8 * end + 8, :] = ref[lead, start : start + 8, :]

    matrix = averaging(cols)
    few = rows // 2
    for i in range(6):
        sums[i * few : (i + 1) * few, :] = pair_sum(u, (i,), 0, few)
    for number, ref in enumerate((kc, ka, mass, hoop)):
        sums[(6 + number) * few : (7 + number) * few, :] = pair_sum(ref, (), 0, few)

    @pl.when(first)
    def _():
        prescribed.wait()
        for i in range(6):
            sums[i * few : (i + 1) * few, :] -= pair_sum(late, (i,), 0, few)

    means = exact_dot(sums[...], matrix)
    parts = [means[i * few : (i + 1) * few] for i in range(10)]
    ckc, cka, cm, ch = parts[6:]
    found = scaled_coefficients(
        ckc, turn(ckc, 1, 0), cka, 4.0 * cm, 4.0 * ch, COARSE_STEP, COARSE_COUPLING
    )
    for number in range(7):
        cc[number, 8 : 8 + few, :] = found[number]
    moved = sum(steps_block(parts[:3], [SPEED * q for q in parts[3:6]], found, 1), [])
    means = exact_dot(
        jnp.concatenate(
            [
                pair_sum(ref, (lead,), 0, few)
                for ref, lead in (field_of(front, back, i) for i in range(6))
            ],
            axis=0,
        ),
        matrix,
    )
    for i in range(6):
        scale = 1.0 if i < 3 else SPEED
        b[i] = scale * means[i * few : (i + 1) * few] - moved[i]


def edges_body(
    front_in, back_in, f_ends, own, own_coarse, b_in, cc_in, from_below, from_above,
    front, back, b, cc, fine, coarse, done, slots, sems,
):
    rows, cols = front.shape[1:]
    few, half_cols = rows // 2, cols // 2
    pair_sum = Halver(slots)
    at = 0
    for number, count in enumerate(FINE_ROWS):
        fine[number, 8 - count : 8, :] = from_below[at : at + count, :]
        fine[number, 8:24, :] = own[number]
        fine[number, 24 : 24 + count, :] = from_above[at : at + count, :]
        at += count
    found = scaled_coefficients(
        fine[6], turn(fine[6], 1, 0), fine[7], fine[8], fine[9], FINE_STEP, FINE_COUPLING
    )
    w, q = steps_block(
        [fine[i] for i in range(3)], [FINE_STEP * fine[3 + i] for i in range(3)], found, 2
    )
    done[...] = f_ends[...]
    for i in range(3):
        done[i, 0:4, :] = w[i][8:12]
        done[i, 12:16, :] = w[i][20:24]
        done[3 + i, 0:4, :] = q[i][8:12] * (1.0 / FINE_STEP)
        done[3 + i, 12:16, :] = q[i][20:24] * (1.0 / FINE_STEP)
    copies = []
    for n, (ref, lead) in enumerate(((front, 0), (back, FRONT))):
        for end, start in enumerate((0, rows - 8)):
            copies.append(
                pltpu.make_async_copy(
                    done.at[lead : lead + ref.shape[0], 8 * end : 8 * end + 8],
                    ref.at[:, start : start + 8],
                    sems.at[2 * n + end],
                )
            )
    for copy in copies:
        copy.start()

    sums = [pair_sum(done, (i,), 0, 8) for i in range(6)]
    means = exact_dot(jnp.concatenate(sums, axis=0), averaging(cols))
    coarse[...] = jnp.ones_like(coarse)
    at = 0
    for number, count in enumerate(COARSE_ROWS):
        coarse[number, 8:16, :] = own_coarse[number]
        for k in range(count):
            line = FINE_TOTAL + at // 2
            place = (slice(line, line + 1), pl.ds((at % 2) * half_cols, half_cols))
            coarse[number, 8 - count + k : 9 - count + k, :] = from_below[place]
            coarse[number, 16 + k : 17 + k, :] = from_above[place]
            at += 1
    found = scaled_coefficients(
        coarse[6], turn(coarse[6], 1, 0), coarse[7], 4.0 * coarse[8], 4.0 * coarse[9],
        COARSE_STEP, COARSE_COUPLING,
    )
    for number in range(7):
        cc[number, 0:12, :] = found[number][0:12]
        cc[number, 12 : few + 8, :] = cc_in[number, 12 : few + 8, :]
        cc[number, few + 8 : few + 16, :] = found[number][16:24]
    w, q = steps_block(
        [coarse[i] for i in range(3)], [SPEED * coarse[3 + i] for i in range(3)], found, 1
    )
    moved = w + q
    b[...] = b_in[...]
    for i in range(6):
        scale = 1.0 if i < 3 else SPEED
        ends = scale * means[8 * i : 8 * i + 8, :]
        b[i, 0:2, :] = ends[0:2] - moved[i][8:10]
        b[i, few - 2 : few, :] = ends[6:8] - moved[i][14:16]
    for copy in copies:
        copy.wait()


def advance(ext, cc, repeats):
    return sum(
        steps_block(
            [ext[i] for i in range(3)],
            [ext[3 + i] for i in range(3)],
            [cc[number] for number in range(7)],
            repeats,
        ),
        [],
    )


def write_edges(message, to_above, to_below):
    few = (message.shape[0] - 24) // 6
    for i in range(6):
        own, beyond, at = i * few, 6 * few + 4 * i, 4 * i
        if i < 3:
            to_above[at : at + 3, :] = message[own + few - 3 : own + few, :]
            to_above[at + 3 : at + 4, :] = message[beyond + 1 : beyond + 2, :]
            to_below[at : at + 1, :] = message[beyond : beyond + 1, :]
            to_below[at + 1 : at + 4, :] = message[own : own + 3, :]
        else:
            to_above[at : at + 2, :] = message[own + few - 2 : own + few, :]
            to_above[at + 2 : at + 4, :] = message[beyond + 2 : beyond + 4, :]
            to_below[at : at + 2, :] = message[beyond : beyond + 2, :]
            to_below[at + 2 : at + 4, :] = message[own : own + 2, :]


def read_message(ext, message, below, above):
    few = ext.shape[1] - 16
    top = 8 + few
    for i in range(6):
        own, beyond, at = i * few, 6 * few + 4 * i, 4 * i
        ext[i, 8:top, :] = message[own : own + few, :]
        if i < 3:
            ext[i, 5:8, :] = below[at : at + 3, :]
            ext[i, 7:8, :] += message[beyond : beyond + 1, :]
            ext[i, 8:9, :] += below[at + 3 : at + 4, :]
            ext[i, top - 1 : top, :] += above[at : at + 1, :]
            ext[i, top : top + 3, :] = above[at + 1 : at + 4, :]
            ext[i, top : top + 1, :] += message[beyond + 1 : beyond + 2, :]
        else:
            ext[i, 6:8, :] = below[at : at + 2, :] + message[beyond : beyond + 2, :]
            ext[i, 8:10, :] += below[at + 2 : at + 4, :]
            ext[i, top - 2 : top, :] += above[at : at + 2, :]
            ext[i, top : top + 2, :] = (
                above[at + 2 : at + 4, :] + message[beyond + 2 : beyond + 4, :]
            )


def pair_body(b_even, b_odd, cc, message, to_above, to_below, ext):
    few = ext.shape[1] - 16
    top = 8 + few
    for i in range(6):
        ext[i, 0:8, :] = jnp.zeros_like(ext[i, 0:8, :])
        ext[i, 8:top, :] = b_even[i]
        ext[i, top : top + 8, :] = jnp.zeros_like(ext[i, 0:8, :])
    for i, value in enumerate(advance(ext, cc, 1)):
        own, beyond = i * few, 6 * few + 4 * i
        message[own : own + few, :] = value[8:top] + b_odd[i]
        if i < 3:
            message[beyond : beyond + 1, :] = value[7:8]
            message[beyond + 1 : beyond + 2, :] = value[top : top + 1]
            message[beyond + 2 : beyond + 4, :] = jnp.zeros_like(value[0:2])
        else:
            message[beyond : beyond + 2, :] = value[6:8]
            message[beyond + 2 : beyond + 4, :] = value[top : top + 2]
    write_edges(message, to_above, to_below)


def chain_body(message, below, above, source, cc, *refs):
    out, to_above, to_below, ext = refs[-4:]
    few = ext.shape[1] - 16
    ext[...] = jnp.zeros_like(ext)
    read_message(ext, message, below, above)
    for i, value in enumerate(advance(ext, cc, 2)):
        own = i * few
        out[own : own + few, :] = value[8 : 8 + few] + source[own : own + few, :]
    out[6 * few :, :] = source[6 * few :, :]
    write_edges(out, to_above, to_below)


def collect_body(rounds, *refs):
    messages, belows, aboves = [refs[k * rounds : (k + 1) * rounds] for k in range(3)]
    total, ext, message, below, above = refs[3 * rounds + 2 :]
    message[...] = sum(ref[...] for ref in messages)
    below[...] = sum(ref[...] for ref in belows)
    above[...] = sum(ref[...] for ref in aboves)
    ext[...] = jnp.zeros_like(ext)
    read_message(ext, message, below, above)
    for i in range(6):
        total[i] = ext[i, 8 : ext.shape[1] - 8, :]


def even_body(ext, b_even, cc, even_end):
    few = ext.shape[1] - 16
    for i, value in enumerate(advance(ext, cc, 1)):
        even_end[i] = value[8 : 8 + few] + b_even[i]


def second_body(front, back, after, out):
    @pl.when(lax.axis_index("cuts") == 1)
    def _():
        out[...] = front[...]

    @pl.when(lax.axis_index("cuts") != 1)
    def _():
        out[...] = back[...]


def third_body(back, after, out):
    out[...] = back[...]


def join_body(front, back, out, sems):
    low = pltpu.make_async_copy(front, out.at[0:FRONT], sems.at[0])
    high = pltpu.make_async_copy(back, out.at[FRONT:6], sems.at[1])
    low.start()
    high.start()
    low.wait()
    high.wait()


def spread_add(values, bases, outs, slots):
    cols = 2 * values.shape[1]
    wide = exact_dot(values, spreading(cols))
    few = wide.shape[0] // len(outs)
    for i, (base, out) in enumerate(zip(bases, outs)):
        for tile in range(cols // LANES):
            part = wide[i * few : (i + 1) * few, tile * LANES : (tile + 1) * LANES]
            slot = slots.at[i * (cols // LANES) + tile]
            slot[pl.ds(0, few, stride=2), :] = part
            slot[pl.ds(1, few, stride=2), :] = part
            at = (slice(None), pl.ds(tile * LANES, LANES))
            out[at] = base[at] + slot[...]


def remainder(parts, out, slots):
    pair_sum = Halver(slots)
    cols = out.shape[2]
    few = out.shape[1] // 2
    sums = [pair_sum(part, (), 0, few) for _, part in parts]
    means = exact_dot(jnp.concatenate(sums, axis=0), averaging(cols))
    spread_add(-means, [part for _, part in parts], [out.at[i] for i, _ in parts], slots)


def early_body(front, back, init, out, slots, sem):
    fields = [field_of(front, back, i) for i in range(6)]
    remainder([(i, ref.at[lead]) for i, (ref, lead) in enumerate(fields)], out, slots)

    @pl.when(lax.axis_index("cuts") == 0)
    def _():
        copy = pltpu.make_async_copy(init, out, sem)
        copy.start()
        copy.wait()


def late_body(base_in, front, back, base, slots, made, sems):
    place = lax.axis_index("cuts")
    for n, (lead, ref, found) in enumerate(
        ((0, front, place == 2), (FRONT, back, (place == 2) | (place == 4)))
    ):
        count = ref.shape[0]

        @pl.when(found)
        def _():
            remainder([(lead + i, ref.at[i]) for i in range(count)], made, slots)
            part = pl.ds(lead, count)
            copy = pltpu.make_async_copy(made.at[part], base.at[part], sems.at[n])
            copy.start()
            copy.wait()


def correct_body(base, own, received, out, slots, made, sems):
    odd = lax.axis_index("cuts") % 2
    copies = []
    for lead in (0, 3):
        values = []
        for i in range(lead, lead + 3):
            value = jnp.where(odd == 1, received[i], own[i])
            values.append(value if i < 3 else value * (1.0 / SPEED))
        part = [lead, lead + 1, lead + 2]
        spread_add(
            jnp.concatenate(values, axis=0),
            [base.at[i] for i in part],
            [made.at[i] for i in part],
            slots,
        )
        copies.append(
            pltpu.make_async_copy(
                made.at[pl.ds(lead, 3)], out.at[pl.ds(lead, 3)], sems.at[lead // 3]
            )
        )
        copies[-1].start()
    for copy in copies:
        copy.wait()


def per_device(start_state, initial_state, circ_stiff, axial_stiff, lumped_mass, hoop_stiff):
    u = start_state[0]
    strips, slices = lax.axis_size("strip"), lax.axis_size("cuts")
    chips = slices // 2
    _, rows, cols = u.shape
    few, half_cols = rows // 2, cols // 2
    state, coarse_state = (6, rows, cols), (6, few, half_cols)
    ext_state = (6, few + 16, half_cols)
    edge = (6 * EDGE, half_cols)
    fields = (circ_stiff, axial_stiff, lumped_mass, hoop_stiff)

    def around_loop(value, by):
        pairs = [(s, (s + by) % strips) for s in range(strips)]
        return lax.ppermute(value, "strip", pairs)

    def send(value, by, moves):
        pairs = [
            (s * slices + source, (s + by) % strips * slices + target)
            for s in range(strips)
            for source, target in moves
        ]
        return lax.ppermute(value, ("strip", "cuts"), pairs)

    def send_with_edges(main, to_above, to_below, moves):
        return (
            send(main, 0, moves),
            send(to_above, 1, moves),
            send(to_below, -1, moves),
        )

    pack = (PACK_ROWS, cols)
    half_state = (3, rows, cols)
    front_state, back_state = (FRONT, rows, cols), (6 - FRONT, rows, cols)
    ends = (6, 16, cols)
    message = (6 * few + 24, half_cols)
    cc_shape = (7, few + 16, half_cols)
    to_above, to_below, own, own_coarse, u_near, *near = run(
        pack_body,
        "pack",
        [pack, pack, (10, 16, cols), (10, 8, half_cols), state] + [(rows, cols)] * 4,
        [u, initial_state, *fields],
        [
            pltpu.VMEM(ends, F32),
            halver_scratch(16, 16, cols),
            pltpu.SemaphoreType.DMA((7,)),
        ],
        specs=[HBM] * 6,
    )
    from_below = around_loop(to_above, 1)
    from_above = around_loop(to_below, -1)
    front, back, b, cc, f_ends = run(
        interior_body,
        "interior",
        [front_state, back_state, coarse_state, cc_shape, ends],
        [u_near, initial_state, *near],
        [
            pltpu.VMEM((7, rows, cols), F32),
            pltpu.VMEM(half_state, F32),
            pltpu.VMEM(half_state, F32),
            pltpu.VMEM((10 * few, cols), F32),
            pltpu.VMEM(state, F32),
            halver_scratch(22, rows, cols),
            pltpu.SemaphoreType.DMA,
        ],
        specs=[VMEM, HBM] + [VMEM] * 4,
    )
    front, back, b, cc = run(
        edges_body,
        "edges",
        [front_state, back_state, coarse_state, cc_shape],
        [front, back, f_ends, own, own_coarse, b, cc, from_below, from_above],
        [
            pltpu.VMEM((10, 32, cols), F32),
            pltpu.VMEM((10, 24, half_cols), F32),
            pltpu.VMEM(ends, F32),
            halver_scratch(6, 16, cols),
            pltpu.SemaphoreType.DMA((4,)),
        ],
        specs=[ANY] * 2 + [VMEM] * 7,
        out_specs=[ANY] * 2 + [VMEM] * 2,
        aliases={0: 0, 1: 1},
    )
    ext = [pltpu.VMEM(ext_state, F32)]
    inside = [(2 * z, 2 * z + 1) for z in range(chips)]
    swap = inside + [(odd, even) for even, odd in inside]
    b_other = send(b, 0, swap)
    source = run(pair_body, "pair", [message, edge, edge], [b, b_other, cc], ext)

    def hops(links):
        return [(2 * z + 1, 2 * z + 2) for z in links if 0 <= z < chips - 1]

    sent_first = send(front, 0, inside + hops(range(1, chips)))
    at_end = source
    arrived = []
    for chip in range(chips - 1):
        arrived.append(send_with_edges(*at_end, [(2 * chip, 2 * chip + 2)]))
        if chip < chips - 2:
            extra = [sent_first] * (chip == 1)
            at_end = run(
                chain_body,
                "chain",
                [message, edge, edge],
                [*arrived[-1], source[0], cc] + extra,
                ext,
                specs=[VMEM] * 5 + [ANY] * len(extra),
            )
        if chip == 0:
            (part,) = run(
                second_body, "second", [back_state], [front, back, at_end[1]],
                specs=[VMEM, VMEM, ANY],
            )
            sent_second = send(part, 0, inside + hops([0, *range(2, chips)]))
        if chip == 1:
            (part,) = run(
                third_body, "third", [back_state], [back, at_end[1]], specs=[VMEM, ANY]
            )
            sent_third = send(part, 0, hops([0, 1]))
    messages, belows, aboves = zip(*arrived)
    (fine_end,) = run(
        join_body,
        "join",
        [state],
        [front, back],
        [pltpu.SemaphoreType.DMA((2,))],
        specs=[ANY] * 2,
        out_specs=[ANY],
        cost=(0, 6 * rows * cols * 8),
    )
    rem_scratch = [
        halver_scratch(6, rows, cols),
        pltpu.VMEM(state, F32),
        pltpu.SemaphoreType.DMA((2,)),
    ]
    (base,) = run(
        early_body,
        "remainder",
        [state],
        [sent_first, sent_second, initial_state],
        [halver_scratch(6, rows, cols), pltpu.SemaphoreType.DMA],
        specs=[VMEM, VMEM, HBM],
        cost=(0, 6 * rows * cols * 8),
    )
    total, wide = run(
        lambda *refs: collect_body(chips - 1, *refs),
        "collect",
        [coarse_state, ext_state],
        [*messages, *belows, *aboves, base, fine_end],
        [pltpu.VMEM(message, F32), pltpu.VMEM(edge, F32), pltpu.VMEM(edge, F32)],
        specs=[VMEM] * (3 * len(messages)) + [ANY, HBM],
    )
    (even_end,) = run(even_body, "even", [coarse_state], [wide, b, cc])
    received = send(even_end, 0, swap)
    (base,) = run(
        late_body,
        "late",
        [state],
        [base, sent_second, sent_third],
        rem_scratch,
        specs=[ANY, VMEM, VMEM],
        out_specs=[ANY],
        aliases={0: 0},
    )
    (new_start,) = run(
        correct_body,
        "correct",
        [state],
        [base, total, received],
        rem_scratch,
        out_specs=[HBM],
    )
    return new_start[None], fine_end[None]


def solution(mesh):
    state = P("cuts", None, "strip", None)
    field = P("strip", None)
    return jax.shard_map(
        per_device,
        mesh=mesh,
        in_specs=(state, P(None, "strip", None), field, field, field, field),
        out_specs=(state, state),
        check_vma=False,
    )
```

```python
import jax
import jax.numpy as jnp
from jax import lax
from jax.experimental import pallas as pl
from jax.experimental.pallas import tpu as pltpu
from jax.sharding import PartitionSpec as P

FINE_STEP = 0.35
COARSE_STEP = 0.7
FINE_COUPLING = 0.25
COARSE_COUPLING = 0.5
SPEED = COARSE_STEP

FINE_ROWS = (3, 3, 3, 2, 2, 2, 3, 2, 2, 2)
COARSE_ROWS = (2, 2, 2, 1, 1, 1, 3, 2, 2, 2)
FINE_TOTAL = sum(FINE_ROWS)
PACK_ROWS = -(-(FINE_TOTAL + -(-sum(COARSE_ROWS) // 2)) // 8) * 8
CHUNK = 16
MARGIN = 8
EDGE = 4

VMEM = pl.BlockSpec(memory_space=pltpu.VMEM)
ANY = pl.BlockSpec(memory_space=pl.ANY)
HBM = pl.BlockSpec(memory_space=pltpu.HBM)
F32 = jnp.float32


def run(body, name, outs, args, scratch=(), specs=None, out_specs=None, aliases=None, cost=None):
    if specs:
        args = [
            pltpu.with_memory_space_constraint(arg, pltpu.HBM) if spec is HBM else arg
            for arg, spec in zip(args, specs)
        ]
    return pl.pallas_call(
        body,
        name=name,
        out_shape=[jax.ShapeDtypeStruct(shape, F32) for shape in outs],
        in_specs=specs or [VMEM] * len(args),
        out_specs=out_specs or [VMEM] * len(outs),
        scratch_shapes=list(scratch),
        input_output_aliases=aliases or {},
        compiler_params=pltpu.CompilerParams(vmem_limit_bytes=20 << 20),
        cost_estimate=cost
        and pl.CostEstimate(flops=cost[0], bytes_accessed=cost[1], transcendentals=0),
    )(*args)


def turn(value, steps, axis):
    return pltpu.roll(value, steps % value.shape[axis], axis)


def scaled_coefficients(kc, kc_low, ka, mass, hoop, step, coupling):
    lane = lax.broadcasted_iota(jnp.int32, ka.shape, 1)
    last = ka.shape[1] - 1
    ka_next = jnp.where(lane == last, 0.0, ka)
    ka_low = jnp.where(lane == 0, 0.0, turn(ka, 1, 1))
    unit = (step * step) / mass
    return (
        kc * unit,
        kc_low * unit,
        ka_next * unit,
        ka_low * unit,
        (kc + kc_low + ka + ka_low) * unit,
        hoop * unit,
        (0.5 * coupling) * unit,
    )


def accelerate(now, above, below, cf):
    up, down, fore, aft, centre, hoop, cross = cf
    out = []
    for i in range(3):
        w = now[i]
        out.append(
            up * above[i]
            + down * below[i]
            + fore * turn(w, -1, 1)
            + aft * turn(w, 1, 1)
            - centre * w
        )
    out[0] = out[0] - cross * (above[2] - below[2])
    out[2] = out[2] + cross * (above[0] - below[0]) - hoop * now[2]
    return out


def accelerate_block(now, cf):
    above = [turn(w, -1, 0) for w in now]
    below = [turn(w, 1, 0) for w in now]
    return accelerate(now, above, below, cf)


def steps_block(w, q, cf, repeats):
    acc = accelerate_block(w, cf)
    for _ in range(repeats):
        half = [a + 0.5 * b for a, b in zip(q, acc)]
        w = [a + b for a, b in zip(w, half)]
        acc = accelerate_block(w, cf)
        q = [a + 0.5 * b for a, b in zip(half, acc)]
    return w, q


def three_parts(value):
    high = value.astype(jnp.bfloat16)
    rest = value - high.astype(F32)
    middle = rest.astype(jnp.bfloat16)
    low = (rest - middle.astype(F32)).astype(jnp.bfloat16)
    return high, middle, low


def exact_dot(value, matrix):
    return sum(
        jnp.dot(part, matrix, preferred_element_type=F32) for part in three_parts(value)[::-1]
    )


def averaging(cols):
    row = lax.broadcasted_iota(jnp.int32, (cols, cols // 2), 0)
    col = lax.broadcasted_iota(jnp.int32, (cols, cols // 2), 1)
    return jnp.where(row // 2 == col, 0.25, 0.0).astype(jnp.bfloat16)


def spreading(cols):
    row = lax.broadcasted_iota(jnp.int32, (cols // 2, cols), 0)
    col = lax.broadcasted_iota(jnp.int32, (cols // 2, cols), 1)
    return jnp.where(col // 2 == row, 1.0, 0.0).astype(jnp.bfloat16)


LANES = 128


class Halver:
    def __init__(self, ref):
        self.ref = ref
        self.used = 0

    def __call__(self, source, lead, start, count):
        pieces = []
        for at in range(0, source.shape[-1], LANES):
            assert self.used < self.ref.shape[0] and 2 * count <= self.ref.shape[1]
            slot = self.ref.at[self.used]
            self.used += 1
            slot[0 : 2 * count, :] = source[
                lead + (pl.ds(start, 2 * count), pl.ds(at, LANES))
            ]
            pieces.append(
                slot[pl.ds(0, count, stride=2), :] + slot[pl.ds(1, count, stride=2), :]
            )
        return jnp.concatenate(pieces, axis=1)


def halver_scratch(fields, rows, cols):
    return pltpu.VMEM((fields * (cols // LANES), rows, LANES), F32)


def is_first():
    return (lax.axis_index("cuts") == 0).astype(F32)


def pack_body(
    u_far, init, kc_far, ka_far, mass_far, hoop_far,
    to_above, to_below, own, own_coarse, u, kc, ka, mass, hoop, middle, early, slots, sems,
):
    rows, cols = kc.shape
    pair_sum = Halver(slots)
    first = is_first()
    copies = [(init.at[:, start : start + 8], early.at[:, pl.ds(8 * end, 8)])
              for end, start in enumerate((0, rows - 8))]
    copies += [(u_far, u), (kc_far, kc), (ka_far, ka), (mass_far, mass), (hoop_far, hoop)]
    copies = [
        pltpu.make_async_copy(source, target, sems.at[n])
        for n, (source, target) in enumerate(copies)
    ]
    for copy in copies:
        copy.start()
    matrix = averaging(cols)
    for copy in copies:
        copy.wait()
    for end, start in enumerate((0, rows - 8)):
        at = pl.ds(8 * end, 8)
        for i in range(6):
            own[i, at, :] = u[i, start : start + 8, :]
        for number, ref in enumerate((kc, ka, mass, hoop)):
            own[6 + number, at, :] = ref[start : start + 8, :]
    at = 0
    for number, count in enumerate(FINE_ROWS):
        to_above[at : at + count, :] = own[number, 16 - count : 16, :]
        to_below[at : at + count, :] = own[number, 0:count, :]
        at += count
    sums = []
    for number in range(10):
        value = pair_sum(own, (number,), 0, 8)
        if number < 6:
            value = value - first * pair_sum(early, (number,), 0, 8)
        sums.append(value)
    means = exact_dot(jnp.concatenate(sums, axis=0), matrix)
    for number in range(10):
        own_coarse[number] = means[8 * number : 8 * number + 8]
    half = cols // 2
    at = 0
    for number, count in enumerate(COARSE_ROWS):
        for k in range(count):
            line = FINE_TOTAL + at // 2
            place = (slice(line, line + 1), pl.ds((at % 2) * half, half))
            low = 8 * number + 8 - count + k
            high = 8 * number + k
            to_above[place] = means[low : low + 1]
            to_below[place] = means[high : high + 1]
            at += 1
    lead = rows // 4 - MARGIN
    middle[...] = u[:, lead : rows - lead, :]


def propagate(u, coefficients, w1, half, f):
    rows = u.shape[1]
    chunk = CHUNK if rows % CHUNK == 0 else 8
    starts = range(0, rows, chunk)

    def around(ref, start):
        found = []
        for i in range(3):
            now = ref[i, start : start + chunk, :]
            if start + chunk < rows:
                above = ref[i, start + 1 : start + chunk + 1, :]
            else:
                above = turn(now, -1, 0)
            if start > 0:
                below = ref[i, start - 1 : start + chunk - 1, :]
            else:
                below = turn(now, 1, 0)
            found.append((now, above, below))
        return zip(*found)

    for start in starts:
        at = pl.ds(start, chunk)
        now, above, below = around(u, start)
        acc = accelerate(now, above, below, coefficients(start, chunk, True))
        for i in range(3):
            moved = FINE_STEP * u[3 + i, at, :] + 0.5 * acc[i]
            half[i, at, :] = moved
            w1[i, at, :] = now[i] + moved
    for start in starts:
        at = pl.ds(start, chunk)
        now, above, below = around(w1, start)
        acc = accelerate(now, above, below, coefficients(start, chunk, False))
        for i in range(3):
            moved = half[i, at, :] + acc[i]
            half[i, at, :] = moved
            f[i, at, :] = now[i] + moved
    for start in starts:
        at = pl.ds(start, chunk)
        now, above, below = around(f, start)
        acc = accelerate(now, above, below, coefficients(start, chunk, False))
        for i in range(3):
            f[3 + i, at, :] = (half[i, at, :] + 0.5 * acc[i]) * (1.0 / FINE_STEP)


def interior_body(
    u, init, kc, ka, mass, hoop, f, b, cc, cf, w1, half, sums, late, slots, sem
):
    pair_sum = Halver(slots)
    rows, cols = kc.shape
    first = lax.axis_index("cuts") == 0
    prescribed = pltpu.make_async_copy(init, late, sem)

    @pl.when(first)
    def _():
        prescribed.start()

    def coefficients(start, count, fresh):
        at = pl.ds(start, count)
        if not fresh:
            return [cf[number, at, :] for number in range(7)]
        stiff = kc[at, :]
        stiff_low = kc[start - 1 : start + count - 1, :] if start else turn(stiff, 1, 0)
        found = scaled_coefficients(
            stiff, stiff_low, ka[at, :], mass[at, :], hoop[at, :], FINE_STEP, FINE_COUPLING
        )
        for number in range(7):
            cf[number, at, :] = found[number]
        return found

    propagate(u, coefficients, w1, half, f)

    matrix = averaging(cols)
    few = rows // 2
    for i in range(6):
        sums[i * few : (i + 1) * few, :] = pair_sum(u, (i,), 0, few)
    for number, ref in enumerate((kc, ka, mass, hoop)):
        sums[(6 + number) * few : (7 + number) * few, :] = pair_sum(ref, (), 0, few)

    @pl.when(first)
    def _():
        prescribed.wait()
        for i in range(6):
            sums[i * few : (i + 1) * few, :] -= pair_sum(late, (i,), 0, few)

    means = exact_dot(sums[...], matrix)
    parts = [means[i * few : (i + 1) * few] for i in range(10)]
    ckc, cka, cm, ch = parts[6:]
    found = scaled_coefficients(
        ckc, turn(ckc, 1, 0), cka, 4.0 * cm, 4.0 * ch, COARSE_STEP, COARSE_COUPLING
    )
    for number in range(7):
        cc[number, 8 : 8 + few, :] = found[number]
    moved = sum(steps_block(parts[:3], [SPEED * q for q in parts[3:6]], found, 1), [])
    means = exact_dot(
        jnp.concatenate([pair_sum(f, (i,), 0, few) for i in range(6)], axis=0), matrix
    )
    for i in range(6):
        scale = 1.0 if i < 3 else SPEED
        b[i] = scale * means[i * few : (i + 1) * few] - moved[i]


def edges_body(
    f, own, own_coarse, b_in, cc_in, from_below, from_above,
    done, b, cc, fine, coarse, slots,
):
    rows, cols = f.shape[1:]
    few, half_cols = rows // 2, cols // 2
    pair_sum = Halver(slots)
    at = 0
    for number, count in enumerate(FINE_ROWS):
        fine[number, 8 - count : 8, :] = from_below[at : at + count, :]
        fine[number, 8:24, :] = own[number]
        fine[number, 24 : 24 + count, :] = from_above[at : at + count, :]
        at += count
    found = scaled_coefficients(
        fine[6], turn(fine[6], 1, 0), fine[7], fine[8], fine[9], FINE_STEP, FINE_COUPLING
    )
    w, q = steps_block(
        [fine[i] for i in range(3)], [FINE_STEP * fine[3 + i] for i in range(3)], found, 2
    )
    for i in range(6):
        done[i, 0:8, :] = f[i, 0:8, :]
        done[i, 8:16, :] = f[i, rows - 8 : rows, :]
    for i in range(3):
        done[i, 0:4, :] = w[i][8:12]
        done[i, 12:16, :] = w[i][20:24]
        done[3 + i, 0:4, :] = q[i][8:12] * (1.0 / FINE_STEP)
        done[3 + i, 12:16, :] = q[i][20:24] * (1.0 / FINE_STEP)

    sums = [pair_sum(done, (i,), 0, 8) for i in range(6)]
    means = exact_dot(jnp.concatenate(sums, axis=0), averaging(cols))
    coarse[...] = jnp.ones_like(coarse)
    at = 0
    for number, count in enumerate(COARSE_ROWS):
        coarse[number, 8:16, :] = own_coarse[number]
        for k in range(count):
            line = FINE_TOTAL + at // 2
            place = (slice(line, line + 1), pl.ds((at % 2) * half_cols, half_cols))
            coarse[number, 8 - count + k : 9 - count + k, :] = from_below[place]
            coarse[number, 16 + k : 17 + k, :] = from_above[place]
            at += 1
    found = scaled_coefficients(
        coarse[6], turn(coarse[6], 1, 0), coarse[7], 4.0 * coarse[8], 4.0 * coarse[9],
        COARSE_STEP, COARSE_COUPLING,
    )
    for number in range(7):
        cc[number, 0:12, :] = found[number][0:12]
        cc[number, 12 : few + 8, :] = cc_in[number, 12 : few + 8, :]
        cc[number, few + 8 : few + 16, :] = found[number][16:24]
    w, q = steps_block(
        [coarse[i] for i in range(3)], [SPEED * coarse[3 + i] for i in range(3)], found, 1
    )
    moved = w + q
    b[...] = b_in[...]
    for i in range(6):
        scale = 1.0 if i < 3 else SPEED
        ends = scale * means[8 * i : 8 * i + 8, :]
        b[i, 0:2, :] = ends[0:2] - moved[i][8:10]
        b[i, few - 2 : few, :] = ends[6:8] - moved[i][14:16]


def advance(ext, cc, repeats):
    return sum(
        steps_block(
            [ext[i] for i in range(3)],
            [ext[3 + i] for i in range(3)],
            [cc[number] for number in range(7)],
            repeats,
        ),
        [],
    )


def write_edges(message, to_above, to_below):
    few = (message.shape[0] - 24) // 6
    for i in range(6):
        own, beyond, at = i * few, 6 * few + 4 * i, 4 * i
        if i < 3:
            to_above[at : at + 3, :] = message[own + few - 3 : own + few, :]
            to_above[at + 3 : at + 4, :] = message[beyond + 1 : beyond + 2, :]
            to_below[at : at + 1, :] = message[beyond : beyond + 1, :]
            to_below[at + 1 : at + 4, :] = message[own : own + 3, :]
        else:
            to_above[at : at + 2, :] = message[own + few - 2 : own + few, :]
            to_above[at + 2 : at + 4, :] = message[beyond + 2 : beyond + 4, :]
            to_below[at : at + 2, :] = message[beyond : beyond + 2, :]
            to_below[at + 2 : at + 4, :] = message[own : own + 2, :]


def read_message(ext, message, below, above):
    few = ext.shape[1] - 16
    top = 8 + few
    for i in range(6):
        own, beyond, at = i * few, 6 * few + 4 * i, 4 * i
        ext[i, 8:top, :] = message[own : own + few, :]
        if i < 3:
            ext[i, 5:8, :] = below[at : at + 3, :]
            ext[i, 7:8, :] += message[beyond : beyond + 1, :]
            ext[i, 8:9, :] += below[at + 3 : at + 4, :]
            ext[i, top - 1 : top, :] += above[at : at + 1, :]
            ext[i, top : top + 3, :] = above[at + 1 : at + 4, :]
            ext[i, top : top + 1, :] += message[beyond + 1 : beyond + 2, :]
        else:
            ext[i, 6:8, :] = below[at : at + 2, :] + message[beyond : beyond + 2, :]
            ext[i, 8:10, :] += below[at + 2 : at + 4, :]
            ext[i, top - 2 : top, :] += above[at : at + 2, :]
            ext[i, top : top + 2, :] = (
                above[at + 2 : at + 4, :] + message[beyond + 2 : beyond + 4, :]
            )


def pair_body(b_even, b_odd, cc, message, to_above, to_below, ext):
    few = ext.shape[1] - 16
    top = 8 + few
    for i in range(6):
        ext[i, 0:8, :] = jnp.zeros_like(ext[i, 0:8, :])
        ext[i, 8:top, :] = b_even[i]
        ext[i, top : top + 8, :] = jnp.zeros_like(ext[i, 0:8, :])
    for i, value in enumerate(advance(ext, cc, 1)):
        own, beyond = i * few, 6 * few + 4 * i
        message[own : own + few, :] = value[8:top] + b_odd[i]
        if i < 3:
            message[beyond : beyond + 1, :] = value[7:8]
            message[beyond + 1 : beyond + 2, :] = value[top : top + 1]
            message[beyond + 2 : beyond + 4, :] = jnp.zeros_like(value[0:2])
        else:
            message[beyond : beyond + 2, :] = value[6:8]
            message[beyond + 2 : beyond + 4, :] = value[top : top + 2]
    write_edges(message, to_above, to_below)


def chain_body(message, below, above, source, cc, *refs):
    out, to_above, to_below, ext = refs[-4:]
    few = ext.shape[1] - 16
    ext[...] = jnp.zeros_like(ext)
    read_message(ext, message, below, above)
    for i, value in enumerate(advance(ext, cc, 2)):
        own = i * few
        out[own : own + few, :] = value[8 : 8 + few] + source[own : own + few, :]
    out[6 * few :, :] = source[6 * few :, :]
    write_edges(out, to_above, to_below)


def collect_body(rounds, *refs):
    messages, belows, aboves = [refs[k * rounds : (k + 1) * rounds] for k in range(3)]
    total, ext = refs[3 * rounds + 2 :]
    chip = lax.axis_index("cuts") // 2
    ext[...] = jnp.zeros_like(ext)
    for number in range(rounds):

        @pl.when(chip == number + 1)
        def _():
            read_message(ext, messages[number], belows[number], aboves[number])

    for i in range(6):
        total[i] = ext[i, 8 : ext.shape[1] - 8, :]


def even_body(ext, b_even, cc, even_end):
    few = ext.shape[1] - 16
    for i, value in enumerate(advance(ext, cc, 1)):
        even_end[i] = value[8 : 8 + few] + b_even[i]


def outer_body(f, ends, out):
    rows = f.shape[1]
    quarter = rows // 4
    out[:, 0:8, :] = ends[:, 0:8, :]
    out[:, 8:quarter, :] = f[:, 8:quarter, :]
    out[:, quarter : 2 * quarter - 8, :] = f[:, rows - quarter : rows - 8, :]
    out[:, 2 * quarter - 8 : 2 * quarter, :] = ends[:, 8:16, :]


def copy_body(value, after, out):
    out[...] = value[...]


def again_body(u, cf, out, w1, half, made):
    lead = cf.shape[1] // 4 - MARGIN

    def coefficients(start, count, fresh):
        return [cf[number, lead + start : lead + start + count, :] for number in range(7)]

    propagate(u, coefficients, w1, half, made)
    out[...] = made[:, MARGIN : made.shape[1] - MARGIN, :]


def join_body(f, ends, out, sems):
    rows = f.shape[1]
    copies = [
        pltpu.make_async_copy(f.at[:, 8 : rows - 8], out.at[:, 8 : rows - 8], sems.at[0]),
        pltpu.make_async_copy(ends.at[:, 0:8], out.at[:, 0:8], sems.at[1]),
        pltpu.make_async_copy(ends.at[:, 8:16], out.at[:, rows - 8 : rows], sems.at[2]),
    ]
    for copy in copies:
        copy.start()
    for copy in copies:
        copy.wait()


def spread_add(values, bases, outs, slots):
    cols = 2 * values.shape[1]
    wide = exact_dot(values, spreading(cols))
    few = wide.shape[0] // len(outs)
    for i, (base, out) in enumerate(zip(bases, outs)):
        for tile in range(cols // LANES):
            part = wide[i * few : (i + 1) * few, tile * LANES : (tile + 1) * LANES]
            assert i * (cols // LANES) + tile < slots.shape[0] and 2 * few <= slots.shape[1]
            slot = slots.at[i * (cols // LANES) + tile]
            slot[pl.ds(0, few, stride=2), :] = part
            slot[pl.ds(1, few, stride=2), :] = part
            at = (slice(None), pl.ds(tile * LANES, LANES))
            out[at] = base[at] + slot[0 : 2 * few, :]


def remainder(parts, outs, slots):
    pair_sum = Halver(slots)
    cols = parts[0].shape[1]
    few = parts[0].shape[0] // 2
    sums = [pair_sum(part, (), 0, few) for part in parts]
    means = exact_dot(jnp.concatenate(sums, axis=0), averaging(cols))
    spread_add(-means, parts, outs, slots)


def outer_parts(ref, quarter):
    rows = ref.shape[1]
    ends = (pl.ds(0, quarter), pl.ds(rows - quarter, quarter))
    return [ref.at[i, end] for i in range(6) for end in ends]


def early_body(inner, outer, after_hop, init, out, picked, slots, sem):
    place = lax.axis_index("cuts")
    rows = out.shape[1]
    quarter = rows // 4
    middle = pl.ds(quarter, rows // 2)

    @pl.when(place == 2)
    def _():
        picked[...] = after_hop[...]

    @pl.when(place != 2)
    def _():
        picked[...] = outer[...]

    @pl.when(place != 0)
    def _():
        remainder(
            [inner.at[i] for i in range(6)], [out.at[i, middle] for i in range(6)], slots
        )
        remainder(outer_parts(picked, quarter), outer_parts(out, quarter), slots)

    @pl.when(place == 0)
    def _():
        copy = pltpu.make_async_copy(init, out, sem)
        copy.start()
        copy.wait()


def correct_body(base, own, received, out, slots, made, sems):
    odd = lax.axis_index("cuts") % 2
    copies = []
    for lead in (0, 3):
        values = []
        for i in range(lead, lead + 3):
            value = jnp.where(odd == 1, received[i], own[i])
            values.append(value if i < 3 else value * (1.0 / SPEED))
        part = [lead, lead + 1, lead + 2]
        spread_add(
            jnp.concatenate(values, axis=0),
            [base.at[i] for i in part],
            [made.at[i] for i in part],
            slots,
        )
        copies.append(
            pltpu.make_async_copy(
                made.at[pl.ds(lead, 3)], out.at[pl.ds(lead, 3)], sems.at[lead // 3]
            )
        )
        copies[-1].start()
    for copy in copies:
        copy.wait()


def per_device(start_state, initial_state, circ_stiff, axial_stiff, lumped_mass, hoop_stiff):
    u = start_state[0]
    strips, slices = lax.axis_size("strip"), lax.axis_size("cuts")
    chips = slices // 2
    _, rows, cols = u.shape
    few, half_cols = rows // 2, cols // 2
    state, coarse_state = (6, rows, cols), (6, few, half_cols)
    ext_state = (6, few + 16, half_cols)
    edge = (6 * EDGE, half_cols)
    fields = (circ_stiff, axial_stiff, lumped_mass, hoop_stiff)

    def around_loop(value, by):
        pairs = [(s, (s + by) % strips) for s in range(strips)]
        return lax.ppermute(value, "strip", pairs)


    def along_cuts(value, moves):
        rest = [j for j in range(slices) if j not in moves]
        pairs = list(moves.items()) + [(j, j ^ 1) for j in rest]
        assert sorted(target for _, target in pairs) == list(range(slices))
        return lax.ppermute(value, "cuts", pairs)

    def hop(value, by, chip):
        a, b = 2 * chip, 2 * chip + 2
        pairs = []
        for s in range(strips):
            here, there = s * slices, (s + by) % strips * slices
            pairs += [(here + a, there + b), (there + b, there + b + 1)]
            pairs += [(there + b + 1, here + a + 1), (here + a + 1, here + a)]
            pairs += [(here + j, here + (j ^ 1)) for j in range(slices) if not a <= j < a + 4]
        return lax.ppermute(value, ("strip", "cuts"), pairs)

    def hop_with_edges(main, to_above, to_below, chip):
        return hop(main, 0, chip), hop(to_above, 1, chip), hop(to_below, -1, chip)

    pack = (PACK_ROWS, cols)
    third = (3, rows, cols)
    ends_shape = (6, 16, cols)
    message = (6 * few + 24, half_cols)
    cc_shape, cf_shape = (7, few + 16, half_cols), (7, rows, cols)
    middle_shape = (6, few + 2 * MARGIN, cols)
    outer_shape = (6, few, cols)
    to_above, to_below, own, own_coarse, u_near, *near, middle = run(
        pack_body,
        "pack",
        [pack, pack, (10, 16, cols), (10, 8, half_cols), state]
        + [(rows, cols)] * 4
        + [middle_shape],
        [u, initial_state, *fields],
        [
            pltpu.VMEM(ends_shape, F32),
            halver_scratch(16, 16, cols),
            pltpu.SemaphoreType.DMA((7,)),
        ],
        specs=[HBM] * 6,
    )
    from_below = around_loop(to_above, 1)
    from_above = around_loop(to_below, -1)
    raw = along_cuts(middle, {j: (j + 1) % slices for j in range(slices)})
    f, b, cc, cf = run(
        interior_body,
        "interior",
        [state, coarse_state, cc_shape, cf_shape],
        [u_near, initial_state, *near],
        [
            pltpu.VMEM(third, F32),
            pltpu.VMEM(third, F32),
            pltpu.VMEM((10 * few, cols), F32),
            pltpu.VMEM(state, F32),
            halver_scratch(22, rows, cols),
            pltpu.SemaphoreType.DMA,
        ],
        specs=[VMEM, HBM] + [VMEM] * 4,
    )
    ends, b, cc = run(
        edges_body,
        "edges",
        [ends_shape, coarse_state, cc_shape],
        [f, own, own_coarse, b, cc, from_below, from_above],
        [
            pltpu.VMEM((10, 32, cols), F32),
            pltpu.VMEM((10, 24, half_cols), F32),
            halver_scratch(6, 16, cols),
        ],
    )
    ext = [pltpu.VMEM(ext_state, F32)]
    b_other = along_cuts(b, {})
    source = run(pair_body, "pair", [message, edge, edge], [b, b_other, cc], ext)
    (outer,) = run(outer_body, "outer", [outer_shape], [f, ends])

    previous = along_cuts(outer, {j: j + 1 for j in range(2, slices - 1)} | {slices - 1: 2})
    at_end = source
    arrived = []
    for chip in range(chips - 1):
        arrived.append(hop_with_edges(*at_end, chip))
        if chip < chips - 2:
            extra = {0: [raw], 1: [previous]}.get(chip, [])
            at_end = run(
                chain_body,
                "chain",
                [message, edge, edge],
                [*arrived[-1], source[0], cc] + extra,
                ext,
                specs=[VMEM] * 5 + [ANY] * len(extra),
            )
        if chip == 0:
            (part,) = run(
                copy_body, "later", [outer_shape], [outer, at_end[1]], specs=[VMEM, ANY]
            )
            after_hop = lax.ppermute(part, "cuts", [(1, 2)])
    messages, belows, aboves = zip(*arrived)
    (fine_end,) = run(
        join_body,
        "join",
        [state],
        [f, ends],
        [pltpu.SemaphoreType.DMA((3,))],
        specs=[ANY] * 2,
        out_specs=[ANY],
        cost=(0, 6 * rows * cols * 8),
    )
    (inner,) = run(
        again_body,
        "again",
        [outer_shape],
        [raw, cf],
        [pltpu.VMEM((3,) + middle_shape[1:], F32)] * 2 + [pltpu.VMEM(middle_shape, F32)],
        cost=(0, 6 * rows * cols * 8),
    )
    rem_scratch = [
        halver_scratch(12, rows, cols),
        pltpu.VMEM(state, F32),
        pltpu.SemaphoreType.DMA((2,)),
    ]
    (base,) = run(
        early_body,
        "remainder",
        [state],
        [inner, previous, after_hop, initial_state],
        [
            pltpu.VMEM(outer_shape, F32),
            halver_scratch(12, few, cols),
            pltpu.SemaphoreType.DMA,
        ],
        specs=[VMEM] * 3 + [HBM],
        cost=(0, 6 * rows * cols * 8),
    )
    total, wide = run(
        lambda *refs: collect_body(chips - 1, *refs),
        "collect",
        [coarse_state, ext_state],
        [*messages, *belows, *aboves, base, fine_end],
        specs=[VMEM] * (3 * len(messages)) + [ANY, HBM],
    )
    (even_end,) = run(even_body, "even", [coarse_state], [wide, b, cc])
    received = along_cuts(even_end, {})
    (new_start,) = run(
        correct_body,
        "correct",
        [state],
        [base, total, received],
        rem_scratch,
        out_specs=[HBM],
    )
    return new_start[None], fine_end[None]


def solution(mesh):
    state = P("cuts", None, "strip", None)
    field = P("strip", None)
    return jax.shard_map(
        per_device,
        mesh=mesh,
        in_specs=(state, P(None, "strip", None), field, field, field, field),
        out_specs=(state, state),
        check_vma=False,
    )
```

```python
import jax
import jax.numpy as jnp
from jax import lax
from jax.experimental import pallas as pl
from jax.experimental.pallas import tpu as pltpu
from jax.sharding import PartitionSpec as P

FINE_STEP = 0.35
COARSE_STEP = 0.7
FINE_COUPLING = 0.25
COARSE_COUPLING = 0.5
SPEED = COARSE_STEP

FINE_ROWS = (3, 3, 3, 2, 2, 2, 3, 2, 2, 2)
COARSE_ROWS = (2, 2, 2, 1, 1, 1, 6, 5, 5, 5)
FINE_TOTAL = sum(FINE_ROWS)
PACK_ROWS = -(-(FINE_TOTAL + -(-sum(COARSE_ROWS) // 2)) // 8) * 8
CHUNK = 16
HALO_COST = int(3.4e9)
LAST_COST = int(1e9)
MARGIN = 8

VMEM = pl.BlockSpec(memory_space=pltpu.VMEM)
ANY = pl.BlockSpec(memory_space=pl.ANY)
HBM = pl.BlockSpec(memory_space=pltpu.HBM)
F32 = jnp.float32


def run(body, name, outs, args, scratch=(), specs=None, out_specs=None, aliases=None, cost=None):
    if specs:
        args = [
            pltpu.with_memory_space_constraint(arg, pltpu.HBM) if spec is HBM else arg
            for arg, spec in zip(args, specs)
        ]
    return pl.pallas_call(
        body,
        name=name,
        out_shape=[jax.ShapeDtypeStruct(shape, F32) for shape in outs],
        in_specs=specs or [VMEM] * len(args),
        out_specs=out_specs or [VMEM] * len(outs),
        scratch_shapes=list(scratch),
        input_output_aliases=aliases or {},
        compiler_params=pltpu.CompilerParams(vmem_limit_bytes=20 << 20),
        cost_estimate=cost
        and pl.CostEstimate(flops=cost[0], bytes_accessed=cost[1], transcendentals=0),
    )(*args)


def turn(value, steps, axis):
    return pltpu.roll(value, steps % value.shape[axis], axis)


def scaled_coefficients(kc, kc_low, ka, mass, hoop, step, coupling):
    lane = lax.broadcasted_iota(jnp.int32, ka.shape, 1)
    last = ka.shape[1] - 1
    ka_next = jnp.where(lane == last, 0.0, ka)
    ka_low = jnp.where(lane == 0, 0.0, turn(ka, 1, 1))
    unit = (step * step) / mass
    return (
        kc * unit,
        kc_low * unit,
        ka_next * unit,
        ka_low * unit,
        (kc + kc_low + ka + ka_low) * unit,
        hoop * unit,
        (0.5 * coupling) * unit,
    )


def accelerate(now, above, below, cf):
    up, down, fore, aft, centre, hoop, cross = cf
    out = []
    for i in range(3):
        w = now[i]
        out.append(
            up * above[i]
            + down * below[i]
            + fore * turn(w, -1, 1)
            + aft * turn(w, 1, 1)
            - centre * w
        )
    out[0] = out[0] - cross * (above[2] - below[2])
    out[2] = out[2] + cross * (above[0] - below[0]) - hoop * now[2]
    return out


def accelerate_block(now, cf):
    above = [turn(w, -1, 0) for w in now]
    below = [turn(w, 1, 0) for w in now]
    return accelerate(now, above, below, cf)


def steps_block(w, q, cf, repeats):
    acc = accelerate_block(w, cf)
    for _ in range(repeats):
        half = [a + 0.5 * b for a, b in zip(q, acc)]
        w = [a + b for a, b in zip(w, half)]
        acc = accelerate_block(w, cf)
        q = [a + 0.5 * b for a, b in zip(half, acc)]
    return w, q


def three_parts(value):
    high = value.astype(jnp.bfloat16)
    rest = value - high.astype(F32)
    middle = rest.astype(jnp.bfloat16)
    low = (rest - middle.astype(F32)).astype(jnp.bfloat16)
    return high, middle, low


def exact_dot(value, matrix):
    return sum(
        jnp.dot(part, matrix, preferred_element_type=F32) for part in three_parts(value)[::-1]
    )


def averaging(cols):
    row = lax.broadcasted_iota(jnp.int32, (cols, cols // 2), 0)
    col = lax.broadcasted_iota(jnp.int32, (cols, cols // 2), 1)
    return jnp.where(row // 2 == col, 0.25, 0.0).astype(jnp.bfloat16)


def spreading(cols):
    row = lax.broadcasted_iota(jnp.int32, (cols // 2, cols), 0)
    col = lax.broadcasted_iota(jnp.int32, (cols // 2, cols), 1)
    return jnp.where(col // 2 == row, 1.0, 0.0).astype(jnp.bfloat16)


LANES = 128


class Halver:
    def __init__(self, ref):
        self.ref = ref
        self.used = 0

    def __call__(self, source, lead, start, count):
        pieces = []
        for at in range(0, source.shape[-1], LANES):
            assert self.used < self.ref.shape[0] and 2 * count <= self.ref.shape[1]
            slot = self.ref.at[self.used]
            self.used += 1
            slot[0 : 2 * count, :] = source[
                lead + (pl.ds(start, 2 * count), pl.ds(at, LANES))
            ]
            pieces.append(
                slot[pl.ds(0, count, stride=2), :] + slot[pl.ds(1, count, stride=2), :]
            )
        return jnp.concatenate(pieces, axis=1)


def halver_scratch(fields, rows, cols):
    return pltpu.VMEM((fields * (cols // LANES), rows + 8, LANES), F32)


def is_first():
    return (lax.axis_index("cuts") == 0).astype(F32)


def pack_body(
    u_far, init, kc_far, ka_far, mass_far, hoop_far,
    to_above, to_below, own, own_coarse, u, kc, ka, mass, hoop, middle, early, slots, sems,
):
    rows, cols = kc.shape
    pair_sum = Halver(slots)
    first = is_first()
    copies = [
        (init.at[:, start : start + 16], early.at[:, pl.ds(16 * end, 16)])
        for end, start in enumerate((0, rows - 16))
    ]
    copies += [(u_far, u), (kc_far, kc), (ka_far, ka), (mass_far, mass), (hoop_far, hoop)]
    copies = [
        pltpu.make_async_copy(source, target, sems.at[n])
        for n, (source, target) in enumerate(copies)
    ]
    for copy in copies:
        copy.start()
    matrix = averaging(cols)
    for copy in copies:
        copy.wait()
    for end, start in enumerate((0, rows - 8)):
        at = pl.ds(8 * end, 8)
        for i in range(6):
            own[i, at, :] = u[i, start : start + 8, :]
        for number, ref in enumerate((kc, ka, mass, hoop)):
            own[6 + number, at, :] = ref[start : start + 8, :]
    at = 0
    for number, count in enumerate(FINE_ROWS):
        to_above[at : at + count, :] = own[number, 16 - count : 16, :]
        to_below[at : at + count, :] = own[number, 0:count, :]
        at += count
    sums = []
    for start in (rows - 16, 0):
        for number, ref in enumerate([u] * 6 + [kc, ka, mass, hoop]):
            value = pair_sum(ref, (number,) if number < 6 else (), start, 8)
            if number < 6:
                value = value - first * pair_sum(early, (number,), 16 * (start > 0), 8)
            sums.append(value)
    means = exact_dot(jnp.concatenate(sums, axis=0), matrix)
    half = cols // 2
    at = 0
    for number, count in enumerate(COARSE_ROWS):
        high, low = means[8 * number : 8 * number + 8], means[80 + 8 * number : 88 + 8 * number]
        own_coarse[number, 0:4, :] = low[0:4]
        own_coarse[number, 4:8, :] = high[4:8]
        for k in range(count):
            line = FINE_TOTAL + at // 2
            place = (slice(line, line + 1), pl.ds((at % 2) * half, half))
            to_above[place] = high[8 - count + k : 9 - count + k]
            to_below[place] = low[k : k + 1]
            at += 1
    lead = rows // 4 - MARGIN
    middle[...] = u[:, lead : rows - lead, :]


def propagate(u, coefficients, w1, half, f):
    rows = u.shape[1]
    chunk = CHUNK if rows % CHUNK == 0 else 8
    starts = range(0, rows, chunk)

    def around(ref, start):
        found = []
        for i in range(3):
            now = ref[i, start : start + chunk, :]
            if start + chunk < rows:
                above = ref[i, start + 1 : start + chunk + 1, :]
            else:
                above = turn(now, -1, 0)
            if start > 0:
                below = ref[i, start - 1 : start + chunk - 1, :]
            else:
                below = turn(now, 1, 0)
            found.append((now, above, below))
        return zip(*found)

    for start in starts:
        at = pl.ds(start, chunk)
        now, above, below = around(u, start)
        acc = accelerate(now, above, below, coefficients(start, chunk, True))
        for i in range(3):
            moved = FINE_STEP * u[3 + i, at, :] + 0.5 * acc[i]
            half[i, at, :] = moved
            w1[i, at, :] = now[i] + moved
    for start in starts:
        at = pl.ds(start, chunk)
        now, above, below = around(w1, start)
        acc = accelerate(now, above, below, coefficients(start, chunk, False))
        for i in range(3):
            moved = half[i, at, :] + acc[i]
            half[i, at, :] = moved
            f[i, at, :] = now[i] + moved
    for start in starts:
        at = pl.ds(start, chunk)
        now, above, below = around(f, start)
        acc = accelerate(now, above, below, coefficients(start, chunk, False))
        for i in range(3):
            f[3 + i, at, :] = (half[i, at, :] + 0.5 * acc[i]) * (1.0 / FINE_STEP)


def interior_body(
    u, init, kc, ka, mass, hoop, f, b, cc, cf, w1, half, sums, late, slots, sem
):
    pair_sum = Halver(slots)
    rows, cols = kc.shape
    first = lax.axis_index("cuts") == 0
    prescribed = pltpu.make_async_copy(init, late, sem)

    @pl.when(first)
    def _():
        prescribed.start()

    def coefficients(start, count, fresh):
        at = pl.ds(start, count)
        if not fresh:
            return [cf[number, at, :] for number in range(7)]
        stiff = kc[at, :]
        stiff_low = kc[start - 1 : start + count - 1, :] if start else turn(stiff, 1, 0)
        found = scaled_coefficients(
            stiff, stiff_low, ka[at, :], mass[at, :], hoop[at, :], FINE_STEP, FINE_COUPLING
        )
        for number in range(7):
            cf[number, at, :] = found[number]
        return found

    propagate(u, coefficients, w1, half, f)

    matrix = averaging(cols)
    few = rows // 2
    for i in range(6):
        sums[i * few : (i + 1) * few, :] = pair_sum(u, (i,), 0, few)
    for number, ref in enumerate((kc, ka, mass, hoop)):
        sums[(6 + number) * few : (7 + number) * few, :] = pair_sum(ref, (), 0, few)

    @pl.when(first)
    def _():
        prescribed.wait()
        for i in range(6):
            sums[i * few : (i + 1) * few, :] -= pair_sum(late, (i,), 0, few)

    means = exact_dot(sums[...], matrix)
    parts = [means[i * few : (i + 1) * few] for i in range(10)]
    ckc, cka, cm, ch = parts[6:]
    found = scaled_coefficients(
        ckc, turn(ckc, 1, 0), cka, 4.0 * cm, 4.0 * ch, COARSE_STEP, COARSE_COUPLING
    )
    for number in range(7):
        cc[number, 8 : 8 + few, :] = found[number]
    moved = sum(steps_block(parts[:3], [SPEED * q for q in parts[3:6]], found, 1), [])
    means = exact_dot(
        jnp.concatenate([pair_sum(f, (i,), 0, few) for i in range(6)], axis=0), matrix
    )
    for i in range(6):
        scale = 1.0 if i < 3 else SPEED
        b[i] = scale * means[i * few : (i + 1) * few] - moved[i]


def edges_body(
    f, own, own_coarse, b_in, cc_in, from_below, from_above,
    done, b, cc, fine, coarse, slots,
):
    rows, cols = f.shape[1:]
    few, half_cols = rows // 2, cols // 2
    pair_sum = Halver(slots)
    at = 0
    for number, count in enumerate(FINE_ROWS):
        fine[number, 8 - count : 8, :] = from_below[at : at + count, :]
        fine[number, 8:24, :] = own[number]
        fine[number, 24 : 24 + count, :] = from_above[at : at + count, :]
        at += count
    found = scaled_coefficients(
        fine[6], turn(fine[6], 1, 0), fine[7], fine[8], fine[9], FINE_STEP, FINE_COUPLING
    )
    w, q = steps_block(
        [fine[i] for i in range(3)], [FINE_STEP * fine[3 + i] for i in range(3)], found, 2
    )
    for i in range(6):
        done[i, 0:8, :] = f[i, 0:8, :]
        done[i, 8:16, :] = f[i, rows - 8 : rows, :]
    for i in range(3):
        done[i, 0:4, :] = w[i][8:12]
        done[i, 12:16, :] = w[i][20:24]
        done[3 + i, 0:4, :] = q[i][8:12] * (1.0 / FINE_STEP)
        done[3 + i, 12:16, :] = q[i][20:24] * (1.0 / FINE_STEP)

    sums = [pair_sum(done, (i,), 0, 8) for i in range(6)]
    means = exact_dot(jnp.concatenate(sums, axis=0), averaging(cols))
    coarse[...] = jnp.ones_like(coarse)
    at = 0
    for number, count in enumerate(COARSE_ROWS):
        coarse[number, 8:16, :] = own_coarse[number]
        for k in range(count):
            line = FINE_TOTAL + at // 2
            place = (slice(line, line + 1), pl.ds((at % 2) * half_cols, half_cols))
            coarse[number, 8 - count + k : 9 - count + k, :] = from_below[place]
            coarse[number, 16 + k : 17 + k, :] = from_above[place]
            at += 1
    found = scaled_coefficients(
        coarse[6], turn(coarse[6], 1, 0), coarse[7], 4.0 * coarse[8], 4.0 * coarse[9],
        COARSE_STEP, COARSE_COUPLING,
    )
    for number in range(7):
        cc[number, 0:12, :] = found[number][0:12]
        cc[number, 12 : few + 8, :] = cc_in[number, 12 : few + 8, :]
        cc[number, few + 8 : few + 16, :] = found[number][16:24]
    w, q = steps_block(
        [coarse[i] for i in range(3)], [SPEED * coarse[3 + i] for i in range(3)], found, 1
    )
    moved = w + q
    b[...] = b_in[...]
    for i in range(6):
        scale = 1.0 if i < 3 else SPEED
        ends = scale * means[8 * i : 8 * i + 8, :]
        b[i, 0:2, :] = ends[0:2] - moved[i][8:10]
        b[i, few - 2 : few, :] = ends[6:8] - moved[i][14:16]


def advance(ext, cc, repeats):
    return sum(
        steps_block(
            [ext[i] for i in range(3)],
            [ext[3 + i] for i in range(3)],
            [cc[number] for number in range(7)],
            repeats,
        ),
        [],
    )


def write_edges(message, to_above, to_below):
    few = (message.shape[0] - 24) // 6
    lines = to_above.shape[0] // 6
    for i in range(6):
        own, beyond, at = i * few, 6 * few + 4 * i, lines * i
        extra = 1 if i < 3 else 2
        rows = lines - extra
        to_above[at : at + rows, :] = message[own + few - rows : own + few, :]
        to_above[at + rows : at + lines, :] = message[beyond + extra : beyond + 2 * extra, :]
        to_below[at : at + extra, :] = message[beyond : beyond + extra, :]
        to_below[at + extra : at + lines, :] = message[own : own + rows, :]


def read_message(ext, message, below, above):
    few = ext.shape[1] - 16
    top = 8 + few
    lines = below.shape[0] // 6
    for i in range(6):
        own, beyond, at = i * few, 6 * few + 4 * i, lines * i
        extra = 1 if i < 3 else 2
        rows = lines - extra
        ext[i, 8:top, :] = message[own : own + few, :]
        ext[i, 8 - rows : 8, :] = below[at : at + rows, :]
        ext[i, top : top + rows, :] = above[at + extra : at + lines, :]
        ext[i, 8 - extra : 8, :] += message[beyond : beyond + extra, :]
        ext[i, top : top + extra, :] += message[beyond + extra : beyond + 2 * extra, :]
        ext[i, 8 : 8 + extra, :] += below[at + rows : at + lines, :]
        ext[i, top - extra : top, :] += above[at : at + extra, :]


def halves(ref):
    return ref.at[0], ref.at[1]


def pair_body(b_even, b_odd, cc, message, to_above, to_below, ext):
    few = ext.shape[1] - 16
    top = 8 + few
    for i in range(6):
        ext[i, 0:8, :] = jnp.zeros_like(ext[i, 0:8, :])
        ext[i, 8:top, :] = b_even[i]
        ext[i, top : top + 8, :] = jnp.zeros_like(ext[i, 0:8, :])
    for i, value in enumerate(advance(ext, cc, 1)):
        own, beyond = i * few, 6 * few + 4 * i
        message[own : own + few, :] = value[8:top] + b_odd[i]
        if i < 3:
            message[beyond : beyond + 1, :] = value[7:8]
            message[beyond + 1 : beyond + 2, :] = value[top : top + 1]
            message[beyond + 2 : beyond + 4, :] = jnp.zeros_like(value[0:2])
        else:
            message[beyond : beyond + 2, :] = value[6:8]
            message[beyond + 2 : beyond + 4, :] = value[top : top + 2]
    write_edges(message, to_above, to_below)


def halo_body(below, above, out):
    out[0] = below[...]
    out[1] = above[...]


def chain_body(message, halo, source, cc, *refs):
    out, to_above, to_below, ext = refs[-4:]
    below, above = halves(halo)
    few = ext.shape[1] - 16
    ext[...] = jnp.zeros_like(ext)
    read_message(ext, message, below, above)
    for i, value in enumerate(advance(ext, cc, 2)):
        own = i * few
        out[own : own + few, :] = value[8 : 8 + few] + source[own : own + few, :]
    out[6 * few :, :] = source[6 * few :, :]
    write_edges(out, to_above, to_below)


def collect_body(rounds, *refs):
    messages, halos = refs[:rounds], refs[rounds : 2 * rounds]
    total, ext = refs[2 * rounds + 2 :]
    chip = lax.axis_index("cuts") // 2
    ext[...] = jnp.zeros_like(ext)
    for number in range(rounds):

        @pl.when(chip == number + 1)
        def _():
            read_message(ext, messages[number], *halves(halos[number]))

    for i in range(6):
        total[i] = ext[i, 8 : ext.shape[1] - 8, :]


def leap_body(message, halo, source, halo_source, cc, *refs):
    out, ext, add = refs[-3:]
    chip = lax.axis_index("cuts") // 2
    rows = ext.shape[1]

    @pl.when((chip == 1) | (chip == 2))
    def _():
        add[...] = jnp.zeros_like(add)
        read_message(add, source, *halves(halo_source))

    @pl.when(chip == 1)
    def _():
        ext[...] = jnp.zeros_like(ext)
        read_message(ext, message, *halves(halo))
        for i, value in enumerate(advance(ext, cc, 2)):
            out[i] = (value + add[i])[4 : rows - 4]

    @pl.when(chip == 2)
    def _():
        out[...] = add[:, 4 : rows - 4, :]


def last_body(leaped, cc, out, ext):
    rows = ext.shape[1]

    @pl.when(lax.axis_index("cuts") // 2 == 3)
    def _():
        ext[...] = jnp.zeros_like(ext)
        ext[:, 4 : rows - 4, :] = leaped[...]
        for i, value in enumerate(advance(ext, cc, 2)):
            out[i] = value


def arrive_body(message, halo, last, step, *refs):
    total, ext = refs[-2:]
    chip = lax.axis_index("cuts") // 2
    rows = ext.shape[1]
    ext[...] = jnp.zeros_like(ext)

    @pl.when(chip == 1)
    def _():
        read_message(ext, message, *halves(halo))

    @pl.when(chip >= 2)
    def _():
        ext[:, 4 : rows - 4, :] = step[...]

    @pl.when(chip == 3)
    def _():
        ext[...] += last[...]

    for i in range(6):
        total[i] = ext[i, 8 : rows - 8, :]


def even_body(ext, b_even, cc, even_end):
    few = ext.shape[1] - 16
    for i, value in enumerate(advance(ext, cc, 1)):
        even_end[i] = value[8 : 8 + few] + b_even[i]


def outer_body(f, ends, out):
    rows = f.shape[1]
    quarter = rows // 4
    out[:, 0:8, :] = ends[:, 0:8, :]
    out[:, 8:quarter, :] = f[:, 8:quarter, :]
    out[:, quarter : 2 * quarter - 8, :] = f[:, rows - quarter : rows - 8, :]
    out[:, 2 * quarter - 8 : 2 * quarter, :] = ends[:, 8:16, :]


def copy_body(value, after, out):
    out[...] = value[...]


def again_body(u, cf, out, w1, half, made):
    lead = cf.shape[1] // 4 - MARGIN

    def coefficients(start, count, fresh):
        return [cf[number, lead + start : lead + start + count, :] for number in range(7)]

    propagate(u, coefficients, w1, half, made)
    out[...] = made[:, MARGIN : made.shape[1] - MARGIN, :]


def join_body(f, ends, out, sems):
    rows = f.shape[1]
    copies = [
        pltpu.make_async_copy(f.at[:, 8 : rows - 8], out.at[:, 8 : rows - 8], sems.at[0]),
        pltpu.make_async_copy(ends.at[:, 0:8], out.at[:, 0:8], sems.at[1]),
        pltpu.make_async_copy(ends.at[:, 8:16], out.at[:, rows - 8 : rows], sems.at[2]),
    ]
    for copy in copies:
        copy.start()
    for copy in copies:
        copy.wait()


def spread_add(values, bases, outs, slots):
    cols = 2 * values.shape[1]
    wide = exact_dot(values, spreading(cols))
    few = wide.shape[0] // len(outs)
    for i, (base, out) in enumerate(zip(bases, outs)):
        for tile in range(cols // LANES):
            part = wide[i * few : (i + 1) * few, tile * LANES : (tile + 1) * LANES]
            assert i * (cols // LANES) + tile < slots.shape[0] and 2 * few <= slots.shape[1]
            slot = slots.at[i * (cols // LANES) + tile]
            slot[pl.ds(0, few, stride=2), :] = part
            slot[pl.ds(1, few, stride=2), :] = part
            at = (slice(None), pl.ds(tile * LANES, LANES))
            out[at] = base[at] + slot[0 : 2 * few, :]


def remainder(parts, outs, slots):
    pair_sum = Halver(slots)
    cols = parts[0].shape[1]
    few = parts[0].shape[0] // 2
    sums = [pair_sum(part, (), 0, few) for part in parts]
    means = exact_dot(jnp.concatenate(sums, axis=0), averaging(cols))
    spread_add(-means, parts, outs, slots)


def outer_parts(ref, quarter):
    rows = ref.shape[1]
    ends = (pl.ds(0, quarter), pl.ds(rows - quarter, quarter))
    return [ref.at[i, end] for i in range(6) for end in ends]


def early_body(inner, outer, init, out, slots, sem):
    place = lax.axis_index("cuts")
    rows = out.shape[1]
    quarter = rows // 4
    middle = pl.ds(quarter, rows // 2)

    @pl.when(place != 0)
    def _():
        remainder(
            [inner.at[i] for i in range(6)], [out.at[i, middle] for i in range(6)], slots
        )
        remainder(outer_parts(outer, quarter), outer_parts(out, quarter), slots)

    @pl.when(place == 0)
    def _():
        copy = pltpu.make_async_copy(init, out, sem)
        copy.start()
        copy.wait()


def late_body(base_in, after_hop, base, slots, made, sems):
    rows = base.shape[1]
    quarter = rows // 4

    @pl.when(lax.axis_index("cuts") == 2)
    def _():
        remainder(outer_parts(after_hop, quarter), outer_parts(made, quarter), slots)
        copies = [
            pltpu.make_async_copy(
                made.at[:, pl.ds(n * quarter, quarter)],
                base.at[:, pl.ds(start, quarter)],
                sems.at[n],
            )
            for n, start in enumerate((0, rows - quarter))
        ]
        for copy in copies:
            copy.start()
        for copy in copies:
            copy.wait()


def correct_body(base, own, received, out, slots, made, sems):
    odd = lax.axis_index("cuts") % 2
    cols = base.shape[2]
    copies = []
    for lead in range(0, 6, 2):
        part = range(lead, lead + 2)
        values = []
        for i in part:
            value = jnp.where(odd == 1, received[i], own[i])
            values.append(value if i < 3 else value * (1.0 / SPEED))
        spread_add(
            jnp.concatenate(values, axis=0),
            [base.at[i] for i in part],
            [made.at[i] for i in part],
            slots.at[pl.ds(cols // LANES * lead, cols // LANES * 2)],
        )
        copies.append(
            pltpu.make_async_copy(
                made.at[pl.ds(lead, 2)], out.at[pl.ds(lead, 2)], sems.at[lead // 2]
            )
        )
        copies[-1].start()
    for copy in copies:
        copy.wait()


def per_device(start_state, initial_state, circ_stiff, axial_stiff, lumped_mass, hoop_stiff):
    u = start_state[0]
    strips, slices = lax.axis_size("strip"), lax.axis_size("cuts")
    chips = slices // 2
    _, rows, cols = u.shape
    few, half_cols = rows // 2, cols // 2
    state, coarse_state = (6, rows, cols), (6, few, half_cols)
    ext_state = (6, few + 16, half_cols)
    leap = chips == 4
    reach = 7 if leap else 3
    edge = (6 * (reach + 1), half_cols)
    fields = (circ_stiff, axial_stiff, lumped_mass, hoop_stiff)

    def around_loop(value, by):
        pairs = [(s, (s + by) % strips) for s in range(strips)]
        return lax.ppermute(value, "strip", pairs)


    def along_cuts(value, moves):
        rest = [j for j in range(slices) if j not in moves]
        pairs = list(moves.items()) + [(j, j ^ 1) for j in rest]
        assert sorted(target for _, target in pairs) == list(range(slices))
        return lax.ppermute(value, "cuts", pairs)

    def hop(value, by, chip):
        third = None
        if chip > 0:
            third = chip + 2 if chip + 2 < chips else chip - 1
        used = {chip, chip + 1, third}
        pairs = []
        for s in range(strips):
            here, there = s * slices, (s + by) % strips * slices
            a, b = here + 2 * chip, there + 2 * chip + 2
            path = [a, b, b + 1]
            if third is not None:
                path += [there + 2 * third, there + 2 * third + 1]
            path.append(a + 1)
            pairs += list(zip(path, path[1:] + path[:1]))
            pairs += [(here + j, here + (j ^ 1)) for j in range(slices) if j // 2 not in used]
        assert sorted(target for _, target in pairs) == list(range(strips * slices))
        return lax.ppermute(value, ("strip", "cuts"), pairs)

    def hop_with_edges(main, to_above, to_below, move):
        edges = [move(to_above, 1), move(to_below, -1)]
        (halo,) = run(
            halo_body, "halo", [(2,) + edge], edges, cost=(HALO_COST, HALO_COST)
        )
        return move(main, 0), halo

    def to_chip_1(value, by):
        pairs = []
        for s in range(strips):
            here, there, beyond = (slices * ((s + k * by) % strips) for k in range(3))
            path = [here, there + 2, beyond + 3, here + 1]
            pairs += list(zip(path, path[1:] + path[:1]))
            for j in range(4, slices, 2):
                pairs += [(here + j, there + j + 1), (here + j + 1, here + j)]
        assert sorted(target for _, target in pairs) == list(range(strips * slices))
        return lax.ppermute(value, ("strip", "cuts"), pairs)

    def around_cuts(value, *path):
        return along_cuts(value, dict(zip(path, path[1:] + path[:1])))

    pack = (PACK_ROWS, cols)
    third = (3, rows, cols)
    ends_shape = (6, 16, cols)
    message = (6 * few + 24, half_cols)
    cc_shape, cf_shape = (7, few + 16, half_cols), (7, rows, cols)
    middle_shape = (6, few + 2 * MARGIN, cols)
    outer_shape = (6, few, cols)
    to_above, to_below, own, own_coarse, u_near, *near, middle = run(
        pack_body,
        "pack",
        [pack, pack, (10, 16, cols), (10, 8, half_cols), state]
        + [(rows, cols)] * 4
        + [middle_shape],
        [u, initial_state, *fields],
        [
            pltpu.VMEM((6, 32, cols), F32),
            halver_scratch(32, 16, cols),
            pltpu.SemaphoreType.DMA((7,)),
        ],
        specs=[HBM] * 6,
    )
    from_below = around_loop(to_above, 1)
    from_above = around_loop(to_below, -1)
    raw = along_cuts(middle, {j: (j + 1) % slices for j in range(slices)})
    f, b, cc, cf = run(
        interior_body,
        "interior",
        [state, coarse_state, cc_shape, cf_shape],
        [u_near, initial_state, *near],
        [
            pltpu.VMEM(third, F32),
            pltpu.VMEM(third, F32),
            pltpu.VMEM((10 * few, cols), F32),
            pltpu.VMEM(state, F32),
            halver_scratch(22, rows, cols),
            pltpu.SemaphoreType.DMA,
        ],
        specs=[VMEM, HBM] + [VMEM] * 4,
    )
    ends, b, cc = run(
        edges_body,
        "edges",
        [ends_shape, coarse_state, cc_shape],
        [f, own, own_coarse, b, cc, from_below, from_above],
        [
            pltpu.VMEM((10, 32, cols), F32),
            pltpu.VMEM((10, 24, half_cols), F32),
            halver_scratch(6, 16, cols),
        ],
    )
    ext = [pltpu.VMEM(ext_state, F32)]
    b_other = along_cuts(b, {})
    source = run(pair_body, "pair", [message, edge, edge], [b, b_other, cc], ext)
    (outer,) = run(outer_body, "outer", [outer_shape], [f, ends])

    previous = along_cuts(outer, {j: j + 1 for j in range(2, slices - 1)} | {slices - 1: 2})
    if leap:
        main, halo = hop_with_edges(*source, to_chip_1)
        halo_source = along_cuts(halo, {})
        (leaped,) = run(
            leap_body,
            "leap",
            [(6, few + 8, half_cols)],
            [main, halo, source[0], halo_source, cc, raw],
            ext * 2,
            specs=[VMEM] * 5 + [ANY],
        )
        after_leap = leaped
        to_chip_3 = around_cuts(leaped, 2, 6, 7, 3)
        to_next = around_cuts(leaped, 2, 4, 6, 7, 5, 3)
        (last,) = run(
            last_body, "last", [ext_state], [to_chip_3, cc], ext, cost=(LAST_COST, LAST_COST)
        )
        close, received_by_chain = arrive_body, [main, halo, last, to_next]
    else:
        at_end = source
        arrived = []
        for chip in range(chips - 1):
            arrived.append(hop_with_edges(*at_end, lambda value, by: hop(value, by, chip)))
            if chip < chips - 2:
                extra = {0: [raw], 1: [previous]}.get(chip, [])
                at_end = run(
                    chain_body,
                    "chain",
                    [message, edge, edge],
                    [*arrived[-1], source[0], cc] + extra,
                    ext,
                    specs=[VMEM] * 4 + [ANY] * len(extra),
                )
            if chip == 0:
                after_leap = at_end[1]
        messages, halos = zip(*arrived)
        close, received_by_chain = lambda *refs: collect_body(chips - 1, *refs), [*messages, *halos]
    (part,) = run(copy_body, "later", [outer_shape], [outer, after_leap], specs=[VMEM, ANY])
    after_hop = lax.ppermute(part, "cuts", [(1, 2)])
    (fine_end,) = run(
        join_body,
        "join",
        [state],
        [f, ends],
        [pltpu.SemaphoreType.DMA((3,))],
        specs=[ANY] * 2,
        out_specs=[ANY],
        cost=(0, 6 * rows * cols * 8),
    )
    (inner,) = run(
        again_body,
        "again",
        [outer_shape],
        [raw, cf],
        [pltpu.VMEM((3,) + middle_shape[1:], F32)] * 2 + [pltpu.VMEM(middle_shape, F32)],
        cost=(0, 6 * rows * cols * 8),
    )
    rem_scratch = [
        halver_scratch(6, rows, cols),
        pltpu.VMEM(state, F32),
        pltpu.SemaphoreType.DMA((3,)),
    ]
    (base,) = run(
        early_body,
        "remainder",
        [state],
        [inner, previous, initial_state],
        [
            halver_scratch(12, few, cols),
            pltpu.SemaphoreType.DMA,
        ],
        specs=[VMEM] * 2 + [HBM],
        cost=(0, 6 * rows * cols * 8),
    )
    total, ended = run(
        close,
        "collect",
        [coarse_state, ext_state],
        [*received_by_chain, base, fine_end],
        specs=[VMEM] * len(received_by_chain) + [ANY, HBM],
    )
    (even_end,) = run(even_body, "even", [coarse_state], [ended, b, cc])
    received = along_cuts(even_end, {})
    (base,) = run(
        late_body,
        "late",
        [state],
        [base, after_hop],
        [
            halver_scratch(12, rows // 4, cols),
            pltpu.VMEM(outer_shape, F32),
            pltpu.SemaphoreType.DMA((2,)),
        ],
        specs=[ANY, VMEM],
        out_specs=[ANY],
        aliases={0: 0},
    )
    (new_start,) = run(
        correct_body,
        "correct",
        [state],
        [base, total, received],
        rem_scratch,
        out_specs=[HBM],
    )
    return new_start[None], fine_end[None]


def solution(mesh):
    state = P("cuts", None, "strip", None)
    field = P("strip", None)
    return jax.shard_map(
        per_device,
        mesh=mesh,
        in_specs=(state, P(None, "strip", None), field, field, field, field),
        out_specs=(state, state),
        check_vma=False,
    )
```

```python
import jax
import jax.numpy as jnp
from jax import lax
from jax.experimental import pallas as pl
from jax.experimental.pallas import tpu as pltpu
from jax.sharding import PartitionSpec as P

FINE_STEP = 0.35
COARSE_STEP = 0.7
FINE_COUPLING = 0.25
COARSE_COUPLING = 0.5
SPEED = COARSE_STEP

FINE_ROWS = (3, 3, 3, 2, 2, 2, 3, 2, 2, 2)
COARSE_ROWS = (2, 2, 2, 1, 1, 1, 6, 5, 5, 5)
FINE_TOTAL = sum(FINE_ROWS)
PACK_ROWS = -(-(FINE_TOTAL + -(-sum(COARSE_ROWS) // 2)) // 8) * 8
CHUNK = 16
HALO_COST = int(2e9)
LAST_COST = int(1e9)
MARGIN = 8

VMEM = pl.BlockSpec(memory_space=pltpu.VMEM)
ANY = pl.BlockSpec(memory_space=pl.ANY)
HBM = pl.BlockSpec(memory_space=pltpu.HBM)
F32 = jnp.float32


def run(body, name, outs, args, scratch=(), specs=None, out_specs=None, aliases=None, cost=None):
    if specs:
        args = [
            pltpu.with_memory_space_constraint(arg, pltpu.HBM) if spec is HBM else arg
            for arg, spec in zip(args, specs)
        ]
    return pl.pallas_call(
        body,
        name=name,
        out_shape=[jax.ShapeDtypeStruct(shape, F32) for shape in outs],
        in_specs=specs or [VMEM] * len(args),
        out_specs=out_specs or [VMEM] * len(outs),
        scratch_shapes=list(scratch),
        input_output_aliases=aliases or {},
        compiler_params=pltpu.CompilerParams(vmem_limit_bytes=20 << 20),
        cost_estimate=cost
        and pl.CostEstimate(flops=cost[0], bytes_accessed=cost[1], transcendentals=0),
    )(*args)


def turn(value, steps, axis):
    return pltpu.roll(value, steps % value.shape[axis], axis)


def scaled_coefficients(kc, kc_low, ka, mass, hoop, step, coupling):
    lane = lax.broadcasted_iota(jnp.int32, ka.shape, 1)
    last = ka.shape[1] - 1
    ka_next = jnp.where(lane == last, 0.0, ka)
    ka_low = jnp.where(lane == 0, 0.0, turn(ka, 1, 1))
    unit = (step * step) / mass
    return (
        kc * unit,
        kc_low * unit,
        ka_next * unit,
        ka_low * unit,
        (kc + kc_low + ka + ka_low) * unit,
        hoop * unit,
        (0.5 * coupling) * unit,
    )


def accelerate(now, above, below, cf):
    up, down, fore, aft, centre, hoop, cross = cf
    out = []
    for i in range(3):
        w = now[i]
        out.append(
            up * above[i]
            + down * below[i]
            + fore * turn(w, -1, 1)
            + aft * turn(w, 1, 1)
            - centre * w
        )
    out[0] = out[0] - cross * (above[2] - below[2])
    out[2] = out[2] + cross * (above[0] - below[0]) - hoop * now[2]
    return out


def accelerate_block(now, cf):
    above = [turn(w, -1, 0) for w in now]
    below = [turn(w, 1, 0) for w in now]
    return accelerate(now, above, below, cf)


def steps_block(w, q, cf, repeats):
    acc = accelerate_block(w, cf)
    for _ in range(repeats):
        half = [a + 0.5 * b for a, b in zip(q, acc)]
        w = [a + b for a, b in zip(w, half)]
        acc = accelerate_block(w, cf)
        q = [a + 0.5 * b for a, b in zip(half, acc)]
    return w, q


def three_parts(value):
    high = value.astype(jnp.bfloat16)
    rest = value - high.astype(F32)
    middle = rest.astype(jnp.bfloat16)
    low = (rest - middle.astype(F32)).astype(jnp.bfloat16)
    return high, middle, low


def exact_dot(value, matrix):
    return sum(
        jnp.dot(part, matrix, preferred_element_type=F32) for part in three_parts(value)[::-1]
    )


def averaging(cols):
    row = lax.broadcasted_iota(jnp.int32, (cols, cols // 2), 0)
    col = lax.broadcasted_iota(jnp.int32, (cols, cols // 2), 1)
    return jnp.where(row // 2 == col, 0.25, 0.0).astype(jnp.bfloat16)


def spreading(cols):
    row = lax.broadcasted_iota(jnp.int32, (cols // 2, cols), 0)
    col = lax.broadcasted_iota(jnp.int32, (cols // 2, cols), 1)
    return jnp.where(col // 2 == row, 1.0, 0.0).astype(jnp.bfloat16)


LANES = 128


class Halver:
    def __init__(self, ref):
        self.ref = ref
        self.used = 0

    def __call__(self, source, lead, start, count):
        pieces = []
        for at in range(0, source.shape[-1], LANES):
            assert self.used < self.ref.shape[0] and 2 * count <= self.ref.shape[1]
            slot = self.ref.at[self.used]
            self.used += 1
            slot[0 : 2 * count, :] = source[
                lead + (pl.ds(start, 2 * count), pl.ds(at, LANES))
            ]
            pieces.append(
                slot[pl.ds(0, count, stride=2), :] + slot[pl.ds(1, count, stride=2), :]
            )
        return jnp.concatenate(pieces, axis=1)


def halver_scratch(fields, rows, cols):
    return pltpu.VMEM((fields * (cols // LANES), rows + 8, LANES), F32)


def is_first():
    return (lax.axis_index("cuts") == 0).astype(F32)


def pack_body(
    u_far, init, kc_far, ka_far, mass_far, hoop_far,
    to_above, to_below, own, own_coarse, u, kc, ka, mass, hoop, middle, early, slots, sems,
):
    rows, cols = kc.shape
    pair_sum = Halver(slots)
    first = is_first()
    copies = [(kc_far, kc), (ka_far, ka), (mass_far, mass), (hoop_far, hoop)]
    copies += [
        (init.at[:, start : start + 16], early.at[:, pl.ds(16 * end, 16)])
        for end, start in enumerate((0, rows - 16))
    ]
    copies.append((u_far, u))
    copies = [
        pltpu.make_async_copy(source, target, sems.at[n])
        for n, (source, target) in enumerate(copies)
    ]
    for copy in copies:
        copy.start()
    matrix = averaging(cols)
    for copy in copies:
        copy.wait()
    for end, start in enumerate((0, rows - 8)):
        at = pl.ds(8 * end, 8)
        for i in range(6):
            own[i, at, :] = u[i, start : start + 8, :]
        for number, ref in enumerate((kc, ka, mass, hoop)):
            own[6 + number, at, :] = ref[start : start + 8, :]
    at = 0
    for number, count in enumerate(FINE_ROWS):
        to_above[at : at + count, :] = own[number, 16 - count : 16, :]
        to_below[at : at + count, :] = own[number, 0:count, :]
        at += count
    sums = []
    for start in (rows - 16, 0):
        for number, ref in enumerate([u] * 6 + [kc, ka, mass, hoop]):
            value = pair_sum(ref, (number,) if number < 6 else (), start, 8)
            if number < 6:
                value = value - first * pair_sum(early, (number,), 16 * (start > 0), 8)
            sums.append(value)
    means = exact_dot(jnp.concatenate(sums, axis=0), matrix)
    half = cols // 2
    at = 0
    for number, count in enumerate(COARSE_ROWS):
        high, low = means[8 * number : 8 * number + 8], means[80 + 8 * number : 88 + 8 * number]
        own_coarse[number, 0:4, :] = low[0:4]
        own_coarse[number, 4:8, :] = high[4:8]
        for k in range(count):
            line = FINE_TOTAL + at // 2
            place = (slice(line, line + 1), pl.ds((at % 2) * half, half))
            to_above[place] = high[8 - count + k : 9 - count + k]
            to_below[place] = low[k : k + 1]
            at += 1
    lead = rows // 4 - MARGIN
    middle[...] = u[:, lead : rows - lead, :]


def propagate(u, coefficients, w1, half, f):
    rows = u.shape[1]
    chunk = CHUNK if rows % CHUNK == 0 else 8
    starts = range(0, rows, chunk)

    def around(ref, start):
        found = []
        for i in range(3):
            now = ref[i, start : start + chunk, :]
            if start + chunk < rows:
                above = ref[i, start + 1 : start + chunk + 1, :]
            else:
                above = turn(now, -1, 0)
            if start > 0:
                below = ref[i, start - 1 : start + chunk - 1, :]
            else:
                below = turn(now, 1, 0)
            found.append((now, above, below))
        return zip(*found)

    for start in starts:
        at = pl.ds(start, chunk)
        now, above, below = around(u, start)
        acc = accelerate(now, above, below, coefficients(start, chunk, True))
        for i in range(3):
            moved = FINE_STEP * u[3 + i, at, :] + 0.5 * acc[i]
            half[i, at, :] = moved
            w1[i, at, :] = now[i] + moved
    for start in starts:
        at = pl.ds(start, chunk)
        now, above, below = around(w1, start)
        acc = accelerate(now, above, below, coefficients(start, chunk, False))
        for i in range(3):
            moved = half[i, at, :] + acc[i]
            half[i, at, :] = moved
            f[i, at, :] = now[i] + moved
    for start in starts:
        at = pl.ds(start, chunk)
        now, above, below = around(f, start)
        acc = accelerate(now, above, below, coefficients(start, chunk, False))
        for i in range(3):
            f[3 + i, at, :] = (half[i, at, :] + 0.5 * acc[i]) * (1.0 / FINE_STEP)


def interior_body(
    u, init, kc, ka, mass, hoop, f, b, cc, cf, w1, half, sums, late, slots, sem
):
    pair_sum = Halver(slots)
    rows, cols = kc.shape
    first = lax.axis_index("cuts") == 0
    prescribed = pltpu.make_async_copy(init, late, sem)

    @pl.when(first)
    def _():
        prescribed.start()

    def coefficients(start, count, fresh):
        at = pl.ds(start, count)
        if not fresh:
            return [cf[number, at, :] for number in range(7)]
        stiff = kc[at, :]
        stiff_low = kc[start - 1 : start + count - 1, :] if start else turn(stiff, 1, 0)
        found = scaled_coefficients(
            stiff, stiff_low, ka[at, :], mass[at, :], hoop[at, :], FINE_STEP, FINE_COUPLING
        )
        for number in range(7):
            cf[number, at, :] = found[number]
        return found

    propagate(u, coefficients, w1, half, f)

    matrix = averaging(cols)
    few = rows // 2
    for i in range(6):
        sums[i * few : (i + 1) * few, :] = pair_sum(u, (i,), 0, few)
    for number, ref in enumerate((kc, ka, mass, hoop)):
        sums[(6 + number) * few : (7 + number) * few, :] = pair_sum(ref, (), 0, few)

    @pl.when(first)
    def _():
        prescribed.wait()
        for i in range(6):
            sums[i * few : (i + 1) * few, :] -= pair_sum(late, (i,), 0, few)

    means = exact_dot(sums[...], matrix)
    parts = [means[i * few : (i + 1) * few] for i in range(10)]
    ckc, cka, cm, ch = parts[6:]
    found = scaled_coefficients(
        ckc, turn(ckc, 1, 0), cka, 4.0 * cm, 4.0 * ch, COARSE_STEP, COARSE_COUPLING
    )
    for number in range(7):
        cc[number, 8 : 8 + few, :] = found[number]
    moved = sum(steps_block(parts[:3], [SPEED * q for q in parts[3:6]], found, 1), [])
    means = exact_dot(
        jnp.concatenate([pair_sum(f, (i,), 0, few) for i in range(6)], axis=0), matrix
    )
    for i in range(6):
        scale = 1.0 if i < 3 else SPEED
        b[i] = scale * means[i * few : (i + 1) * few] - moved[i]


def edges_body(
    f, own, own_coarse, b_in, cc_in, from_below, from_above,
    done, b, cc, fine, coarse, slots,
):
    rows, cols = f.shape[1:]
    few, half_cols = rows // 2, cols // 2
    pair_sum = Halver(slots)
    at = 0
    for number, count in enumerate(FINE_ROWS):
        fine[number, 8 - count : 8, :] = from_below[at : at + count, :]
        fine[number, 8:24, :] = own[number]
        fine[number, 24 : 24 + count, :] = from_above[at : at + count, :]
        at += count
    found = scaled_coefficients(
        fine[6], turn(fine[6], 1, 0), fine[7], fine[8], fine[9], FINE_STEP, FINE_COUPLING
    )
    w, q = steps_block(
        [fine[i] for i in range(3)], [FINE_STEP * fine[3 + i] for i in range(3)], found, 2
    )
    for i in range(6):
        done[i, 0:8, :] = f[i, 0:8, :]
        done[i, 8:16, :] = f[i, rows - 8 : rows, :]
    for i in range(3):
        done[i, 0:4, :] = w[i][8:12]
        done[i, 12:16, :] = w[i][20:24]
        done[3 + i, 0:4, :] = q[i][8:12] * (1.0 / FINE_STEP)
        done[3 + i, 12:16, :] = q[i][20:24] * (1.0 / FINE_STEP)

    sums = [pair_sum(done, (i,), 0, 8) for i in range(6)]
    means = exact_dot(jnp.concatenate(sums, axis=0), averaging(cols))
    coarse[...] = jnp.ones_like(coarse)
    at = 0
    for number, count in enumerate(COARSE_ROWS):
        coarse[number, 8:16, :] = own_coarse[number]
        for k in range(count):
            line = FINE_TOTAL + at // 2
            place = (slice(line, line + 1), pl.ds((at % 2) * half_cols, half_cols))
            coarse[number, 8 - count + k : 9 - count + k, :] = from_below[place]
            coarse[number, 16 + k : 17 + k, :] = from_above[place]
            at += 1
    found = scaled_coefficients(
        coarse[6], turn(coarse[6], 1, 0), coarse[7], 4.0 * coarse[8], 4.0 * coarse[9],
        COARSE_STEP, COARSE_COUPLING,
    )
    for number in range(7):
        cc[number, 0:12, :] = found[number][0:12]
        cc[number, 12 : few + 8, :] = cc_in[number, 12 : few + 8, :]
        cc[number, few + 8 : few + 16, :] = found[number][16:24]
    w, q = steps_block(
        [coarse[i] for i in range(3)], [SPEED * coarse[3 + i] for i in range(3)], found, 1
    )
    moved = w + q
    b[...] = b_in[...]
    for i in range(6):
        scale = 1.0 if i < 3 else SPEED
        ends = scale * means[8 * i : 8 * i + 8, :]
        b[i, 0:2, :] = ends[0:2] - moved[i][8:10]
        b[i, few - 2 : few, :] = ends[6:8] - moved[i][14:16]


def advance(ext, cc, repeats):
    return sum(
        steps_block(
            [ext[i] for i in range(3)],
            [ext[3 + i] for i in range(3)],
            [cc[number] for number in range(7)],
            repeats,
        ),
        [],
    )


def write_edges(message, to_above, to_below):
    few = (message.shape[0] - 24) // 6
    lines = to_above.shape[0] // 6
    for i in range(6):
        own, beyond, at = i * few, 6 * few + 4 * i, lines * i
        extra = 1 if i < 3 else 2
        rows = lines - extra
        to_above[at : at + rows, :] = message[own + few - rows : own + few, :]
        to_above[at + rows : at + lines, :] = message[beyond + extra : beyond + 2 * extra, :]
        to_below[at : at + extra, :] = message[beyond : beyond + extra, :]
        to_below[at + extra : at + lines, :] = message[own : own + rows, :]


def read_message(ext, message, below, above):
    few = ext.shape[1] - 16
    top = 8 + few
    lines = below.shape[0] // 6
    for i in range(6):
        own, beyond, at = i * few, 6 * few + 4 * i, lines * i
        extra = 1 if i < 3 else 2
        rows = lines - extra
        ext[i, 8:top, :] = message[own : own + few, :]
        ext[i, 8 - rows : 8, :] = below[at : at + rows, :]
        ext[i, top : top + rows, :] = above[at + extra : at + lines, :]
        ext[i, 8 - extra : 8, :] += message[beyond : beyond + extra, :]
        ext[i, top : top + extra, :] += message[beyond + extra : beyond + 2 * extra, :]
        ext[i, 8 : 8 + extra, :] += below[at + rows : at + lines, :]
        ext[i, top - extra : top, :] += above[at : at + extra, :]


def halves(ref):
    return ref.at[0], ref.at[1]


def pair_body(b, b_other, cc, message, to_above, to_below, ext, late):
    few = ext.shape[1] - 16
    top = 8 + few
    odd = lax.axis_index("cuts") % 2
    ext[:, 0:8, :] = jnp.zeros_like(ext[:, 0:8, :])
    ext[:, top : top + 8, :] = jnp.zeros_like(ext[:, 0:8, :])

    @pl.when(odd == 0)
    def _():
        ext[:, 8:top, :] = b[...]
        late[...] = b_other[...]

    @pl.when(odd == 1)
    def _():
        ext[:, 8:top, :] = b_other[...]
        late[...] = b[...]

    for i, value in enumerate(advance(ext, cc, 1)):
        own, beyond = i * few, 6 * few + 4 * i
        message[own : own + few, :] = value[8:top] + late[i]
        if i < 3:
            message[beyond : beyond + 1, :] = value[7:8]
            message[beyond + 1 : beyond + 2, :] = value[top : top + 1]
            message[beyond + 2 : beyond + 4, :] = jnp.zeros_like(value[0:2])
        else:
            message[beyond : beyond + 2, :] = value[6:8]
            message[beyond + 2 : beyond + 4, :] = value[top : top + 2]
    write_edges(message, to_above, to_below)


def halo_body(below, above, out):
    out[0] = below[...]
    out[1] = above[...]


def chain_body(message, halo, source, cc, *refs):
    out, to_above, to_below, ext = refs[-4:]
    below, above = halves(halo)
    few = ext.shape[1] - 16
    ext[...] = jnp.zeros_like(ext)
    read_message(ext, message, below, above)
    for i, value in enumerate(advance(ext, cc, 2)):
        own = i * few
        out[own : own + few, :] = value[8 : 8 + few] + source[own : own + few, :]
    out[6 * few :, :] = source[6 * few :, :]
    write_edges(out, to_above, to_below)


def collect_body(rounds, *refs):
    messages, halos = refs[:rounds], refs[rounds : 2 * rounds]
    total, ext = refs[2 * rounds + 2 :]
    chip = lax.axis_index("cuts") // 2
    ext[...] = jnp.zeros_like(ext)
    for number in range(rounds):

        @pl.when(chip == number + 1)
        def _():
            read_message(ext, messages[number], *halves(halos[number]))

    for i in range(6):
        total[i] = ext[i, 8 : ext.shape[1] - 8, :]


def leap_body(message, halo, source, halo_source, cc, *refs):
    out, ext, add = refs[-3:]
    chip = lax.axis_index("cuts") // 2
    rows = ext.shape[1]

    @pl.when((chip == 1) | (chip == 2))
    def _():
        add[...] = jnp.zeros_like(add)
        read_message(add, source, *halves(halo_source))

    @pl.when(chip == 1)
    def _():
        ext[...] = jnp.zeros_like(ext)
        read_message(ext, message, *halves(halo))
        for i, value in enumerate(advance(ext, cc, 2)):
            out[i] = (value + add[i])[4 : rows - 4]

    @pl.when(chip == 2)
    def _():
        out[...] = add[:, 4 : rows - 4, :]


def last_body(leaped, cc, out, ext):
    rows = ext.shape[1]

    @pl.when(lax.axis_index("cuts") // 2 == 3)
    def _():
        ext[...] = jnp.zeros_like(ext)
        ext[:, 4 : rows - 4, :] = leaped[...]
        for i, value in enumerate(advance(ext, cc, 2)):
            out[i] = value


def arrive_body(message, halo, last, step, *refs):
    total, ext = refs[-2:]
    chip = lax.axis_index("cuts") // 2
    rows = ext.shape[1]
    ext[...] = jnp.zeros_like(ext)

    @pl.when(chip == 1)
    def _():
        read_message(ext, message, *halves(halo))

    @pl.when(chip >= 2)
    def _():
        ext[:, 4 : rows - 4, :] = step[...]

    @pl.when(chip == 3)
    def _():
        ext[...] += last[...]

    for i in range(6):
        total[i] = ext[i, 8 : rows - 8, :]


def even_body(ext, b_even, cc, even_end):
    few = ext.shape[1] - 16
    for i, value in enumerate(advance(ext, cc, 1)):
        even_end[i] = value[8 : 8 + few] + b_even[i]


def outer_body(f, ends, out):
    rows = f.shape[1]
    quarter = rows // 4
    out[:, 0:8, :] = ends[:, 0:8, :]
    out[:, 8:quarter, :] = f[:, 8:quarter, :]
    out[:, quarter : 2 * quarter - 8, :] = f[:, rows - quarter : rows - 8, :]
    out[:, 2 * quarter - 8 : 2 * quarter, :] = ends[:, 8:16, :]


def copy_body(value, after, out):
    out[...] = value[...]


def again_body(u, cf, out, w1, half, made):
    lead = cf.shape[1] // 4 - MARGIN

    def coefficients(start, count, fresh):
        return [cf[number, lead + start : lead + start + count, :] for number in range(7)]

    propagate(u, coefficients, w1, half, made)
    out[...] = made[:, MARGIN : made.shape[1] - MARGIN, :]


def join_body(f, ends, out, sems):
    rows = f.shape[1]
    copies = [
        pltpu.make_async_copy(f.at[:, 8 : rows - 8], out.at[:, 8 : rows - 8], sems.at[0]),
        pltpu.make_async_copy(ends.at[:, 0:8], out.at[:, 0:8], sems.at[1]),
        pltpu.make_async_copy(ends.at[:, 8:16], out.at[:, rows - 8 : rows], sems.at[2]),
    ]
    for copy in copies:
        copy.start()
    for copy in copies:
        copy.wait()


def spread_add(values, bases, outs, slots):
    cols = 2 * values.shape[1]
    wide = exact_dot(values, spreading(cols))
    few = wide.shape[0] // len(outs)
    for i, (base, out) in enumerate(zip(bases, outs)):
        for tile in range(cols // LANES):
            part = wide[i * few : (i + 1) * few, tile * LANES : (tile + 1) * LANES]
            assert i * (cols // LANES) + tile < slots.shape[0] and 2 * few <= slots.shape[1]
            slot = slots.at[i * (cols // LANES) + tile]
            slot[pl.ds(0, few, stride=2), :] = part
            slot[pl.ds(1, few, stride=2), :] = part
            at = (slice(None), pl.ds(tile * LANES, LANES))
            out[at] = base[at] + slot[0 : 2 * few, :]


def remainder(parts, outs, slots):
    pair_sum = Halver(slots)
    cols = parts[0].shape[1]
    few = parts[0].shape[0] // 2
    sums = [pair_sum(part, (), 0, few) for part in parts]
    means = exact_dot(jnp.concatenate(sums, axis=0), averaging(cols))
    spread_add(-means, parts, outs, slots)


def outer_parts(ref, quarter):
    rows = ref.shape[1]
    ends = (pl.ds(0, quarter), pl.ds(rows - quarter, quarter))
    return [ref.at[i, end] for i in range(6) for end in ends]


def early_body(inner, outer, init, out, slots, sem):
    place = lax.axis_index("cuts")
    rows = out.shape[1]
    quarter = rows // 4
    middle = pl.ds(quarter, rows // 2)

    @pl.when(place != 0)
    def _():
        remainder(
            [inner.at[i] for i in range(6)], [out.at[i, middle] for i in range(6)], slots
        )
        remainder(outer_parts(outer, quarter), outer_parts(out, quarter), slots)

    @pl.when(place == 0)
    def _():
        copy = pltpu.make_async_copy(init, out, sem)
        copy.start()
        copy.wait()


def late_body(base_in, after_hop, base, slots, made, sems):
    rows = base.shape[1]
    quarter = rows // 4

    @pl.when(lax.axis_index("cuts") == 2)
    def _():
        remainder(outer_parts(after_hop, quarter), outer_parts(made, quarter), slots)
        copies = [
            pltpu.make_async_copy(
                made.at[:, pl.ds(n * quarter, quarter)],
                base.at[:, pl.ds(start, quarter)],
                sems.at[n],
            )
            for n, start in enumerate((0, rows - quarter))
        ]
        for copy in copies:
            copy.start()
        for copy in copies:
            copy.wait()


def correct_body(base, own, received, out, slots, made, sems):
    odd = lax.axis_index("cuts") % 2
    cols = base.shape[2]
    copies = []
    for lead in range(0, 6, 2):
        part = range(lead, lead + 2)
        values = []
        for i in part:
            value = jnp.where(odd == 1, received[i], own[i])
            values.append(value if i < 3 else value * (1.0 / SPEED))
        spread_add(
            jnp.concatenate(values, axis=0),
            [base.at[i] for i in part],
            [made.at[i] for i in part],
            slots.at[pl.ds(cols // LANES * lead, cols // LANES * 2)],
        )
        copies.append(
            pltpu.make_async_copy(
                made.at[pl.ds(lead, 2)], out.at[pl.ds(lead, 2)], sems.at[lead // 2]
            )
        )
        copies[-1].start()
    for copy in copies:
        copy.wait()


def per_device(start_state, initial_state, circ_stiff, axial_stiff, lumped_mass, hoop_stiff):
    u = start_state[0]
    strips, slices = lax.axis_size("strip"), lax.axis_size("cuts")
    chips = slices // 2
    _, rows, cols = u.shape
    few, half_cols = rows // 2, cols // 2
    state, coarse_state = (6, rows, cols), (6, few, half_cols)
    ext_state = (6, few + 16, half_cols)
    leap = chips == 4
    reach = 7 if leap else 3
    edge = (6 * (reach + 1), half_cols)
    fields = (circ_stiff, axial_stiff, lumped_mass, hoop_stiff)

    def around_loop(value, by):
        pairs = [(s, (s + by) % strips) for s in range(strips)]
        return lax.ppermute(value, "strip", pairs)


    def along_cuts(value, moves):
        rest = [j for j in range(slices) if j not in moves]
        pairs = list(moves.items()) + [(j, j ^ 1) for j in rest]
        assert sorted(target for _, target in pairs) == list(range(slices))
        return lax.ppermute(value, "cuts", pairs)

    def hop(value, by, chip):
        third = None
        if chip > 0:
            third = chip + 2 if chip + 2 < chips else chip - 1
        used = {chip, chip + 1, third}
        pairs = []
        for s in range(strips):
            here, there = s * slices, (s + by) % strips * slices
            a, b = here + 2 * chip, there + 2 * chip + 2
            path = [a, b, b + 1]
            if third is not None:
                path += [there + 2 * third, there + 2 * third + 1]
            path.append(a + 1)
            pairs += list(zip(path, path[1:] + path[:1]))
            pairs += [(here + j, here + (j ^ 1)) for j in range(slices) if j // 2 not in used]
        assert sorted(target for _, target in pairs) == list(range(strips * slices))
        return lax.ppermute(value, ("strip", "cuts"), pairs)

    def hop_with_edges(main, to_above, to_below, move):
        edges = [move(to_above, 1), move(to_below, -1)]
        (halo,) = run(
            halo_body, "halo", [(2,) + edge], edges, cost=(HALO_COST, HALO_COST)
        )
        return move(main, 0), halo

    def to_chip_1(value, by):
        pairs = []
        for s in range(strips):
            here, there, beyond = (slices * ((s + k * by) % strips) for k in range(3))
            path = [here, there + 2, beyond + 3, here + 1]
            if by:
                path = [here + 1, there + 2, beyond + 3, here]
            pairs += list(zip(path, path[1:] + path[:1]))
            for j in range(4, slices, 2):
                pairs += [(here + j, there + j + 1), (here + j + 1, here + j)]
        assert sorted(target for _, target in pairs) == list(range(strips * slices))
        return lax.ppermute(value, ("strip", "cuts"), pairs)

    def around_cuts(value, *path):
        return along_cuts(value, dict(zip(path, path[1:] + path[:1])))

    pack = (PACK_ROWS, cols)
    third = (3, rows, cols)
    ends_shape = (6, 16, cols)
    message = (6 * few + 24, half_cols)
    cc_shape, cf_shape = (7, few + 16, half_cols), (7, rows, cols)
    middle_shape = (6, few + 2 * MARGIN, cols)
    outer_shape = (6, few, cols)
    to_above, to_below, own, own_coarse, u_near, *near, middle = run(
        pack_body,
        "pack",
        [pack, pack, (10, 16, cols), (10, 8, half_cols), state]
        + [(rows, cols)] * 4
        + [middle_shape],
        [u, initial_state, *fields],
        [
            pltpu.VMEM((6, 32, cols), F32),
            halver_scratch(32, 16, cols),
            pltpu.SemaphoreType.DMA((7,)),
        ],
        specs=[HBM] * 6,
    )
    from_below = around_loop(to_above, 1)
    from_above = around_loop(to_below, -1)
    raw = along_cuts(middle, {j: (j + 1) % slices for j in range(slices)})
    f, b, cc, cf = run(
        interior_body,
        "interior",
        [state, coarse_state, cc_shape, cf_shape],
        [u_near, initial_state, *near],
        [
            pltpu.VMEM(third, F32),
            pltpu.VMEM(third, F32),
            pltpu.VMEM((10 * few, cols), F32),
            pltpu.VMEM(state, F32),
            halver_scratch(22, rows, cols),
            pltpu.SemaphoreType.DMA,
        ],
        specs=[VMEM, HBM] + [VMEM] * 4,
    )
    ends, b, cc = run(
        edges_body,
        "edges",
        [ends_shape, coarse_state, cc_shape],
        [f, own, own_coarse, b, cc, from_below, from_above],
        [
            pltpu.VMEM((10, 32, cols), F32),
            pltpu.VMEM((10, 24, half_cols), F32),
            halver_scratch(6, 16, cols),
        ],
    )
    ext = [pltpu.VMEM(ext_state, F32)]
    b_other = along_cuts(b, {})
    source = run(
        pair_body,
        "pair",
        [message, edge, edge],
        [b, b_other, cc],
        ext + [pltpu.VMEM(coarse_state, F32)],
    )
    (outer,) = run(outer_body, "outer", [outer_shape], [f, ends])

    previous = along_cuts(outer, {j: j + 1 for j in range(2, slices - 1)} | {slices - 1: 2})
    if leap:
        main, halo = hop_with_edges(*source, to_chip_1)
        halo_source = along_cuts(halo, {})
        (leaped,) = run(
            leap_body,
            "leap",
            [(6, few + 8, half_cols)],
            [main, halo, source[0], halo_source, cc, raw],
            ext * 2,
            specs=[VMEM] * 5 + [ANY],
        )
        after_leap = leaped
        to_chip_3 = around_cuts(leaped, 2, 6, 7, 3)
        to_next = around_cuts(leaped, 2, 4, 6, 7, 5, 3)
        (last,) = run(
            last_body, "last", [ext_state], [to_chip_3, cc], ext, cost=(LAST_COST, LAST_COST)
        )
        close, received_by_chain = arrive_body, [main, halo, last, to_next]
    else:
        at_end = source
        arrived = []
        for chip in range(chips - 1):
            arrived.append(hop_with_edges(*at_end, lambda value, by: hop(value, by, chip)))
            if chip < chips - 2:
                extra = {0: [raw], 1: [previous]}.get(chip, [])
                at_end = run(
                    chain_body,
                    "chain",
                    [message, edge, edge],
                    [*arrived[-1], source[0], cc] + extra,
                    ext,
                    specs=[VMEM] * 4 + [ANY] * len(extra),
                )
            if chip == 0:
                after_leap = at_end[1]
        messages, halos = zip(*arrived)
        close, received_by_chain = lambda *refs: collect_body(chips - 1, *refs), [*messages, *halos]
    (part,) = run(copy_body, "later", [outer_shape], [outer, after_leap], specs=[VMEM, ANY])
    after_hop = lax.ppermute(part, "cuts", [(1, 2)])
    (fine_end,) = run(
        join_body,
        "join",
        [state],
        [f, ends],
        [pltpu.SemaphoreType.DMA((3,))],
        specs=[ANY] * 2,
        out_specs=[ANY],
        cost=(0, 6 * rows * cols * 8),
    )
    (inner,) = run(
        again_body,
        "again",
        [outer_shape],
        [raw, cf],
        [pltpu.VMEM((3,) + middle_shape[1:], F32)] * 2 + [pltpu.VMEM(middle_shape, F32)],
        cost=(0, 6 * rows * cols * 8),
    )
    rem_scratch = [
        halver_scratch(6, rows, cols),
        pltpu.VMEM(state, F32),
        pltpu.SemaphoreType.DMA((3,)),
    ]
    (base,) = run(
        early_body,
        "remainder",
        [state],
        [inner, previous, initial_state],
        [
            halver_scratch(12, few, cols),
            pltpu.SemaphoreType.DMA,
        ],
        specs=[VMEM] * 2 + [HBM],
        cost=(0, 6 * rows * cols * 8),
    )
    total, ended = run(
        close,
        "collect",
        [coarse_state, ext_state],
        [*received_by_chain, base, fine_end],
        specs=[VMEM] * len(received_by_chain) + [ANY, HBM],
    )
    (even_end,) = run(even_body, "even", [coarse_state], [ended, b, cc])
    received = along_cuts(even_end, {})
    (base,) = run(
        late_body,
        "late",
        [state],
        [base, after_hop],
        [
            halver_scratch(12, rows // 4, cols),
            pltpu.VMEM(outer_shape, F32),
            pltpu.SemaphoreType.DMA((2,)),
        ],
        specs=[ANY, VMEM],
        out_specs=[ANY],
        aliases={0: 0},
    )
    (new_start,) = run(
        correct_body,
        "correct",
        [state],
        [base, total, received],
        rem_scratch,
        out_specs=[HBM],
    )
    return new_start[None], fine_end[None]


def solution(mesh):
    state = P("cuts", None, "strip", None)
    field = P("strip", None)
    return jax.shard_map(
        per_device,
        mesh=mesh,
        in_specs=(state, P(None, "strip", None), field, field, field, field),
        out_specs=(state, state),
        check_vma=False,
    )
```

```python
import jax
import jax.numpy as jnp
from jax import lax
from jax.experimental import pallas as pl
from jax.experimental.pallas import tpu as pltpu
from jax.sharding import PartitionSpec as P

FINE_STEP = 0.35
COARSE_STEP = 0.7
FINE_COUPLING = 0.25
COARSE_COUPLING = 0.5
SPEED = COARSE_STEP

FINE_ROWS = (3, 3, 3, 2, 2, 2, 3, 2, 2, 2)
COARSE_ROWS = (2, 2, 2, 1, 1, 1, 6, 5, 5, 5)
FINE_TOTAL = sum(FINE_ROWS)
PACK_ROWS = -(-(FINE_TOTAL + -(-sum(COARSE_ROWS) // 2)) // 8) * 8
CHUNK = 16
HALO_COST = int(2e9)
LAST_COST = int(1e9)
MARGIN = 8

VMEM = pl.BlockSpec(memory_space=pltpu.VMEM)
ANY = pl.BlockSpec(memory_space=pl.ANY)
HBM = pl.BlockSpec(memory_space=pltpu.HBM)
F32 = jnp.float32


def run(body, name, outs, args, scratch=(), specs=None, out_specs=None, aliases=None, cost=None):
    if specs:
        args = [
            pltpu.with_memory_space_constraint(arg, pltpu.HBM) if spec is HBM else arg
            for arg, spec in zip(args, specs)
        ]
    return pl.pallas_call(
        body,
        name=name,
        out_shape=[jax.ShapeDtypeStruct(shape, F32) for shape in outs],
        in_specs=specs or [VMEM] * len(args),
        out_specs=out_specs or [VMEM] * len(outs),
        scratch_shapes=list(scratch),
        input_output_aliases=aliases or {},
        compiler_params=pltpu.CompilerParams(vmem_limit_bytes=20 << 20),
        cost_estimate=cost
        and pl.CostEstimate(flops=cost[0], bytes_accessed=cost[1], transcendentals=0),
    )(*args)


def turn(value, steps, axis):
    return pltpu.roll(value, steps % value.shape[axis], axis)


def scaled_coefficients(kc, kc_low, ka, mass, hoop, step, coupling):
    lane = lax.broadcasted_iota(jnp.int32, ka.shape, 1)
    last = ka.shape[1] - 1
    ka_next = jnp.where(lane == last, 0.0, ka)
    ka_low = jnp.where(lane == 0, 0.0, turn(ka, 1, 1))
    unit = (step * step) / mass
    return (
        kc * unit,
        kc_low * unit,
        ka_next * unit,
        ka_low * unit,
        (kc + kc_low + ka + ka_low) * unit,
        hoop * unit,
        (0.5 * coupling) * unit,
    )


def accelerate(now, above, below, cf):
    up, down, fore, aft, centre, hoop, cross = cf
    out = []
    for i in range(3):
        w = now[i]
        out.append(
            up * above[i]
            + down * below[i]
            + fore * turn(w, -1, 1)
            + aft * turn(w, 1, 1)
            - centre * w
        )
    out[0] = out[0] - cross * (above[2] - below[2])
    out[2] = out[2] + cross * (above[0] - below[0]) - hoop * now[2]
    return out


def accelerate_block(now, cf):
    above = [turn(w, -1, 0) for w in now]
    below = [turn(w, 1, 0) for w in now]
    return accelerate(now, above, below, cf)


def steps_block(w, q, cf, repeats):
    acc = accelerate_block(w, cf)
    for _ in range(repeats):
        half = [a + 0.5 * b for a, b in zip(q, acc)]
        w = [a + b for a, b in zip(w, half)]
        acc = accelerate_block(w, cf)
        q = [a + 0.5 * b for a, b in zip(half, acc)]
    return w, q


def exact_dot(value, matrix):
    split = []
    for _ in range(3):
        split.append(value.astype(jnp.bfloat16))
        value = value - split[-1].astype(F32)
    return sum(jnp.dot(part, matrix, preferred_element_type=F32) for part in split[::-1])


def averaging(cols):
    row = lax.broadcasted_iota(jnp.int32, (cols, cols // 2), 0)
    col = lax.broadcasted_iota(jnp.int32, (cols, cols // 2), 1)
    return jnp.where(row // 2 == col, 0.25, 0.0).astype(jnp.bfloat16)


def spreading(cols):
    row = lax.broadcasted_iota(jnp.int32, (cols // 2, cols), 0)
    col = lax.broadcasted_iota(jnp.int32, (cols // 2, cols), 1)
    return jnp.where(col // 2 == row, 1.0, 0.0).astype(jnp.bfloat16)


LANES = 128


class Halver:
    def __init__(self, ref):
        self.ref = ref
        self.used = 0

    def __call__(self, source, lead, start, count):
        pieces = []
        for at in range(0, source.shape[-1], LANES):
            assert self.used < self.ref.shape[0] and 2 * count <= self.ref.shape[1]
            slot = self.ref.at[self.used]
            self.used += 1
            slot[0 : 2 * count, :] = source[
                lead + (pl.ds(start, 2 * count), pl.ds(at, LANES))
            ]
            pieces.append(
                slot[pl.ds(0, count, stride=2), :] + slot[pl.ds(1, count, stride=2), :]
            )
        return jnp.concatenate(pieces, axis=1)


def halver_scratch(fields, rows, cols):
    return pltpu.VMEM((fields * (cols // LANES), rows + 8, LANES), F32)


def is_first():
    return (lax.axis_index("cuts") == 0).astype(F32)


def pack_body(
    u_far, init, kc_far, ka_far, mass_far, hoop_far,
    to_above, to_below, own, own_coarse, u, kc, ka, mass, hoop, middle, early, slots, sems,
):
    rows, cols = kc.shape
    pair_sum = Halver(slots)
    first = is_first()
    copies = [(kc_far, kc), (ka_far, ka), (mass_far, mass), (hoop_far, hoop)]
    copies += [
        (init.at[:, start : start + 8], early.at[:, pl.ds(8 * end, 8)])
        for end, start in enumerate((0, rows - 8))
    ]
    copies.append((u_far, u))
    copies = [
        pltpu.make_async_copy(source, target, sems.at[n])
        for n, (source, target) in enumerate(copies)
    ]
    for copy in copies:
        copy.start()
    matrix = averaging(cols)
    half = cols // 2
    fine_at = [sum(FINE_ROWS[:number]) for number in range(10)]
    coarse_at = [sum(COARSE_ROWS[:number]) for number in range(10)]

    def pack(numbers, sources, sums, ends):
        for number, (ref, place) in zip(numbers, sources):
            own[number, 0:8, :] = ref[place + (slice(0, 8), slice(None))]
            own[number, 8:16, :] = ref[place + (slice(rows - 8, rows), slice(None))]
            at, count = fine_at[number], FINE_ROWS[number]
            to_above[at : at + count, :] = own[number, 16 - count : 16, :]
            to_below[at : at + count, :] = own[number, 0:count, :]
        means = exact_dot(jnp.concatenate(sums, axis=0), matrix)
        for n, number in enumerate(numbers):
            low = means[2 * n * ends : (2 * n + 1) * ends]
            high = means[(2 * n + 1) * ends : (2 * n + 2) * ends]
            own_coarse[number, 0:4, :] = low[0:4]
            own_coarse[number, 4:8, :] = high[ends - 4 : ends]
            count = COARSE_ROWS[number]
            for k in range(count):
                at = coarse_at[number] + k
                line = FINE_TOTAL + at // 2
                where = (slice(line, line + 1), pl.ds((at % 2) * half, half))
                to_above[where] = high[ends - count + k : ends - count + k + 1]
                to_below[where] = low[k : k + 1]

    for copy in copies[:4]:
        copy.wait()
    sources = [(ref, ()) for ref in (kc, ka, mass, hoop)]
    sums = [pair_sum(ref, (), start, 8) for ref, _ in sources for start in (0, rows - 16)]
    pack(range(6, 10), sources, sums, 8)
    for copy in copies[4:]:
        copy.wait()
    sums = []
    for i in range(6):
        for end, start in enumerate((0, rows - 8)):
            sums.append(pair_sum(u, (i,), start, 4) - first * pair_sum(early, (i,), 8 * end, 4))
    pack(range(6), [(u, (i,)) for i in range(6)], sums, 4)
    lead = rows // 4 - MARGIN
    middle[...] = u[:, lead : rows - lead, :]


def propagate(u, coefficients, w1, half, f):
    rows = u.shape[1]
    chunk = CHUNK if rows % CHUNK == 0 else 8
    starts = range(0, rows, chunk)

    def around(ref, start):
        found = []
        for i in range(3):
            now = ref[i, start : start + chunk, :]
            if start + chunk < rows:
                above = ref[i, start + 1 : start + chunk + 1, :]
            else:
                above = turn(now, -1, 0)
            if start > 0:
                below = ref[i, start - 1 : start + chunk - 1, :]
            else:
                below = turn(now, 1, 0)
            found.append((now, above, below))
        return zip(*found)

    for start in starts:
        at = pl.ds(start, chunk)
        now, above, below = around(u, start)
        acc = accelerate(now, above, below, coefficients(start, chunk, True))
        for i in range(3):
            moved = FINE_STEP * u[3 + i, at, :] + 0.5 * acc[i]
            half[i, at, :] = moved
            w1[i, at, :] = now[i] + moved
    for start in starts:
        at = pl.ds(start, chunk)
        now, above, below = around(w1, start)
        acc = accelerate(now, above, below, coefficients(start, chunk, False))
        for i in range(3):
            moved = half[i, at, :] + acc[i]
            half[i, at, :] = moved
            f[i, at, :] = now[i] + moved
    for start in starts:
        at = pl.ds(start, chunk)
        now, above, below = around(f, start)
        acc = accelerate(now, above, below, coefficients(start, chunk, False))
        for i in range(3):
            f[3 + i, at, :] = (half[i, at, :] + 0.5 * acc[i]) * (1.0 / FINE_STEP)


def interior_body(
    u, init, kc, ka, mass, hoop, f, b, cc, cf, w1, half, sums, late, slots, sem
):
    pair_sum = Halver(slots)
    rows, cols = kc.shape
    first = lax.axis_index("cuts") == 0
    prescribed = pltpu.make_async_copy(init, late, sem)

    @pl.when(first)
    def _():
        prescribed.start()

    def coefficients(start, count, fresh):
        at = pl.ds(start, count)
        if not fresh:
            return [cf[number, at, :] for number in range(7)]
        stiff = kc[at, :]
        stiff_low = kc[start - 1 : start + count - 1, :] if start else turn(stiff, 1, 0)
        found = scaled_coefficients(
            stiff, stiff_low, ka[at, :], mass[at, :], hoop[at, :], FINE_STEP, FINE_COUPLING
        )
        for number in range(7):
            cf[number, at, :] = found[number]
        return found

    propagate(u, coefficients, w1, half, f)

    matrix = averaging(cols)
    few = rows // 2
    for i in range(6):
        sums[i * few : (i + 1) * few, :] = pair_sum(u, (i,), 0, few)
    for number, ref in enumerate((kc, ka, mass, hoop)):
        sums[(6 + number) * few : (7 + number) * few, :] = pair_sum(ref, (), 0, few)

    @pl.when(first)
    def _():
        prescribed.wait()
        for i in range(6):
            sums[i * few : (i + 1) * few, :] -= pair_sum(late, (i,), 0, few)

    means = exact_dot(sums[...], matrix)
    parts = [means[i * few : (i + 1) * few] for i in range(10)]
    ckc, cka, cm, ch = parts[6:]
    found = scaled_coefficients(
        ckc, turn(ckc, 1, 0), cka, 4.0 * cm, 4.0 * ch, COARSE_STEP, COARSE_COUPLING
    )
    for number in range(7):
        cc[number, 8 : 8 + few, :] = found[number]
    moved = sum(steps_block(parts[:3], [SPEED * q for q in parts[3:6]], found, 1), [])
    means = exact_dot(
        jnp.concatenate([pair_sum(f, (i,), 0, few) for i in range(6)], axis=0), matrix
    )
    for i in range(6):
        scale = 1.0 if i < 3 else SPEED
        b[i] = scale * means[i * few : (i + 1) * few] - moved[i]


def edges_body(
    f, own, own_coarse, b_in, cc_in, from_below, from_above,
    done, b, cc, fine, coarse, slots,
):
    rows, cols = f.shape[1:]
    few, half_cols = rows // 2, cols // 2
    pair_sum = Halver(slots)
    at = 0
    for number, count in enumerate(FINE_ROWS):
        fine[number, 8 - count : 8, :] = from_below[at : at + count, :]
        fine[number, 8:24, :] = own[number]
        fine[number, 24 : 24 + count, :] = from_above[at : at + count, :]
        at += count
    found = scaled_coefficients(
        fine[6], turn(fine[6], 1, 0), fine[7], fine[8], fine[9], FINE_STEP, FINE_COUPLING
    )
    w, q = steps_block(
        [fine[i] for i in range(3)], [FINE_STEP * fine[3 + i] for i in range(3)], found, 2
    )
    for i in range(6):
        done[i, 0:8, :] = f[i, 0:8, :]
        done[i, 8:16, :] = f[i, rows - 8 : rows, :]
    for i in range(3):
        done[i, 0:4, :] = w[i][8:12]
        done[i, 12:16, :] = w[i][20:24]
        done[3 + i, 0:4, :] = q[i][8:12] * (1.0 / FINE_STEP)
        done[3 + i, 12:16, :] = q[i][20:24] * (1.0 / FINE_STEP)

    sums = [pair_sum(done, (i,), 0, 8) for i in range(6)]
    means = exact_dot(jnp.concatenate(sums, axis=0), averaging(cols))
    coarse[...] = jnp.ones_like(coarse)
    at = 0
    for number, count in enumerate(COARSE_ROWS):
        coarse[number, 8:16, :] = own_coarse[number]
        for k in range(count):
            line = FINE_TOTAL + at // 2
            place = (slice(line, line + 1), pl.ds((at % 2) * half_cols, half_cols))
            coarse[number, 8 - count + k : 9 - count + k, :] = from_below[place]
            coarse[number, 16 + k : 17 + k, :] = from_above[place]
            at += 1
    found = scaled_coefficients(
        coarse[6], turn(coarse[6], 1, 0), coarse[7], 4.0 * coarse[8], 4.0 * coarse[9],
        COARSE_STEP, COARSE_COUPLING,
    )
    for number in range(7):
        cc[number, 0:12, :] = found[number][0:12]
        cc[number, 12 : few + 8, :] = cc_in[number, 12 : few + 8, :]
        cc[number, few + 8 : few + 16, :] = found[number][16:24]
    w, q = steps_block(
        [coarse[i] for i in range(3)], [SPEED * coarse[3 + i] for i in range(3)], found, 1
    )
    moved = w + q
    b[...] = b_in[...]
    for i in range(6):
        scale = 1.0 if i < 3 else SPEED
        ends = scale * means[8 * i : 8 * i + 8, :]
        b[i, 0:2, :] = ends[0:2] - moved[i][8:10]
        b[i, few - 2 : few, :] = ends[6:8] - moved[i][14:16]


def advance(ext, cc, repeats):
    return sum(
        steps_block(
            [ext[i] for i in range(3)],
            [ext[3 + i] for i in range(3)],
            [cc[number] for number in range(7)],
            repeats,
        ),
        [],
    )


def write_edges(message, to_above, to_below):
    few = (message.shape[0] - 24) // 6
    lines = to_above.shape[0] // 6
    for i in range(6):
        own, beyond, at = i * few, 6 * few + 4 * i, lines * i
        extra = 1 if i < 3 else 2
        rows = lines - extra
        to_above[at : at + rows, :] = message[own + few - rows : own + few, :]
        to_above[at + rows : at + lines, :] = message[beyond + extra : beyond + 2 * extra, :]
        to_below[at : at + extra, :] = message[beyond : beyond + extra, :]
        to_below[at + extra : at + lines, :] = message[own : own + rows, :]


def read_message(ext, message, below, above):
    few = ext.shape[1] - 16
    top = 8 + few
    lines = below.shape[0] // 6
    for i in range(6):
        own, beyond, at = i * few, 6 * few + 4 * i, lines * i
        extra = 1 if i < 3 else 2
        rows = lines - extra
        ext[i, 8:top, :] = message[own : own + few, :]
        ext[i, 8 - rows : 8, :] = below[at : at + rows, :]
        ext[i, top : top + rows, :] = above[at + extra : at + lines, :]
        ext[i, 8 - extra : 8, :] += message[beyond : beyond + extra, :]
        ext[i, top : top + extra, :] += message[beyond + extra : beyond + 2 * extra, :]
        ext[i, 8 : 8 + extra, :] += below[at + rows : at + lines, :]
        ext[i, top - extra : top, :] += above[at : at + extra, :]


def halves(ref):
    return ref.at[0], ref.at[1]


def pair_body(b, b_other, cc, message, to_above, to_below, ext, late):
    few = ext.shape[1] - 16
    top = 8 + few
    odd = lax.axis_index("cuts") % 2
    ext[:, 0:8, :] = jnp.zeros_like(ext[:, 0:8, :])
    ext[:, top : top + 8, :] = jnp.zeros_like(ext[:, 0:8, :])

    @pl.when(odd == 0)
    def _():
        ext[:, 8:top, :] = b[...]
        late[...] = b_other[...]

    @pl.when(odd == 1)
    def _():
        ext[:, 8:top, :] = b_other[...]
        late[...] = b[...]

    for i, value in enumerate(advance(ext, cc, 1)):
        own, beyond = i * few, 6 * few + 4 * i
        message[own : own + few, :] = value[8:top] + late[i]
        if i < 3:
            message[beyond : beyond + 1, :] = value[7:8]
            message[beyond + 1 : beyond + 2, :] = value[top : top + 1]
            message[beyond + 2 : beyond + 4, :] = jnp.zeros_like(value[0:2])
        else:
            message[beyond : beyond + 2, :] = value[6:8]
            message[beyond + 2 : beyond + 4, :] = value[top : top + 2]
    write_edges(message, to_above, to_below)


def halo_body(below, above, out):
    out[0] = below[...]
    out[1] = above[...]


def chain_body(message, halo, source, cc, *refs):
    out, to_above, to_below, ext = refs[-4:]
    below, above = halves(halo)
    few = ext.shape[1] - 16
    ext[...] = jnp.zeros_like(ext)
    read_message(ext, message, below, above)
    for i, value in enumerate(advance(ext, cc, 2)):
        own = i * few
        out[own : own + few, :] = value[8 : 8 + few] + source[own : own + few, :]
    out[6 * few :, :] = source[6 * few :, :]
    write_edges(out, to_above, to_below)


def collect_body(rounds, *refs):
    messages, halos = refs[:rounds], refs[rounds : 2 * rounds]
    total, ext = refs[2 * rounds + 2 :]
    chip = lax.axis_index("cuts") // 2
    ext[...] = jnp.zeros_like(ext)
    for number in range(rounds):

        @pl.when(chip == number + 1)
        def _():
            read_message(ext, messages[number], *halves(halos[number]))

    for i in range(6):
        total[i] = ext[i, 8 : ext.shape[1] - 8, :]


def leap_body(message, halo, source, halo_source, cc, *refs):
    far, near, ext, add = refs[-4:]
    chip = lax.axis_index("cuts") // 2
    few = ext.shape[1] - 16
    top = 8 + few

    def put(i, value):
        own, beyond = i * few, 6 * few + 4 * i
        far[i] = value[4 : top + 4]
        near[own : own + few, :] = value[8:top]
        near[beyond : beyond + 2, :] = value[6:8]
        near[beyond + 2 : beyond + 4, :] = value[top : top + 2]

    @pl.when((chip == 1) | (chip == 2))
    def _():
        add[...] = jnp.zeros_like(add)
        read_message(add, source, *halves(halo_source))

    @pl.when(chip == 1)
    def _():
        ext[...] = jnp.zeros_like(ext)
        read_message(ext, message, *halves(halo))
        for i, value in enumerate(advance(ext, cc, 2)):
            put(i, value + add[i])

    @pl.when(chip == 2)
    def _():
        for i in range(6):
            put(i, add[i])


def last_body(leaped, cc, out, ext):
    rows = ext.shape[1]

    @pl.when(lax.axis_index("cuts") // 2 == 3)
    def _():
        ext[...] = jnp.zeros_like(ext)
        ext[:, 4 : rows - 4, :] = leaped[...]
        for i, value in enumerate(advance(ext, cc, 2)):
            out[i] = value


def arrive_body(message, halo, last, step, *refs):
    total, ext = refs[-2:]
    chip = lax.axis_index("cuts") // 2
    rows = ext.shape[1]
    few = rows - 16
    ext[...] = jnp.zeros_like(ext)

    @pl.when(chip == 1)
    def _():
        read_message(ext, message, *halves(halo))

    @pl.when(chip >= 2)
    def _():
        for i in range(6):
            own, beyond = i * few, 6 * few + 4 * i
            ext[i, 8 : 8 + few, :] = step[own : own + few, :]
            ext[i, 6:8, :] = step[beyond : beyond + 2, :]
            ext[i, 8 + few : 10 + few, :] = step[beyond + 2 : beyond + 4, :]

    @pl.when(chip == 3)
    def _():
        ext[...] += last[...]

    for i in range(6):
        total[i] = ext[i, 8 : rows - 8, :]


def even_body(ext, b_even, cc, even_end):
    few = ext.shape[1] - 16
    for i, value in enumerate(advance(ext, cc, 1)):
        even_end[i] = value[8 : 8 + few] + b_even[i]


def outer_body(f, ends, out):
    rows = f.shape[1]
    quarter = rows // 4
    out[:, 0:8, :] = ends[:, 0:8, :]
    out[:, 8:quarter, :] = f[:, 8:quarter, :]
    out[:, quarter : 2 * quarter - 8, :] = f[:, rows - quarter : rows - 8, :]
    out[:, 2 * quarter - 8 : 2 * quarter, :] = ends[:, 8:16, :]


def copy_body(value, after, out):
    out[...] = value[...]


def again_body(u, cf, out, w1, half, made):
    lead = cf.shape[1] // 4 - MARGIN

    def coefficients(start, count, fresh):
        return [cf[number, lead + start : lead + start + count, :] for number in range(7)]

    propagate(u, coefficients, w1, half, made)
    out[...] = made[:, MARGIN : made.shape[1] - MARGIN, :]


def join_body(f, ends, out, sems):
    rows = f.shape[1]
    copies = [
        pltpu.make_async_copy(f.at[:, 8 : rows - 8], out.at[:, 8 : rows - 8], sems.at[0]),
        pltpu.make_async_copy(ends.at[:, 0:8], out.at[:, 0:8], sems.at[1]),
        pltpu.make_async_copy(ends.at[:, 8:16], out.at[:, rows - 8 : rows], sems.at[2]),
    ]
    for copy in copies:
        copy.start()
    for copy in copies:
        copy.wait()


def spread_add(values, bases, outs, slots):
    cols = 2 * values.shape[1]
    wide = exact_dot(values, spreading(cols))
    few = wide.shape[0] // len(outs)
    for i, (base, out) in enumerate(zip(bases, outs)):
        for tile in range(cols // LANES):
            part = wide[i * few : (i + 1) * few, tile * LANES : (tile + 1) * LANES]
            assert i * (cols // LANES) + tile < slots.shape[0] and 2 * few <= slots.shape[1]
            slot = slots.at[i * (cols // LANES) + tile]
            slot[pl.ds(0, few, stride=2), :] = part
            slot[pl.ds(1, few, stride=2), :] = part
            at = (slice(None), pl.ds(tile * LANES, LANES))
            out[at] = base[at] + slot[0 : 2 * few, :]


def remainder(parts, outs, slots):
    pair_sum = Halver(slots)
    cols = parts[0].shape[1]
    few = parts[0].shape[0] // 2
    sums = [pair_sum(part, (), 0, few) for part in parts]
    means = exact_dot(jnp.concatenate(sums, axis=0), averaging(cols))
    spread_add(-means, parts, outs, slots)


def outer_parts(ref, quarter):
    rows = ref.shape[1]
    ends = (pl.ds(0, quarter), pl.ds(rows - quarter, quarter))
    return [ref.at[i, end] for i in range(6) for end in ends]


def early_body(inner, outer, init, out, slots, sem):
    place = lax.axis_index("cuts")
    rows = out.shape[1]
    quarter = rows // 4
    middle = pl.ds(quarter, rows // 2)

    @pl.when(place != 0)
    def _():
        remainder(
            [inner.at[i] for i in range(6)], [out.at[i, middle] for i in range(6)], slots
        )
        remainder(outer_parts(outer, quarter), outer_parts(out, quarter), slots)

    @pl.when(place == 0)
    def _():
        copy = pltpu.make_async_copy(init, out, sem)
        copy.start()
        copy.wait()


def late_body(base_in, after_hop, base, slots, made, sems):
    rows = base.shape[1]
    quarter = rows // 4

    @pl.when(lax.axis_index("cuts") == 2)
    def _():
        remainder(outer_parts(after_hop, quarter), outer_parts(made, quarter), slots)
        copies = [
            pltpu.make_async_copy(
                made.at[:, pl.ds(n * quarter, quarter)],
                base.at[:, pl.ds(start, quarter)],
                sems.at[n],
            )
            for n, start in enumerate((0, rows - quarter))
        ]
        for copy in copies:
            copy.start()
        for copy in copies:
            copy.wait()


def correct_body(base, own, received, out, slots, made, sems):
    odd = lax.axis_index("cuts") % 2
    cols = base.shape[2]
    copies = []
    for lead in range(0, 6, 2):
        part = range(lead, lead + 2)
        values = []
        for i in part:
            value = jnp.where(odd == 1, received[i], own[i])
            values.append(value if i < 3 else value * (1.0 / SPEED))
        spread_add(
            jnp.concatenate(values, axis=0),
            [base.at[i] for i in part],
            [made.at[i] for i in part],
            slots.at[pl.ds(cols // LANES * lead, cols // LANES * 2)],
        )
        copies.append(
            pltpu.make_async_copy(
                made.at[pl.ds(lead, 2)], out.at[pl.ds(lead, 2)], sems.at[lead // 2]
            )
        )
        copies[-1].start()
    for copy in copies:
        copy.wait()


def per_device(start_state, initial_state, circ_stiff, axial_stiff, lumped_mass, hoop_stiff):
    u = start_state[0]
    strips, slices = lax.axis_size("strip"), lax.axis_size("cuts")
    chips = slices // 2
    _, rows, cols = u.shape
    few, half_cols = rows // 2, cols // 2
    state, coarse_state = (6, rows, cols), (6, few, half_cols)
    ext_state = (6, few + 16, half_cols)
    leap = chips == 4
    reach = 7 if leap else 3
    edge = (6 * (reach + 1), half_cols)
    fields = (circ_stiff, axial_stiff, lumped_mass, hoop_stiff)

    def around_loop(value, by):
        pairs = [(s, (s + by) % strips) for s in range(strips)]
        return lax.ppermute(value, "strip", pairs)


    def along_cuts(value, moves):
        rest = [j for j in range(slices) if j not in moves]
        pairs = list(moves.items()) + [(j, j ^ 1) for j in rest]
        assert sorted(target for _, target in pairs) == list(range(slices))
        return lax.ppermute(value, "cuts", pairs)

    def hop(value, by, chip):
        third = None
        if chip > 0:
            third = chip + 2 if chip + 2 < chips else chip - 1
        used = {chip, chip + 1, third}
        pairs = []
        for s in range(strips):
            here, there = s * slices, (s + by) % strips * slices
            a, b = here + 2 * chip, there + 2 * chip + 2
            path = [a, b, b + 1]
            if third is not None:
                path += [there + 2 * third, there + 2 * third + 1]
            path.append(a + 1)
            pairs += list(zip(path, path[1:] + path[:1]))
            pairs += [(here + j, here + (j ^ 1)) for j in range(slices) if j // 2 not in used]
        assert sorted(target for _, target in pairs) == list(range(strips * slices))
        return lax.ppermute(value, ("strip", "cuts"), pairs)

    def hop_with_edges(main, to_above, to_below, move):
        edges = [move(to_above, 1), move(to_below, -1)]
        (halo,) = run(
            halo_body, "halo", [(2,) + edge], edges, cost=(HALO_COST, HALO_COST)
        )
        return move(main, 0), halo

    def to_chip_1(value, by):
        pairs = []
        for s in range(strips):
            here, there, beyond = (slices * ((s + k * by) % strips) for k in range(3))
            path = [here, there + 2, beyond + 3, here + 1]
            if by:
                path = [here + 1, there + 2, beyond + 3, here]
            pairs += list(zip(path, path[1:] + path[:1]))
            for j in range(4, slices, 2):
                pairs += [(here + j, there + j + 1), (here + j + 1, here + j)]
        assert sorted(target for _, target in pairs) == list(range(strips * slices))
        return lax.ppermute(value, ("strip", "cuts"), pairs)

    def around_cuts(value, *path):
        return along_cuts(value, dict(zip(path, path[1:] + path[:1])))

    pack = (PACK_ROWS, cols)
    third = (3, rows, cols)
    ends_shape = (6, 16, cols)
    message = (6 * few + 24, half_cols)
    cc_shape, cf_shape = (7, few + 16, half_cols), (7, rows, cols)
    middle_shape = (6, few + 2 * MARGIN, cols)
    outer_shape = (6, few, cols)
    to_above, to_below, own, own_coarse, u_near, *near, middle = run(
        pack_body,
        "pack",
        [pack, pack, (10, 16, cols), (10, 8, half_cols), state]
        + [(rows, cols)] * 4
        + [middle_shape],
        [u, initial_state, *fields],
        [
            pltpu.VMEM(ends_shape, F32),
            halver_scratch(32, 16, cols),
            pltpu.SemaphoreType.DMA((7,)),
        ],
        specs=[HBM] * 6,
    )
    from_below = around_loop(to_above, 1)
    from_above = around_loop(to_below, -1)
    raw = along_cuts(middle, {j: (j + 1) % slices for j in range(slices)})
    f, b, cc, cf = run(
        interior_body,
        "interior",
        [state, coarse_state, cc_shape, cf_shape],
        [u_near, initial_state, *near],
        [
            pltpu.VMEM(third, F32),
            pltpu.VMEM(third, F32),
            pltpu.VMEM((10 * few, cols), F32),
            pltpu.VMEM(state, F32),
            halver_scratch(22, rows, cols),
            pltpu.SemaphoreType.DMA,
        ],
        specs=[VMEM, HBM] + [VMEM] * 4,
    )
    ends, b, cc = run(
        edges_body,
        "edges",
        [ends_shape, coarse_state, cc_shape],
        [f, own, own_coarse, b, cc, from_below, from_above],
        [
            pltpu.VMEM((10, 32, cols), F32),
            pltpu.VMEM((10, 24, half_cols), F32),
            halver_scratch(6, 16, cols),
        ],
    )
    ext = [pltpu.VMEM(ext_state, F32)]
    b_other = along_cuts(b, {})
    source = run(
        pair_body,
        "pair",
        [message, edge, edge],
        [b, b_other, cc],
        ext + [pltpu.VMEM(coarse_state, F32)],
    )
    (outer,) = run(outer_body, "outer", [outer_shape], [f, ends])

    previous = along_cuts(outer, {j: j + 1 for j in range(2, slices - 1)} | {slices - 1: 2})
    if leap:
        main, halo = hop_with_edges(*source, to_chip_1)
        halo_source = along_cuts(halo, {})
        far, near = run(
            leap_body,
            "leap",
            [(6, few + 8, half_cols), message],
            [main, halo, source[0], halo_source, cc, raw],
            ext * 2,
            specs=[VMEM] * 5 + [ANY],
        )
        after_leap = near
        to_chip_3 = around_cuts(far, 2, 6, 7, 3)
        to_next = around_cuts(near, 2, 4, 6, 7, 5, 3)
        (last,) = run(
            last_body, "last", [ext_state], [to_chip_3, cc], ext, cost=(LAST_COST, LAST_COST)
        )
        close, received_by_chain = arrive_body, [main, halo, last, to_next]
    else:
        at_end = source
        arrived = []
        for chip in range(chips - 1):
            arrived.append(hop_with_edges(*at_end, lambda value, by: hop(value, by, chip)))
            if chip < chips - 2:
                extra = {0: [raw], 1: [previous]}.get(chip, [])
                at_end = run(
                    chain_body,
                    "chain",
                    [message, edge, edge],
                    [*arrived[-1], source[0], cc] + extra,
                    ext,
                    specs=[VMEM] * 4 + [ANY] * len(extra),
                )
            if chip == 0:
                after_leap = at_end[1]
        messages, halos = zip(*arrived)
        close, received_by_chain = lambda *refs: collect_body(chips - 1, *refs), [*messages, *halos]
    (part,) = run(copy_body, "later", [outer_shape], [outer, after_leap], specs=[VMEM, ANY])
    after_hop = lax.ppermute(part, "cuts", [(1, 2)])
    (fine_end,) = run(
        join_body,
        "join",
        [state],
        [f, ends],
        [pltpu.SemaphoreType.DMA((3,))],
        specs=[ANY] * 2,
        out_specs=[ANY],
        cost=(0, 6 * rows * cols * 8),
    )
    (inner,) = run(
        again_body,
        "again",
        [outer_shape],
        [raw, cf],
        [pltpu.VMEM((3,) + middle_shape[1:], F32)] * 2 + [pltpu.VMEM(middle_shape, F32)],
        cost=(0, 6 * rows * cols * 8),
    )
    rem_scratch = [
        halver_scratch(6, rows, cols),
        pltpu.VMEM(state, F32),
        pltpu.SemaphoreType.DMA((3,)),
    ]
    (base,) = run(
        early_body,
        "remainder",
        [state],
        [inner, previous, initial_state],
        [
            halver_scratch(12, few, cols),
            pltpu.SemaphoreType.DMA,
        ],
        specs=[VMEM] * 2 + [HBM],
        cost=(0, 6 * rows * cols * 8),
    )
    total, ended = run(
        close,
        "collect",
        [coarse_state, ext_state],
        [*received_by_chain, base, fine_end],
        specs=[VMEM] * len(received_by_chain) + [ANY, HBM],
    )
    (even_end,) = run(even_body, "even", [coarse_state], [ended, b, cc])
    received = along_cuts(even_end, {})
    (base,) = run(
        late_body,
        "late",
        [state],
        [base, after_hop],
        [
            halver_scratch(12, rows // 4, cols),
            pltpu.VMEM(outer_shape, F32),
            pltpu.SemaphoreType.DMA((2,)),
        ],
        specs=[ANY, VMEM],
        out_specs=[ANY],
        aliases={0: 0},
    )
    (new_start,) = run(
        correct_body,
        "correct",
        [state],
        [base, total, received],
        rem_scratch,
        out_specs=[HBM],
    )
    return new_start[None], fine_end[None]


def solution(mesh):
    state = P("cuts", None, "strip", None)
    field = P("strip", None)
    return jax.shard_map(
        per_device,
        mesh=mesh,
        in_specs=(state, P(None, "strip", None), field, field, field, field),
        out_specs=(state, state),
        check_vma=False,
    )
```

```python
import jax
import jax.numpy as jnp
from jax import lax
from jax.experimental import pallas as pl
from jax.experimental.pallas import tpu as pltpu
from jax.sharding import PartitionSpec as P

FINE_STEP = 0.35
COARSE_STEP = 0.7
FINE_COUPLING = 0.25
COARSE_COUPLING = 0.5
SPEED = COARSE_STEP

FINE_ROWS = (3, 3, 3, 2, 2, 2, 3, 2, 2, 2)
COARSE_ROWS = (2, 2, 2, 1, 1, 1, 6, 5, 5, 5)
FINE_TOTAL = sum(FINE_ROWS)
PACK_ROWS = -(-(FINE_TOTAL + -(-sum(COARSE_ROWS) // 2)) // 8) * 8
CHUNK = 16
HALO_COST = int(2e9)
LAST_COST = int(1e9)
MARGIN = 8

VMEM = pl.BlockSpec(memory_space=pltpu.VMEM)
ANY = pl.BlockSpec(memory_space=pl.ANY)
HBM = pl.BlockSpec(memory_space=pltpu.HBM)
F32 = jnp.float32


def run(body, name, outs, args, scratch=(), specs=None, out_specs=None, aliases=None, cost=None):
    if specs:
        args = [
            pltpu.with_memory_space_constraint(arg, pltpu.HBM) if spec is HBM else arg
            for arg, spec in zip(args, specs)
        ]
    return pl.pallas_call(
        body,
        name=name,
        out_shape=[jax.ShapeDtypeStruct(shape, F32) for shape in outs],
        in_specs=specs or [VMEM] * len(args),
        out_specs=out_specs or [VMEM] * len(outs),
        scratch_shapes=list(scratch),
        input_output_aliases=aliases or {},
        compiler_params=pltpu.CompilerParams(vmem_limit_bytes=20 << 20),
        cost_estimate=cost
        and pl.CostEstimate(flops=cost[0], bytes_accessed=cost[1], transcendentals=0),
    )(*args)


def turn(value, steps, axis):
    return pltpu.roll(value, steps % value.shape[axis], axis)


def scaled_coefficients(kc, kc_low, ka, mass, hoop, step, coupling):
    lane = lax.broadcasted_iota(jnp.int32, ka.shape, 1)
    last = ka.shape[1] - 1
    ka_next = jnp.where(lane == last, 0.0, ka)
    ka_low = jnp.where(lane == 0, 0.0, turn(ka, 1, 1))
    unit = (step * step) / mass
    return (
        kc * unit,
        kc_low * unit,
        ka_next * unit,
        ka_low * unit,
        (kc + kc_low + ka + ka_low) * unit,
        hoop * unit,
        (0.5 * coupling) * unit,
    )


def accelerate(now, above, below, cf):
    up, down, fore, aft, centre, hoop, cross = cf
    out = []
    for i in range(3):
        w = now[i]
        out.append(
            up * above[i]
            + down * below[i]
            + fore * turn(w, -1, 1)
            + aft * turn(w, 1, 1)
            - centre * w
        )
    out[0] = out[0] - cross * (above[2] - below[2])
    out[2] = out[2] + cross * (above[0] - below[0]) - hoop * now[2]
    return out


def accelerate_block(now, cf):
    above = [turn(w, -1, 0) for w in now]
    below = [turn(w, 1, 0) for w in now]
    return accelerate(now, above, below, cf)


def steps_block(w, q, cf, repeats):
    acc = accelerate_block(w, cf)
    for _ in range(repeats):
        half = [a + 0.5 * b for a, b in zip(q, acc)]
        w = [a + b for a, b in zip(w, half)]
        acc = accelerate_block(w, cf)
        q = [a + 0.5 * b for a, b in zip(half, acc)]
    return w, q


def exact_dot(value, matrix):
    split = []
    for _ in range(3):
        split.append(value.astype(jnp.bfloat16))
        value = value - split[-1].astype(F32)
    return sum(jnp.dot(part, matrix, preferred_element_type=F32) for part in split[::-1])


def averaging(cols):
    row = lax.broadcasted_iota(jnp.int32, (cols, cols // 2), 0)
    col = lax.broadcasted_iota(jnp.int32, (cols, cols // 2), 1)
    return jnp.where(row // 2 == col, 0.25, 0.0).astype(jnp.bfloat16)


def spreading(cols):
    row = lax.broadcasted_iota(jnp.int32, (cols // 2, cols), 0)
    col = lax.broadcasted_iota(jnp.int32, (cols // 2, cols), 1)
    return jnp.where(col // 2 == row, 1.0, 0.0).astype(jnp.bfloat16)


LANES = 128


class Halver:
    def __init__(self, ref):
        self.ref = ref
        self.used = 0

    def __call__(self, source, lead, start, count):
        pieces = []
        for at in range(0, source.shape[-1], LANES):
            assert self.used < self.ref.shape[0] and 2 * count <= self.ref.shape[1]
            slot = self.ref.at[self.used]
            self.used += 1
            slot[0 : 2 * count, :] = source[
                lead + (pl.ds(start, 2 * count), pl.ds(at, LANES))
            ]
            pieces.append(
                slot[pl.ds(0, count, stride=2), :] + slot[pl.ds(1, count, stride=2), :]
            )
        return jnp.concatenate(pieces, axis=1)


def halver_scratch(fields, rows, cols):
    return pltpu.VMEM((fields * (cols // LANES), rows + 8, LANES), F32)


def is_first():
    return (lax.axis_index("cuts") == 0).astype(F32)


def pack_body(
    u_far, init, kc_far, ka_far, mass_far, hoop_far,
    to_above, to_below, own, own_coarse, u, kc, ka, mass, hoop, middle, early, slots, sems,
):
    rows, cols = kc.shape
    pair_sum = Halver(slots)
    first = is_first()
    copies = [(kc_far, kc), (ka_far, ka), (mass_far, mass), (hoop_far, hoop)]
    copies += [
        (init.at[:, start : start + 8], early.at[:, pl.ds(8 * end, 8)])
        for end, start in enumerate((0, rows - 8))
    ]
    copies.append((u_far, u))
    copies = [
        pltpu.make_async_copy(source, target, sems.at[n])
        for n, (source, target) in enumerate(copies)
    ]
    for copy in copies:
        copy.start()
    matrix = averaging(cols)
    half = cols // 2
    fine_at = [sum(FINE_ROWS[:number]) for number in range(10)]
    coarse_at = [sum(COARSE_ROWS[:number]) for number in range(10)]

    def pack(numbers, sources, sums, ends):
        for number, (ref, place) in zip(numbers, sources):
            own[number, 0:8, :] = ref[place + (slice(0, 8), slice(None))]
            own[number, 8:16, :] = ref[place + (slice(rows - 8, rows), slice(None))]
            at, count = fine_at[number], FINE_ROWS[number]
            to_above[at : at + count, :] = own[number, 16 - count : 16, :]
            to_below[at : at + count, :] = own[number, 0:count, :]
        means = exact_dot(jnp.concatenate(sums, axis=0), matrix)
        for n, number in enumerate(numbers):
            low = means[2 * n * ends : (2 * n + 1) * ends]
            high = means[(2 * n + 1) * ends : (2 * n + 2) * ends]
            own_coarse[number, 0:4, :] = low[0:4]
            own_coarse[number, 4:8, :] = high[ends - 4 : ends]
            count = COARSE_ROWS[number]
            for k in range(count):
                at = coarse_at[number] + k
                line = FINE_TOTAL + at // 2
                where = (slice(line, line + 1), pl.ds((at % 2) * half, half))
                to_above[where] = high[ends - count + k : ends - count + k + 1]
                to_below[where] = low[k : k + 1]

    for copy in copies[:4]:
        copy.wait()
    sources = [(ref, ()) for ref in (kc, ka, mass, hoop)]
    sums = [pair_sum(ref, (), start, 8) for ref, _ in sources for start in (0, rows - 16)]
    pack(range(6, 10), sources, sums, 8)
    for copy in copies[4:]:
        copy.wait()
    sums = []
    for i in range(6):
        for end, start in enumerate((0, rows - 8)):
            sums.append(pair_sum(u, (i,), start, 4) - first * pair_sum(early, (i,), 8 * end, 4))
    pack(range(6), [(u, (i,)) for i in range(6)], sums, 4)
    lead = rows // 4 - MARGIN
    middle[...] = u[:, lead : rows - lead, :]


def propagate(u, coefficients, w1, half, f):
    rows = u.shape[1]
    chunk = CHUNK if rows % CHUNK == 0 else 8
    starts = range(0, rows, chunk)

    def around(ref, start):
        found = []
        for i in range(3):
            now = ref[i, start : start + chunk, :]
            if start + chunk < rows:
                above = ref[i, start + 1 : start + chunk + 1, :]
            else:
                above = turn(now, -1, 0)
            if start > 0:
                below = ref[i, start - 1 : start + chunk - 1, :]
            else:
                below = turn(now, 1, 0)
            found.append((now, above, below))
        return zip(*found)

    for start in starts:
        at = pl.ds(start, chunk)
        now, above, below = around(u, start)
        acc = accelerate(now, above, below, coefficients(start, chunk, True))
        for i in range(3):
            moved = FINE_STEP * u[3 + i, at, :] + 0.5 * acc[i]
            half[i, at, :] = moved
            w1[i, at, :] = now[i] + moved
    for start in starts:
        at = pl.ds(start, chunk)
        now, above, below = around(w1, start)
        acc = accelerate(now, above, below, coefficients(start, chunk, False))
        for i in range(3):
            moved = half[i, at, :] + acc[i]
            half[i, at, :] = moved
            f[i, at, :] = now[i] + moved
    for start in starts:
        at = pl.ds(start, chunk)
        now, above, below = around(f, start)
        acc = accelerate(now, above, below, coefficients(start, chunk, False))
        for i in range(3):
            f[3 + i, at, :] = (half[i, at, :] + 0.5 * acc[i]) * (1.0 / FINE_STEP)


def interior_body(
    u, init, kc, ka, mass, hoop, f, b, cc, cf, w1, half, sums, late, slots, sem
):
    pair_sum = Halver(slots)
    rows, cols = kc.shape
    first = lax.axis_index("cuts") == 0
    prescribed = pltpu.make_async_copy(init, late, sem)

    @pl.when(first)
    def _():
        prescribed.start()

    def coefficients(start, count, fresh):
        at = pl.ds(start, count)
        if not fresh:
            return [cf[number, at, :] for number in range(7)]
        stiff = kc[at, :]
        stiff_low = kc[start - 1 : start + count - 1, :] if start else turn(stiff, 1, 0)
        found = scaled_coefficients(
            stiff, stiff_low, ka[at, :], mass[at, :], hoop[at, :], FINE_STEP, FINE_COUPLING
        )
        for number in range(7):
            cf[number, at, :] = found[number]
        return found

    propagate(u, coefficients, w1, half, f)

    matrix = averaging(cols)
    few = rows // 2
    for i in range(6):
        sums[i * few : (i + 1) * few, :] = pair_sum(u, (i,), 0, few)
    for number, ref in enumerate((kc, ka, mass, hoop)):
        sums[(6 + number) * few : (7 + number) * few, :] = pair_sum(ref, (), 0, few)

    @pl.when(first)
    def _():
        prescribed.wait()
        for i in range(6):
            sums[i * few : (i + 1) * few, :] -= pair_sum(late, (i,), 0, few)

    means = exact_dot(sums[...], matrix)
    parts = [means[i * few : (i + 1) * few] for i in range(10)]
    ckc, cka, cm, ch = parts[6:]
    found = scaled_coefficients(
        ckc, turn(ckc, 1, 0), cka, 4.0 * cm, 4.0 * ch, COARSE_STEP, COARSE_COUPLING
    )
    for number in range(7):
        cc[number, 8 : 8 + few, :] = found[number]
    moved = sum(steps_block(parts[:3], [SPEED * q for q in parts[3:6]], found, 1), [])
    means = exact_dot(
        jnp.concatenate([pair_sum(f, (i,), 0, few) for i in range(6)], axis=0), matrix
    )
    for i in range(6):
        scale = 1.0 if i < 3 else SPEED
        b[i] = scale * means[i * few : (i + 1) * few] - moved[i]


def edges_body(
    f, own, own_coarse, b_in, cc_in, from_below, from_above,
    done, b, cc, fine, coarse, slots,
):
    rows, cols = f.shape[1:]
    few, half_cols = rows // 2, cols // 2
    pair_sum = Halver(slots)
    at = 0
    for number, count in enumerate(FINE_ROWS):
        fine[number, 8 - count : 8, :] = from_below[at : at + count, :]
        fine[number, 8:24, :] = own[number]
        fine[number, 24 : 24 + count, :] = from_above[at : at + count, :]
        at += count
    found = scaled_coefficients(
        fine[6], turn(fine[6], 1, 0), fine[7], fine[8], fine[9], FINE_STEP, FINE_COUPLING
    )
    w, q = steps_block(
        [fine[i] for i in range(3)], [FINE_STEP * fine[3 + i] for i in range(3)], found, 2
    )
    for i in range(6):
        done[i, 0:8, :] = f[i, 0:8, :]
        done[i, 8:16, :] = f[i, rows - 8 : rows, :]
    for i in range(3):
        done[i, 0:4, :] = w[i][8:12]
        done[i, 12:16, :] = w[i][20:24]
        done[3 + i, 0:4, :] = q[i][8:12] * (1.0 / FINE_STEP)
        done[3 + i, 12:16, :] = q[i][20:24] * (1.0 / FINE_STEP)

    sums = [pair_sum(done, (i,), 0, 8) for i in range(6)]
    means = exact_dot(jnp.concatenate(sums, axis=0), averaging(cols))
    coarse[...] = jnp.ones_like(coarse)
    at = 0
    for number, count in enumerate(COARSE_ROWS):
        coarse[number, 8:16, :] = own_coarse[number]
        for k in range(count):
            line = FINE_TOTAL + at // 2
            place = (slice(line, line + 1), pl.ds((at % 2) * half_cols, half_cols))
            coarse[number, 8 - count + k : 9 - count + k, :] = from_below[place]
            coarse[number, 16 + k : 17 + k, :] = from_above[place]
            at += 1
    found = scaled_coefficients(
        coarse[6], turn(coarse[6], 1, 0), coarse[7], 4.0 * coarse[8], 4.0 * coarse[9],
        COARSE_STEP, COARSE_COUPLING,
    )
    for number in range(7):
        cc[number, 0:12, :] = found[number][0:12]
        cc[number, 12 : few + 8, :] = cc_in[number, 12 : few + 8, :]
        cc[number, few + 8 : few + 16, :] = found[number][16:24]
    w, q = steps_block(
        [coarse[i] for i in range(3)], [SPEED * coarse[3 + i] for i in range(3)], found, 1
    )
    moved = w + q
    b[...] = b_in[...]
    for i in range(6):
        scale = 1.0 if i < 3 else SPEED
        ends = scale * means[8 * i : 8 * i + 8, :]
        b[i, 0:2, :] = ends[0:2] - moved[i][8:10]
        b[i, few - 2 : few, :] = ends[6:8] - moved[i][14:16]


def advance(ext, cc, repeats):
    return sum(
        steps_block(
            [ext[i] for i in range(3)],
            [ext[3 + i] for i in range(3)],
            [cc[number] for number in range(7)],
            repeats,
        ),
        [],
    )


def write_edges(message, to_above, to_below):
    few = (message.shape[0] - 24) // 6
    lines = to_above.shape[0] // 6
    for i in range(6):
        own, beyond, at = i * few, 6 * few + 4 * i, lines * i
        extra = 1 if i < 3 else 2
        rows = lines - extra
        to_above[at : at + rows, :] = message[own + few - rows : own + few, :]
        to_above[at + rows : at + lines, :] = message[beyond + extra : beyond + 2 * extra, :]
        to_below[at : at + extra, :] = message[beyond : beyond + extra, :]
        to_below[at + extra : at + lines, :] = message[own : own + rows, :]


def read_message(ext, message, below, above):
    few = ext.shape[1] - 16
    top = 8 + few
    lines = below.shape[0] // 6
    for i in range(6):
        own, beyond, at = i * few, 6 * few + 4 * i, lines * i
        extra = 1 if i < 3 else 2
        rows = lines - extra
        ext[i, 8:top, :] = message[own : own + few, :]
        ext[i, 8 - rows : 8, :] = below[at : at + rows, :]
        ext[i, top : top + rows, :] = above[at + extra : at + lines, :]
        ext[i, 8 - extra : 8, :] += message[beyond : beyond + extra, :]
        ext[i, top : top + extra, :] += message[beyond + extra : beyond + 2 * extra, :]
        ext[i, 8 : 8 + extra, :] += below[at + rows : at + lines, :]
        ext[i, top - extra : top, :] += above[at : at + extra, :]


def halves(ref):
    return ref.at[0], ref.at[1]


def pair_body(b, b_other, cc, message, to_above, to_below, ext, late):
    few = ext.shape[1] - 16
    top = 8 + few
    odd = lax.axis_index("cuts") % 2
    ext[:, 0:8, :] = jnp.zeros_like(ext[:, 0:8, :])
    ext[:, top : top + 8, :] = jnp.zeros_like(ext[:, 0:8, :])

    @pl.when(odd == 0)
    def _():
        ext[:, 8:top, :] = b[...]
        late[...] = b_other[...]

    @pl.when(odd == 1)
    def _():
        ext[:, 8:top, :] = b_other[...]
        late[...] = b[...]

    for i, value in enumerate(advance(ext, cc, 1)):
        own, beyond = i * few, 6 * few + 4 * i
        message[own : own + few, :] = value[8:top] + late[i]
        if i < 3:
            message[beyond : beyond + 1, :] = value[7:8]
            message[beyond + 1 : beyond + 2, :] = value[top : top + 1]
            message[beyond + 2 : beyond + 4, :] = jnp.zeros_like(value[0:2])
        else:
            message[beyond : beyond + 2, :] = value[6:8]
            message[beyond + 2 : beyond + 4, :] = value[top : top + 2]
    write_edges(message, to_above, to_below)


def halo_body(below, above, out):
    out[0] = below[...]
    out[1] = above[...]


def chain_body(message, halo, source, cc, *refs):
    out, to_above, to_below, ext = refs[-4:]
    below, above = halves(halo)
    few = ext.shape[1] - 16
    ext[...] = jnp.zeros_like(ext)
    read_message(ext, message, below, above)
    for i, value in enumerate(advance(ext, cc, 2)):
        own = i * few
        out[own : own + few, :] = value[8 : 8 + few] + source[own : own + few, :]
    out[6 * few :, :] = source[6 * few :, :]
    write_edges(out, to_above, to_below)


def collect_body(rounds, *refs):
    messages, halos = refs[:rounds], refs[rounds : 2 * rounds]
    total, ext = refs[2 * rounds + 2 :]
    chip = lax.axis_index("cuts") // 2
    ext[...] = jnp.zeros_like(ext)
    for number in range(rounds):

        @pl.when(chip == number + 1)
        def _():
            read_message(ext, messages[number], *halves(halos[number]))

    for i in range(6):
        total[i] = ext[i, 8 : ext.shape[1] - 8, :]


def leap_body(message, halo, source, halo_source, cc, *refs):
    far, near, ext, add = refs[-4:]
    chip = lax.axis_index("cuts") // 2
    few = ext.shape[1] - 16
    top = 8 + few

    def put(i, value):
        own, beyond = i * few, 6 * few + 4 * i
        far[i] = value[4 : top + 4]
        near[own : own + few, :] = value[8:top]
        near[beyond : beyond + 2, :] = value[6:8]
        near[beyond + 2 : beyond + 4, :] = value[top : top + 2]

    @pl.when((chip == 1) | (chip == 2))
    def _():
        add[...] = jnp.zeros_like(add)
        read_message(add, source, *halves(halo_source))

    @pl.when(chip == 1)
    def _():
        ext[...] = jnp.zeros_like(ext)
        read_message(ext, message, *halves(halo))
        for i, value in enumerate(advance(ext, cc, 2)):
            put(i, value + add[i])

    @pl.when(chip == 2)
    def _():
        for i in range(6):
            put(i, add[i])


def last_body(leaped, cc, out, ext):
    rows = ext.shape[1]

    @pl.when(lax.axis_index("cuts") // 2 == 3)
    def _():
        ext[...] = jnp.zeros_like(ext)
        ext[:, 4 : rows - 4, :] = leaped[...]
        for i, value in enumerate(advance(ext, cc, 2)):
            out[i] = value


def arrive_body(message, halo, last, step, *refs):
    total, ext = refs[-2:]
    chip = lax.axis_index("cuts") // 2
    rows = ext.shape[1]
    few = rows - 16
    ext[...] = jnp.zeros_like(ext)

    @pl.when(chip == 1)
    def _():
        read_message(ext, message, *halves(halo))

    @pl.when(chip >= 2)
    def _():
        for i in range(6):
            own, beyond = i * few, 6 * few + 4 * i
            ext[i, 8 : 8 + few, :] = step[own : own + few, :]
            ext[i, 6:8, :] = step[beyond : beyond + 2, :]
            ext[i, 8 + few : 10 + few, :] = step[beyond + 2 : beyond + 4, :]

    @pl.when(chip == 3)
    def _():
        ext[...] += last[...]

    for i in range(6):
        total[i] = ext[i, 8 : rows - 8, :]


def even_body(ext, b_even, cc, even_end):
    few = ext.shape[1] - 16
    for i, value in enumerate(advance(ext, cc, 1)):
        even_end[i] = value[8 : 8 + few] + b_even[i]


def outer_body(f, ends, out):
    rows = f.shape[1]
    quarter = rows // 4
    out[:, 0:8, :] = ends[:, 0:8, :]
    out[:, 8:quarter, :] = f[:, 8:quarter, :]
    out[:, quarter : 2 * quarter - 8, :] = f[:, rows - quarter : rows - 8, :]
    out[:, 2 * quarter - 8 : 2 * quarter, :] = ends[:, 8:16, :]


def copy_body(value, after, out):
    out[...] = value[...]


def again_body(u, cf, out, w1, half, made):
    lead = cf.shape[1] // 4 - MARGIN

    def coefficients(start, count, fresh):
        return [cf[number, lead + start : lead + start + count, :] for number in range(7)]

    propagate(u, coefficients, w1, half, made)
    out[...] = made[:, MARGIN : made.shape[1] - MARGIN, :]


def join_body(f, ends, out, sems):
    rows = f.shape[1]
    copies = [
        pltpu.make_async_copy(f.at[:, 8 : rows - 8], out.at[:, 8 : rows - 8], sems.at[0]),
        pltpu.make_async_copy(ends.at[:, 0:8], out.at[:, 0:8], sems.at[1]),
        pltpu.make_async_copy(ends.at[:, 8:16], out.at[:, rows - 8 : rows], sems.at[2]),
    ]
    for copy in copies:
        copy.start()
    for copy in copies:
        copy.wait()


def spread_add(values, bases, outs, slots):
    cols = 2 * values.shape[1]
    wide = exact_dot(values, spreading(cols))
    few = wide.shape[0] // len(outs)
    for i, (base, out) in enumerate(zip(bases, outs)):
        for tile in range(cols // LANES):
            part = wide[i * few : (i + 1) * few, tile * LANES : (tile + 1) * LANES]
            assert i * (cols // LANES) + tile < slots.shape[0] and 2 * few <= slots.shape[1]
            slot = slots.at[i * (cols // LANES) + tile]
            slot[pl.ds(0, few, stride=2), :] = part
            slot[pl.ds(1, few, stride=2), :] = part
            at = (slice(None), pl.ds(tile * LANES, LANES))
            out[at] = base[at] + slot[0 : 2 * few, :]


def remainder(parts, outs, slots):
    pair_sum = Halver(slots)
    cols = parts[0].shape[1]
    few = parts[0].shape[0] // 2
    sums = [pair_sum(part, (), 0, few) for part in parts]
    means = exact_dot(jnp.concatenate(sums, axis=0), averaging(cols))
    spread_add(-means, parts, outs, slots)


def outer_parts(ref, quarter):
    rows = ref.shape[1]
    ends = (pl.ds(0, quarter), pl.ds(rows - quarter, quarter))
    return [ref.at[i, end] for i in range(6) for end in ends]


def early_body(inner, outer, init, out, slots, sem):
    place = lax.axis_index("cuts")
    rows = out.shape[1]
    quarter = rows // 4
    middle = pl.ds(quarter, rows // 2)

    @pl.when(place != 0)
    def _():
        remainder(
            [inner.at[i] for i in range(6)], [out.at[i, middle] for i in range(6)], slots
        )
        remainder(outer_parts(outer, quarter), outer_parts(out, quarter), slots)

    @pl.when(place == 0)
    def _():
        copy = pltpu.make_async_copy(init, out, sem)
        copy.start()
        copy.wait()


def late_body(base_in, after_hop, base, slots, made, sems):
    rows = base.shape[1]
    quarter = rows // 4

    @pl.when(lax.axis_index("cuts") == 2)
    def _():
        remainder(outer_parts(after_hop, quarter), outer_parts(made, quarter), slots)
        copies = [
            pltpu.make_async_copy(
                made.at[:, pl.ds(n * quarter, quarter)],
                base.at[:, pl.ds(start, quarter)],
                sems.at[n],
            )
            for n, start in enumerate((0, rows - quarter))
        ]
        for copy in copies:
            copy.start()
        for copy in copies:
            copy.wait()


def correct_body(base, own, received, out, slots, made, sems):
    odd = lax.axis_index("cuts") % 2
    cols = base.shape[2]
    copies = []
    for lead in range(6):
        part = range(lead, lead + 1)
        values = []
        for i in part:
            value = jnp.where(odd == 1, received[i], own[i])
            values.append(value if i < 3 else value * (1.0 / SPEED))
        spread_add(
            jnp.concatenate(values, axis=0),
            [base.at[i] for i in part],
            [made.at[i] for i in part],
            slots.at[pl.ds(cols // LANES * lead, cols // LANES)],
        )
        copies.append(
            pltpu.make_async_copy(
                made.at[pl.ds(lead, 1)], out.at[pl.ds(lead, 1)], sems.at[lead]
            )
        )
        copies[-1].start()
    for copy in copies:
        copy.wait()


def per_device(start_state, initial_state, circ_stiff, axial_stiff, lumped_mass, hoop_stiff):
    u = start_state[0]
    strips, slices = lax.axis_size("strip"), lax.axis_size("cuts")
    chips = slices // 2
    _, rows, cols = u.shape
    few, half_cols = rows // 2, cols // 2
    state, coarse_state = (6, rows, cols), (6, few, half_cols)
    ext_state = (6, few + 16, half_cols)
    leap = chips == 4
    reach = 7 if leap else 3
    edge = (6 * (reach + 1), half_cols)
    fields = (circ_stiff, axial_stiff, lumped_mass, hoop_stiff)

    def around_loop(value, by):
        pairs = [(s, (s + by) % strips) for s in range(strips)]
        return lax.ppermute(value, "strip", pairs)


    def along_cuts(value, moves):
        rest = [j for j in range(slices) if j not in moves]
        pairs = list(moves.items()) + [(j, j ^ 1) for j in rest]
        assert sorted(target for _, target in pairs) == list(range(slices))
        return lax.ppermute(value, "cuts", pairs)

    def hop(value, by, chip):
        third = None
        if chip > 0:
            third = chip + 2 if chip + 2 < chips else chip - 1
        used = {chip, chip + 1, third}
        pairs = []
        for s in range(strips):
            here, there = s * slices, (s + by) % strips * slices
            a, b = here + 2 * chip, there + 2 * chip + 2
            path = [a, b, b + 1]
            if third is not None:
                path += [there + 2 * third, there + 2 * third + 1]
            path.append(a + 1)
            pairs += list(zip(path, path[1:] + path[:1]))
            pairs += [(here + j, here + (j ^ 1)) for j in range(slices) if j // 2 not in used]
        assert sorted(target for _, target in pairs) == list(range(strips * slices))
        return lax.ppermute(value, ("strip", "cuts"), pairs)

    def hop_with_edges(main, to_above, to_below, move):
        edges = [move(to_above, 1), move(to_below, -1)]
        (halo,) = run(
            halo_body, "halo", [(2,) + edge], edges, cost=(HALO_COST, HALO_COST)
        )
        return move(main, 0), halo

    def to_chip_1(value, by):
        pairs = []
        for s in range(strips):
            here, there, beyond = (slices * ((s + k * by) % strips) for k in range(3))
            path = [here, there + 2, beyond + 3, here + 1]
            if by:
                path = [here + 1, there + 2, beyond + 3, here]
            pairs += list(zip(path, path[1:] + path[:1]))
            for j in range(4, slices, 2):
                pairs += [(here + j, there + j + 1), (here + j + 1, here + j)]
        assert sorted(target for _, target in pairs) == list(range(strips * slices))
        return lax.ppermute(value, ("strip", "cuts"), pairs)

    def around_cuts(value, *path):
        return along_cuts(value, dict(zip(path, path[1:] + path[:1])))

    pack = (PACK_ROWS, cols)
    third = (3, rows, cols)
    ends_shape = (6, 16, cols)
    message = (6 * few + 24, half_cols)
    cc_shape, cf_shape = (7, few + 16, half_cols), (7, rows, cols)
    middle_shape = (6, few + 2 * MARGIN, cols)
    outer_shape = (6, few, cols)
    to_above, to_below, own, own_coarse, u_near, *near, middle = run(
        pack_body,
        "pack",
        [pack, pack, (10, 16, cols), (10, 8, half_cols), state]
        + [(rows, cols)] * 4
        + [middle_shape],
        [u, initial_state, *fields],
        [
            pltpu.VMEM(ends_shape, F32),
            halver_scratch(32, 16, cols),
            pltpu.SemaphoreType.DMA((7,)),
        ],
        specs=[HBM] * 6,
    )
    from_below = around_loop(to_above, 1)
    from_above = around_loop(to_below, -1)
    raw = along_cuts(middle, {j: (j + 1) % slices for j in range(slices)})
    f, b, cc, cf = run(
        interior_body,
        "interior",
        [state, coarse_state, cc_shape, cf_shape],
        [u_near, initial_state, *near],
        [
            pltpu.VMEM(third, F32),
            pltpu.VMEM(third, F32),
            pltpu.VMEM((10 * few, cols), F32),
            pltpu.VMEM(state, F32),
            halver_scratch(22, rows, cols),
            pltpu.SemaphoreType.DMA,
        ],
        specs=[VMEM, HBM] + [VMEM] * 4,
    )
    ends, b, cc = run(
        edges_body,
        "edges",
        [ends_shape, coarse_state, cc_shape],
        [f, own, own_coarse, b, cc, from_below, from_above],
        [
            pltpu.VMEM((10, 32, cols), F32),
            pltpu.VMEM((10, 24, half_cols), F32),
            halver_scratch(6, 16, cols),
        ],
    )
    ext = [pltpu.VMEM(ext_state, F32)]
    b_other = along_cuts(b, {})
    source = run(
        pair_body,
        "pair",
        [message, edge, edge],
        [b, b_other, cc],
        ext + [pltpu.VMEM(coarse_state, F32)],
    )
    (outer,) = run(outer_body, "outer", [outer_shape], [f, ends])

    previous = along_cuts(outer, {j: j + 1 for j in range(2, slices - 1)} | {slices - 1: 2})
    if leap:
        main, halo = hop_with_edges(*source, to_chip_1)
        halo_source = along_cuts(halo, {})
        far, near = run(
            leap_body,
            "leap",
            [(6, few + 8, half_cols), message],
            [main, halo, source[0], halo_source, cc, raw],
            ext * 2,
            specs=[VMEM] * 5 + [ANY],
        )
        after_leap = near
        to_chip_3 = around_cuts(far, 2, 6, 7, 3)
        to_next = around_cuts(near, 2, 4, 6, 7, 5, 3)
        (last,) = run(
            last_body, "last", [ext_state], [to_chip_3, cc], ext, cost=(LAST_COST, LAST_COST)
        )
        close, received_by_chain = arrive_body, [main, halo, last, to_next]
    else:
        at_end = source
        arrived = []
        for chip in range(chips - 1):
            arrived.append(hop_with_edges(*at_end, lambda value, by: hop(value, by, chip)))
            if chip < chips - 2:
                extra = {0: [raw], 1: [previous]}.get(chip, [])
                at_end = run(
                    chain_body,
                    "chain",
                    [message, edge, edge],
                    [*arrived[-1], source[0], cc] + extra,
                    ext,
                    specs=[VMEM] * 4 + [ANY] * len(extra),
                )
            if chip == 0:
                after_leap = at_end[1]
        messages, halos = zip(*arrived)
        close, received_by_chain = lambda *refs: collect_body(chips - 1, *refs), [*messages, *halos]
    (part,) = run(copy_body, "later", [outer_shape], [outer, after_leap], specs=[VMEM, ANY])
    after_hop = lax.ppermute(part, "cuts", [(1, 2)])
    (fine_end,) = run(
        join_body,
        "join",
        [state],
        [f, ends],
        [pltpu.SemaphoreType.DMA((3,))],
        specs=[ANY] * 2,
        out_specs=[ANY],
        cost=(0, 6 * rows * cols * 8),
    )
    (inner,) = run(
        again_body,
        "again",
        [outer_shape],
        [raw, cf],
        [pltpu.VMEM((3,) + middle_shape[1:], F32)] * 2 + [pltpu.VMEM(middle_shape, F32)],
        cost=(0, 6 * rows * cols * 8),
    )
    rem_scratch = [
        halver_scratch(6, rows, cols),
        pltpu.VMEM(state, F32),
        pltpu.SemaphoreType.DMA((6,)),
    ]
    (base,) = run(
        early_body,
        "remainder",
        [state],
        [inner, previous, initial_state],
        [
            halver_scratch(12, few, cols),
            pltpu.SemaphoreType.DMA,
        ],
        specs=[VMEM] * 2 + [HBM],
        cost=(0, 6 * rows * cols * 8),
    )
    total, ended = run(
        close,
        "collect",
        [coarse_state, ext_state],
        [*received_by_chain, base, fine_end],
        specs=[VMEM] * len(received_by_chain) + [ANY, HBM],
    )
    (even_end,) = run(even_body, "even", [coarse_state], [ended, b, cc])
    received = along_cuts(even_end, {})
    (base,) = run(
        late_body,
        "late",
        [state],
        [base, after_hop],
        [
            halver_scratch(12, rows // 4, cols),
            pltpu.VMEM(outer_shape, F32),
            pltpu.SemaphoreType.DMA((2,)),
        ],
        specs=[ANY, VMEM],
        out_specs=[ANY],
        aliases={0: 0},
    )
    (new_start,) = run(
        correct_body,
        "correct",
        [state],
        [base, total, received],
        rem_scratch,
        out_specs=[HBM],
    )
    return new_start[None], fine_end[None]


def solution(mesh):
    state = P("cuts", None, "strip", None)
    field = P("strip", None)
    return jax.shard_map(
        per_device,
        mesh=mesh,
        in_specs=(state, P(None, "strip", None), field, field, field, field),
        out_specs=(state, state),
        check_vma=False,
    )
```
